32 devices in a mesh: groups: 2 (over x), ctx: 16 (over z, y, core).
Axes of the slice: x: 2, y: 2, z: 4, core: 2. Of those that a mesh axis runs over, the one named last changes fastest.
Arguments:
- context: bfloat16 [96, 256, 1024], P(('groups', 'ctx')), parts along dimension 0, may hold values from -6 to 6
- counts: int32 [32], P('groups'), parts along dimension 0, may hold values from 1 to 3, as said below
- queries: bfloat16 [128, 4096], P(('groups', 'ctx')), parts along dimension 0, may hold values from -120 to 120
- norm_gain: bfloat16 [1024], replicated, may hold values from 0.099609375 to 1.8984375
- w_query: bfloat16 [1024, 1024], replicated, may hold values from -1 to 1
- w_key: bfloat16 [1024, 1024], replicated, may hold values from -9 to 9
- w_value: bfloat16 [1024, 1024], replicated, may hold values from -0.1875 to 0.1875
- w_out: bfloat16 [1024, 1024], replicated, may hold values from -0.1875 to 0.1875
- final_gain: bfloat16 [1024], replicated, may hold values from 0.099609375 to 1.8984375
- w_kv: bfloat16 [1024, 2048], P(None, 'ctx'), may hold values from -0.1875 to 0.1875
Outputs:
- attended_context: bfloat16 [128, 4096], P(('groups', 'ctx')), parts along dimension 0
The draws below stay inside these ranges and needn't reach their ends.
There are 2 independent parts, one for each index of `groups`. The reference program is written for one: setup_inputs(seed, part) draws one part's arguments, and reference() takes and returns one part's arrays. A program takes and returns all parts, laid end to end along the dimension named above; an argument that names none is the same for every part. Nothing has to cross between parts.
Inputs may be any that keep to these rules, and one draw needn't show every extreme that they name: Device d's slots are d * 3 to d * 3 + 2, and only the first counts[d] of them hold live blocks. The largest count equals 3 in every draw. For every d below 8, counts[d] + counts[d + 8] is at most 4, and equals it for some d in every draw.
All inputs are finite; a program needn't handle non-finite values.
Results may differ from the reference program's by a relative error of at most 0.025.
The reference program's roundings to bfloat16 on the way count: a program that leaves them out, or rounds other values in their place, can miss the bound.
Values may be sent and summed in bfloat16 or wider, within the bound.
No kernel may reach another device: no remote copies, remote signals or barrier semaphores. Data moves between devices by JAX's collectives and lax.ppermute only.
A program may use at most 128 MiB of HBM per device.

```python
import math
import jax
import jax.numpy as jnp
from jax import lax

D_ENC = 1024
ENC_HEADS = 16
ENC_HD = 64
BLOCK = 256
KV_HEADS = 8
HEAD_DIM = 128
GROUP = 4
KVW = 2048
QW = 4096
MEAN = 1
CAP = 3
SLOTS = 48
QT = 64
N_CTX = 16


def draw_w_query(key, part):
    key = jax.random.fold_in(key, 11)
    own_noise = jnp.clip(jax.random.normal(key, (D_ENC, D_ENC), jnp.float32), -6.0, 6.0)
    return (own_noise / math.sqrt(D_ENC)).astype(jnp.bfloat16)


def draw_w_key(key, part):
    key = jax.random.fold_in(key, 12)
    own_noise = jnp.clip(jax.random.normal(key, (D_ENC, D_ENC), jnp.float32), -6.0, 6.0)
    return (own_noise / math.sqrt(D_ENC)).astype(jnp.bfloat16)


def draw_queries(key, part):
    key = jax.random.fold_in(key, 31)
    first_key = jax.random.fold_in(key, 0)
    return jnp.clip(jax.random.normal(first_key, (QT, QW), jnp.float32), -6.0, 6.0).astype(jnp.bfloat16)


def draw_counts(key, part):
    key = jax.random.fold_in(key, 21)
    first_key, second_key, third_key = jax.random.split(key, 3)
    half_count = N_CTX // 2
    doubled = jax.random.randint(first_key, (N_CTX,), 0, 4) == 0
    base_count = jnp.where(doubled, 2 * MEAN, MEAN)
    heavy_pair = jax.random.randint(second_key, (), 0, half_count)
    heavy_side = jax.random.randint(third_key, (), 0, 2)
    heavy_device = heavy_pair + heavy_side * half_count
    light_device = heavy_pair + (1 - heavy_side) * half_count
    device_number = jnp.arange(N_CTX)
    counts = jnp.where(device_number == heavy_device, CAP, jnp.where(device_number == light_device, MEAN, base_count))
    return counts.astype(jnp.int32)


def shard_levels(rng, shape, shards, low, high):
    level, own = 1.0, jax.random.fold_in(rng, 6)
    for axis_at, shards_of in shards:
        draws = jnp.exp(jax.random.uniform(jax.random.fold_in(own, axis_at), (shards_of,), jnp.float32, low / len(shards), high / len(shards)))
        level = level * jnp.repeat(draws, shape[axis_at] // shards_of).reshape([-1 if axis == axis_at else 1 for axis in range(len(shape))])
    return level


def scatter_about(rng, extent, width, bound, shards=(), held_as=jnp.bfloat16):
    level = shard_levels(rng, extent, shards, -0.22, 0.18) if shards else 1.0
    result = jax.random.normal(rng, extent, jnp.float32) * width * level
    return jnp.minimum(jnp.maximum(result, -bound), bound).astype(held_as)


def setup_inputs(seed: int = 0, part: int = 0) -> dict:
    key_list = jax.random.split(jax.random.key(seed), 11)
    part_splits = jax.random.split(jax.random.fold_in(key_list[10], part), 11)
    context = scatter_about(part_splits[0], (SLOTS, BLOCK, D_ENC), 1.0, 6.0, ((0, 16),))
    counts = draw_counts(jax.random.fold_in(jax.random.fold_in(key_list[10], part), 71), part)
    queries = draw_queries(jax.random.fold_in(jax.random.fold_in(key_list[10], part), 71), part)
    norm_gain = jnp.clip(1.0 + 0.18 * jax.random.normal(key_list[3], (D_ENC,), jnp.float32), 0.099609375, 1.8984375).astype(jnp.bfloat16)
    w_query = draw_w_query(jax.random.fold_in(key_list[10], 71), part)
    w_key = draw_w_key(jax.random.fold_in(key_list[10], 71), part)
    w_value = scatter_about(key_list[6], (D_ENC, D_ENC), D_ENC ** -0.5, 0.1875)
    w_out = scatter_about(key_list[7], (D_ENC, D_ENC), D_ENC ** -0.5, 0.1875)
    final_gain = jnp.clip(1.0 + 0.18 * jax.random.normal(key_list[8], (D_ENC,), jnp.float32), 0.099609375, 1.8984375).astype(jnp.bfloat16)
    w_kv = scatter_about(key_list[9], (D_ENC, KVW), D_ENC ** -0.5, 0.1875, ((1, 16),))
    return {"context": context, "counts": counts, "queries": queries, "norm_gain": norm_gain, "w_query": w_query, "w_key": w_key, "w_value": w_value, "w_out": w_out, "final_gain": final_gain, "w_kv": w_kv}


def narrow(values):
    return lax.optimization_barrier(values.astype(jnp.bfloat16))

def root_scale(values, gain):
    values = values.astype(jnp.float32)
    return values * lax.rsqrt(lax.optimization_barrier(jnp.mean(values * values, axis=-1, keepdims=True)) + 1e-05) * gain.astype(jnp.float32)

def rotary_tables(length, head_width):
    position = jnp.arange(length).astype(jnp.float32)[:, None]
    frequency = jnp.exp(jnp.arange(head_width // 2).astype(jnp.float32) * (-2.0 * math.log(10000.0) / head_width))
    phase_angle = position * frequency[None, :]
    return (jnp.cos(phase_angle)[:, None, :], jnp.sin(phase_angle)[:, None, :])

def rotate(values, cosine_table, sine_table):
    half_width = values.shape[-1] // 2
    lower_half = values[..., :half_width]
    upper_half = values[..., half_width:]
    return jnp.concatenate([lower_half * cosine_table - upper_half * sine_table, upper_half * cosine_table + lower_half * sine_table], axis=-1)

def encode_block(block_rows, norm_gain, w_query, w_key, w_value, w_out, final_gain, w_kv):
    normed = narrow(root_scale(block_rows, norm_gain))
    cosine_table, sine_table = rotary_tables(BLOCK, ENC_HD)

    def project(weight):
        return jnp.dot(normed, weight, preferred_element_type=jnp.float32).reshape(BLOCK, ENC_HEADS, ENC_HD)
    query_rows = narrow(rotate(project(w_query), cosine_table, sine_table)).astype(jnp.float32)
    key_rows = narrow(rotate(project(w_key), cosine_table, sine_table)).astype(jnp.float32)
    value_rows = narrow(project(w_value)).astype(jnp.float32)
    scores = jnp.einsum('qhd,khd->hqk', query_rows, key_rows) / math.sqrt(ENC_HD)
    weights = narrow(jax.nn.softmax(scores, axis=-1)).astype(jnp.float32)
    mixed_rows = narrow(jnp.einsum('hqk,khd->qhd', weights, value_rows)).reshape(BLOCK, D_ENC)
    residual = block_rows.astype(jnp.float32) + jnp.dot(mixed_rows, w_out, preferred_element_type=jnp.float32)
    final_norm = narrow(root_scale(residual, final_gain))
    return narrow(jnp.dot(final_norm, w_kv, preferred_element_type=jnp.float32))

def reference(context, counts, queries, norm_gain, w_query, w_key, w_value, w_out, final_gain, w_kv):
    alive_slot = jnp.arange(SLOTS) % CAP < jnp.repeat(counts, CAP)

    def one_slot(slot_args):
        block_rows, alive = slot_args
        return lax.cond(alive, lambda rows_in: encode_block(rows_in, norm_gain, w_query, w_key, w_value, w_out, final_gain, w_kv), lambda rows_in: jnp.zeros((BLOCK, KVW), jnp.bfloat16), block_rows)
    key_value = lax.map(one_slot, (context, alive_slot))
    grouped = queries.astype(jnp.float32).reshape(QT, KV_HEADS, GROUP, HEAD_DIM)

    def slot_scores(slot_kv):
        key_rows = slot_kv[:, :KV_HEADS * HEAD_DIM].astype(jnp.float32).reshape(BLOCK, KV_HEADS, HEAD_DIM)
        return jnp.einsum('rkgd,tkd->rkgt', grouped, key_rows) / math.sqrt(HEAD_DIM)

    def max_step(running_top, slot_args):
        slot_kv, alive = slot_args
        return (jnp.where(alive, jnp.maximum(running_top, lax.optimization_barrier(jnp.max(slot_scores(slot_kv), axis=-1))), running_top), None)
    start_top = jnp.full((QT, KV_HEADS, GROUP), -jnp.inf, jnp.float32)
    row_top, _ = lax.scan(max_step, start_top, (key_value, alive_slot))

    def sum_step(totals, slot_args):
        slot_kv, alive = slot_args
        weights = jnp.where(alive, jnp.exp(slot_scores(slot_kv) - row_top[..., None]), 0.0)
        value_rows = slot_kv[:, KV_HEADS * HEAD_DIM:].astype(jnp.float32).reshape(BLOCK, KV_HEADS, HEAD_DIM)
        numerator = totals[0] + jnp.einsum('rkgt,tkd->rkgd', narrow(weights).astype(jnp.float32), value_rows)
        return ((numerator, totals[1] + lax.optimization_barrier(jnp.sum(weights, axis=-1))), None)
    start_sums = (jnp.zeros((QT, KV_HEADS, GROUP, HEAD_DIM), jnp.float32), jnp.zeros((QT, KV_HEADS, GROUP), jnp.float32))
    (numerator, denominator), _ = lax.scan(sum_step, start_sums, (key_value, alive_slot))
    return (numerator / denominator[..., None]).reshape(QT, QW).astype(jnp.bfloat16)
```

```python
import functools
import math

import jax
import jax.numpy as jnp
from jax import lax
from jax.experimental import pallas as pl
from jax.experimental.pallas import tpu as pltpu
from jax.sharding import PartitionSpec as P

D_ENC = 1024
ENC_HEADS = 16
ENC_HD = 64
BLOCK = 256
KV_HEADS = 8
HEAD_DIM = 128
Q_HEADS = 32
GROUP = 4
QW = 4096
CAP = 3
HALF_HEADS = KV_HEADS // 2
LANES = 128
F32 = jnp.float32
BF16 = jnp.bfloat16
VMEM = pl.BlockSpec(memory_space=pltpu.VMEM)
SMEM = pl.BlockSpec(memory_space=pltpu.SMEM)


def root_scale(values, gain):
    values = values.astype(F32)
    return (
        values
        * lax.rsqrt(jnp.mean(values * values, axis=-1, keepdims=True) + 1e-05)
        * gain.astype(F32)
    )


def rotary_lanes():
    position = jnp.arange(BLOCK).astype(F32)[:, None]
    frequency = jnp.exp(jnp.arange(ENC_HD // 2).astype(F32) * (-2.0 * math.log(10000.0) / ENC_HD))
    angle = position * frequency[None, :]
    cosine, sine = jnp.cos(angle), jnp.sin(angle)
    return (
        jnp.concatenate([cosine, cosine, cosine, cosine], axis=1),
        jnp.concatenate([-sine, sine, -sine, sine], axis=1),
    )


def encoder_kernel(alive_ref, x_ref, alt_ref, wq_ref, wk_ref, wv_ref, wo_ref, gain_ref, fgain_ref,
                   cos_ref, sin_ref, out_ref, mixed_ref):
    @pl.when(alive_ref[0] != 0)
    def _():
        block = jnp.where(alive_ref[1] != 0, alt_ref[...], x_ref[...])
        normed = root_scale(block, gain_ref[...]).astype(BF16)
        cosine, sine = cos_ref[...], sin_ref[...]
        lane = lax.broadcasted_iota(jnp.int32, (BLOCK, LANES), 1)
        lower = (lane % ENC_HD) < ENC_HD // 2
        first = lane < ENC_HD

        def rotate(values):
            swapped = jnp.where(
                lower,
                pltpu.roll(values, LANES - ENC_HD // 2, 1),
                pltpu.roll(values, ENC_HD // 2, 1),
            )
            return (values * cosine + swapped * sine).astype(BF16)

        for part in range(4):
            columns = slice(part * 256, (part + 1) * 256)
            query = jnp.dot(normed, wq_ref[:, columns], preferred_element_type=F32)
            key = jnp.dot(normed, wk_ref[:, columns], preferred_element_type=F32)
            value = jnp.dot(normed, wv_ref[:, columns], preferred_element_type=F32).astype(BF16)
            for pair in range(2):
                cut = slice(pair * LANES, (pair + 1) * LANES)
                query_pair = rotate(query[:, cut]) * jnp.asarray(0.125, BF16)
                key_pair = rotate(key[:, cut])
                value_pair = value[:, cut]
                mixed = []
                for head in range(2):
                    own = first if head == 0 else jnp.logical_not(first)
                    scores = lax.dot_general(
                        jnp.where(own, query_pair, jnp.zeros_like(query_pair)), key_pair,
                        (((1,), (1,)), ((), ())), preferred_element_type=F32,
                    )
                    weights = jnp.exp(scores - jnp.max(scores, axis=-1, keepdims=True))
                    weights = weights / jnp.sum(weights, axis=-1, keepdims=True)
                    mixed.append(jnp.dot(weights.astype(BF16), value_pair, preferred_element_type=F32))
                start = part * 256 + pair * LANES
                mixed_ref[:, start : start + LANES] = jnp.where(first, mixed[0], mixed[1]).astype(BF16)
        residual = block.astype(F32) + jnp.dot(mixed_ref[...], wo_ref[...], preferred_element_type=F32)
        out_ref[...] = root_scale(residual, fgain_ref[...]).astype(BF16)


def encode(alive, block, other, weights):
    return pl.pallas_call(
        encoder_kernel,
        out_shape=jax.ShapeDtypeStruct((BLOCK, D_ENC), BF16),
        in_specs=[SMEM] + [VMEM] * 10,
        out_specs=VMEM,
        scratch_shapes=[pltpu.VMEM((BLOCK, D_ENC), BF16)],
        compiler_params=pltpu.CompilerParams(vmem_limit_bytes=32 * 2**20),
        cost_estimate=pl.CostEstimate(flops=4 * 10**9, bytes_accessed=9 * 2**20, transcendentals=2**20),
    )(alive, block, other, *weights)


def three_parts(values):
    high = values.astype(BF16).astype(F32)
    middle = (values - high).astype(BF16).astype(F32)
    return high, middle, values - high - middle


def cross_kernel(place_ref, own0, own1, own2, other0, other1, other2, *refs):
    loads, out_ref, query_ref, key_ref, value_ref, total_ref, top_ref, sum_ref = (
        refs[:8], refs[8], refs[9], refs[10], refs[11], refs[12], refs[13], refs[14])
    lines = query_ref.shape[1]
    chip_lines = lines // 8
    for step in range(4):
        for side in range(2):
            load = loads[2 * step + side]
            chip = place_ref[2 + 2 * step + side]
            for head in range(HALF_HEADS):
                start = pl.multiple_of(chip * chip_lines, chip_lines)
                query_ref[head, pl.ds(start, chip_lines), :] = load[
                    D_ENC + head * chip_lines : D_ENC + (head + 1) * chip_lines, :]
    total_ref[...] = jnp.zeros_like(total_ref)
    sum_ref[...] = jnp.zeros_like(sum_ref)
    top_ref[...] = jnp.full_like(top_ref, -jnp.inf)

    def add_block(tokens_ref):
        tokens = tokens_ref[...]
        for step in range(4):
            pair = jnp.concatenate([loads[2 * step][:D_ENC, :], loads[2 * step + 1][:D_ENC, :]], axis=1)
            both = jnp.dot(tokens, pair, preferred_element_type=F32).astype(BF16)
            for side in range(2):
                chip = place_ref[2 + 2 * step + side]
                key_ref[chip] = both[:, side * LANES : (side + 1) * LANES]
        for head in range(HALF_HEADS):
            scores = lax.dot_general(
                query_ref[head], key_ref[head], (((1,), (1,)), ((), ())), preferred_element_type=F32
            ) * (1.0 / math.sqrt(HEAD_DIM))
            old_top = top_ref[head]
            new_top = jnp.maximum(old_top, jnp.max(scores, axis=-1, keepdims=True))
            weights = jnp.exp(scores - new_top[:, :1])
            shrink = jnp.exp(old_top - new_top)
            top_ref[head] = new_top
            sum_ref[head] = sum_ref[head] * shrink + jnp.sum(weights, axis=-1, keepdims=True)
            total_ref[head] = total_ref[head] * shrink + jnp.dot(
                weights.astype(BF16), key_ref[HALF_HEADS + head], preferred_element_type=F32)

    for count_at, group in ((0, (own0, own1, own2)), (1, (other0, other1, other2))):
        for slot in range(CAP):
            pl.when(place_ref[count_at] > slot)(functools.partial(add_block, group[slot]))

    lane = lax.broadcasted_iota(jnp.int32, (lines, LANES), 1)
    notes = jnp.zeros((lines, LANES), F32)
    for head in range(HALF_HEADS):
        pieces = three_parts(top_ref[head]) + three_parts(sum_ref[head])
        for at, piece in enumerate(pieces):
            notes = jnp.where(lane == 6 * head + at, piece, notes)
        own_lines = lines // out_ref.shape[0]
        out_ref[:, head] = total_ref[head].astype(BF16).reshape(out_ref.shape[0], own_lines, LANES)
    out_ref[:, HALF_HEADS] = notes.astype(BF16).reshape(out_ref.shape[0], own_lines, LANES)


def cross(places, place, tokens, loads):
    lines = places * 16
    return pl.pallas_call(
        cross_kernel,
        out_shape=jax.ShapeDtypeStruct((places, HALF_HEADS + 1, 16, LANES), BF16),
        in_specs=[SMEM] + [VMEM] * 14,
        out_specs=VMEM,
        scratch_shapes=[
            pltpu.VMEM((HALF_HEADS, lines, LANES), BF16),
            pltpu.VMEM((KV_HEADS, BLOCK, LANES), BF16),
            pltpu.VMEM((8, LANES), BF16),
            pltpu.VMEM((HALF_HEADS, lines, LANES), F32),
            pltpu.VMEM((HALF_HEADS, lines, LANES), F32),
            pltpu.VMEM((HALF_HEADS, lines, LANES), F32),
        ],
        compiler_params=pltpu.CompilerParams(vmem_limit_bytes=40 * 2**20),
        cost_estimate=pl.CostEstimate(flops=6 * 10**9, bytes_accessed=8 * 2**20, transcendentals=2**20),
    )(place, *tokens, *loads)


def combine_kernel(parts_ref, out_ref):
    places = parts_ref.shape[0]
    for core in range(2):
        notes = [parts_ref[2 * chip + core, HALF_HEADS].astype(F32) for chip in range(places // 2)]
        for head in range(HALF_HEADS):
            at = 6 * head
            tops = [n[:, at : at + 1] + n[:, at + 1 : at + 2] + n[:, at + 2 : at + 3] for n in notes]
            sums = [n[:, at + 3 : at + 4] + n[:, at + 4 : at + 5] + n[:, at + 5 : at + 6] for n in notes]
            top = functools.reduce(jnp.maximum, tops)
            numerator, denominator = 0.0, 0.0
            for chip in range(places // 2):
                share = jnp.exp(tops[chip] - top)
                numerator += share * parts_ref[2 * chip + core, head].astype(F32)
                denominator += share * sums[chip]
            out_ref[2 * head + core] = (numerator / denominator).astype(BF16)


def combine(parts):
    return pl.pallas_call(
        combine_kernel,
        out_shape=jax.ShapeDtypeStruct((KV_HEADS, 16, LANES), BF16),
        in_specs=[VMEM],
        out_specs=VMEM,
    )(parts)


NEXT_Z = (1, 3, 0, 2)


def swap_core(values):
    return lax.ppermute(values, "ctx", [(i, i ^ 1) for i in range(lax.axis_size("ctx"))])


def swap_y(values):
    return lax.ppermute(values, "ctx", [(i, i ^ 2) for i in range(16)])


def round_z(values):
    return lax.ppermute(values, "ctx", [(i, 4 * NEXT_Z[i // 4] + i % 4) for i in range(16)])


def local(context, counts, queries, norm_gain, w_query, w_key, w_value, w_out, final_gain, w_kv):
    places = lax.axis_size("ctx")
    me = lax.axis_index("ctx")
    core = me % 2
    own_count = lax.dynamic_index_in_dim(counts, me, keepdims=False)
    other_count = lax.dynamic_index_in_dim(counts, me + 1 - 2 * core, keepdims=False)
    gives = (own_count == 3) & (other_count == 1)
    takes = (own_count == 1) & (other_count == 3)
    own_live = own_count - gives.astype(jnp.int32) + takes.astype(jnp.int32)
    other_live = other_count + gives.astype(jnp.int32) - takes.astype(jnp.int32)
    taken = swap_core(context[2])

    split = queries.reshape(4, HALF_HEADS, 2, GROUP, HEAD_DIM).transpose(2, 1, 0, 3, 4)
    split = split.reshape(2, HALF_HEADS, 16, HEAD_DIM)
    keep = jnp.where(core == 0, split[0], split[1])
    give = jnp.where(core == 0, split[1], split[0])
    got = swap_core(give)
    chip_rows = jnp.concatenate(
        [jnp.where(core == 0, keep, got)[:, None], jnp.where(core == 0, got, keep)[:, None]], axis=1
    ).reshape(HALF_HEADS * 32, HEAD_DIM)
    load0 = jnp.concatenate([w_kv, chip_rows], axis=0)

    cosine, sine = rotary_lanes()
    weights = (w_query, w_key, w_value, w_out, norm_gain[None], final_gain[None], cosine, sine)
    flag = lambda alive, alt: jnp.stack([alive.astype(jnp.int32), alt.astype(jnp.int32)])

    beside0 = swap_y(load0)
    load1 = round_z(load0)
    token0 = encode(flag(own_live > 0, own_live < 0), context[0], taken, weights)
    far0 = swap_core(token0)
    beside1 = swap_y(load1)
    load2 = round_z(load1)
    token1 = encode(flag(own_live > 1, takes), context[1], taken, weights)
    far1 = swap_core(token1)
    beside2 = swap_y(load2)
    load3 = round_z(load2)
    token2 = encode(flag(own_live > 2, own_live < 0), context[2], taken, weights)
    far2 = swap_core(token2)
    beside3 = swap_y(load3)

    z, y = me // 4, me // 2 % 2
    before = jnp.array([2, 0, 3, 1], jnp.int32)
    chips = []
    for _ in range(4):
        chips += [2 * z + y, 2 * z + 1 - y]
        z = before[z]
    place = jnp.stack([own_live, other_live] + chips).astype(jnp.int32)
    parts = cross(
        places, place, (token0, token1, token2, far0, far1, far2),
        (load0, beside0, load1, beside1, load2, beside2, load3, beside3),
    )
    parts = lax.all_to_all(parts, "ctx", 0, 0, tiled=True)
    result = combine(parts)
    return result.reshape(KV_HEADS, 4, GROUP, HEAD_DIM).transpose(1, 0, 2, 3).reshape(4, QW)


def rotary_tables(length, head_width):
    position = jnp.arange(length).astype(jnp.float32)[:, None]
    frequency = jnp.exp(
        jnp.arange(head_width // 2).astype(jnp.float32) * (-2.0 * math.log(10000.0) / head_width)
    )
    phase_angle = position * frequency[None, :]
    return (jnp.cos(phase_angle)[:, None, :], jnp.sin(phase_angle)[:, None, :])


def rotate(values, cosine_table, sine_table):
    half_width = values.shape[-1] // 2
    lower_half = values[..., :half_width]
    upper_half = values[..., half_width:]
    return jnp.concatenate(
        [
            lower_half * cosine_table - upper_half * sine_table,
            upper_half * cosine_table + lower_half * sine_table,
        ],
        axis=-1,
    )


def weighted_sums(cross_scores, top_scores, key_alive, cross_values):
    cross_weights = jnp.where(key_alive, jnp.exp(cross_scores - top_scores[..., None]), 0.0)
    total_rows = cross_scores.shape[0]
    denominator = jnp.sum(cross_weights, axis=-1).reshape(total_rows, Q_HEADS)
    numerator = jnp.einsum(
        "rkgt,tkd->rkgd",
        cross_weights.astype(jnp.bfloat16),
        cross_values,
        preferred_element_type=jnp.float32,
    )
    return (numerator.reshape(total_rows, QW), denominator)


def local_any(context, counts, queries, norm_gain, w_query, w_key, w_value, w_out, final_gain, w_kv):
    places = lax.axis_size("ctx")
    device_index = lax.axis_index("ctx")
    device_number = jnp.arange(places)
    own_count = jnp.sum(jnp.where(device_number == device_index, counts, 0))
    alive_slot = jnp.arange(CAP) < own_count
    slot_count = context.shape[0]
    row_count = slot_count * BLOCK
    normed = root_scale(context, norm_gain).astype(jnp.bfloat16).reshape(row_count, D_ENC)
    cosine_table, sine_table = rotary_tables(BLOCK, ENC_HD)

    def project(weight):
        return jnp.dot(normed, weight, preferred_element_type=jnp.float32).reshape(
            slot_count, BLOCK, ENC_HEADS, ENC_HD
        )

    query_rows = rotate(project(w_query), cosine_table, sine_table).astype(jnp.bfloat16)
    key_rows = rotate(project(w_key), cosine_table, sine_table).astype(jnp.bfloat16)
    value_rows = project(w_value).astype(jnp.bfloat16)
    scores = jnp.einsum(
        "sqhd,skhd->shqk", query_rows, key_rows, preferred_element_type=jnp.float32
    ) / math.sqrt(ENC_HD)
    weights = jax.nn.softmax(scores, axis=-1).astype(jnp.bfloat16)
    mixed_rows = jnp.einsum(
        "shqk,skhd->sqhd", weights, value_rows, preferred_element_type=jnp.float32
    )
    mixed_rows = mixed_rows.astype(jnp.bfloat16).reshape(row_count, D_ENC)
    residual = context.reshape(row_count, D_ENC).astype(jnp.float32) + jnp.dot(
        mixed_rows, w_out, preferred_element_type=jnp.float32
    )
    final_norm = root_scale(residual, final_gain).astype(jnp.bfloat16)
    key_value = jnp.dot(
        final_norm,
        lax.all_gather(w_kv, "ctx", axis=1, tiled=True),
        preferred_element_type=jnp.float32,
    ).astype(jnp.bfloat16)
    cross_keys = key_value[:, : KV_HEADS * HEAD_DIM].reshape(row_count, KV_HEADS, HEAD_DIM)
    cross_values = key_value[:, KV_HEADS * HEAD_DIM :].reshape(row_count, KV_HEADS, HEAD_DIM)
    every_query = lax.all_gather(queries, "ctx", axis=0, tiled=True)
    total_rows = every_query.shape[0]
    grouped = every_query.reshape(total_rows, KV_HEADS, GROUP, HEAD_DIM)
    cross_scores = jnp.einsum(
        "rkgd,tkd->rkgt", grouped, cross_keys, preferred_element_type=jnp.float32
    ) / math.sqrt(HEAD_DIM)
    key_alive = jnp.repeat(alive_slot, BLOCK)
    local_top = jnp.max(jnp.where(key_alive, cross_scores, -jnp.inf), axis=-1)
    row_top = lax.pmax(local_top.astype(jnp.bfloat16), "ctx").astype(local_top.dtype)
    numerator, denominator = weighted_sums(cross_scores, row_top, key_alive, cross_values)
    own_numerator, own_denominator = (
        lax.psum_scatter(numerator, "ctx", scatter_dimension=0, tiled=True),
        lax.psum_scatter(denominator, "ctx", scatter_dimension=0, tiled=True),
    )
    own_rows = own_numerator.shape[0]
    result = own_numerator.reshape(own_rows, Q_HEADS, HEAD_DIM) / own_denominator[..., None]
    return result.reshape(own_rows, QW).astype(jnp.bfloat16)


def solution(mesh):
    in_specs = (
        P(("groups", "ctx"), None, None),
        P("groups"),
        P(("groups", "ctx"), None),
        P(),
        P(),
        P(),
        P(),
        P(),
        P(),
        P(None, "ctx"),
    )
    out_specs = P(("groups", "ctx"), None)
    small = mesh.shape["ctx"] == 16
    return jax.shard_map(local if small else local_any, mesh=mesh, in_specs=in_specs, out_specs=out_specs, check_vma=False)
```

```python
import functools
import math

import jax
import jax.numpy as jnp
import numpy as np
from jax import lax
from jax.experimental import pallas as pl
from jax.experimental.pallas import tpu as pltpu
from jax.sharding import PartitionSpec as P

D_ENC = 1024
ENC_HEADS = 16
ENC_HD = 64
BLOCK = 256
KV_HEADS = 8
HEAD_DIM = 128
Q_HEADS = 32
GROUP = 4
QW = 4096
CAP = 3
HALF_HEADS = KV_HEADS // 2
LANES = 128
CHIPS = 8
ROWS = 4
LINES = ROWS * GROUP
F32 = jnp.float32
BF16 = jnp.bfloat16
VMEM = pl.BlockSpec(memory_space=pltpu.VMEM)
SMEM = pl.BlockSpec(memory_space=pltpu.SMEM)
ANY = pl.BlockSpec(memory_space=pl.ANY)
PARTS = 4
PART = D_ENC // PARTS


def root_scale(values, gain):
    values = values.astype(F32)
    return (
        values
        * lax.rsqrt(jnp.mean(values * values, axis=-1, keepdims=True) + 1e-05)
        * gain.astype(F32)
    )


def rotary_lanes():
    position = np.arange(BLOCK, dtype=np.float64)[:, None]
    frequency = 10000.0 ** (-2.0 * np.arange(ENC_HD // 2) / ENC_HD)
    angle = position * frequency[None, :]
    cosine, sine = np.cos(angle), np.sin(angle)
    return (
        jnp.asarray(np.concatenate([cosine, cosine, cosine, cosine], axis=1), F32),
        jnp.asarray(np.concatenate([-sine, sine, -sine, sine], axis=1), F32),
    )


def live_counts(counts_ref):
    me = lax.axis_index("ctx")
    own, other = counts_ref[me], counts_ref[me + 1 - 2 * lax.rem(me, 2)]
    gives = jnp.where((own == 3) & (other == 1), 1, 0)
    takes = jnp.where((own == 1) & (other == 3), 1, 0)
    return own - gives + takes, other + gives - takes, takes


def query_kernel(query_ref, keep_ref, give_ref):
    core = lax.rem(lax.axis_index("ctx"), 2)
    width = GROUP * HEAD_DIM
    for out_ref, parity in ((keep_ref, core), (give_ref, 1 - core)):
        for head in range(HALF_HEADS):
            start = pl.multiple_of((2 * head + parity) * width, width)
            rows = query_ref[:, pl.ds(start, width)].astype(F32)
            out_ref[head] = jnp.concatenate(
                [rows[:, g * LANES : (g + 1) * LANES] for g in range(GROUP)], axis=0
            ).astype(BF16)


def split_queries(queries):
    shape = jax.ShapeDtypeStruct((HALF_HEADS, LINES, LANES), BF16)
    return pl.pallas_call(
        query_kernel, out_shape=(shape, shape), in_specs=[VMEM], out_specs=(VMEM, VMEM),
    )(queries)


def encoder_kernel(slot, counts_ref, context_ref, taken_ref, wq_ref, wk_ref, wv_ref, wo_ref, gain_ref, fgain_ref,
                   cos_ref, sin_ref, out_ref, mixed_ref, x_ref, q_buf, k_buf, v_buf, o_buf, sems, x_sem):
    live, _, takes = live_counts(counts_ref)

    @pl.when(live > slot)
    def _():
        if slot == 1:
            @pl.when(takes != 0)
            def _():
                pltpu.make_async_copy(taken_ref, x_ref, x_sem).start()

            @pl.when(takes == 0)
            def _():
                pltpu.make_async_copy(context_ref.at[slot], x_ref, x_sem).start()
        else:
            pltpu.make_async_copy(context_ref.at[slot], x_ref, x_sem).start()

        copies = []
        for part in range(PARTS):
            columns = slice(part * PART, (part + 1) * PART)
            copies.append([
                pltpu.make_async_copy(hbm.at[:, columns], buf.at[:, columns], sems.at[part, at])
                for at, (hbm, buf) in enumerate(((wq_ref, q_buf), (wk_ref, k_buf), (wv_ref, v_buf)))
            ])
        for group in copies:
            for copy in group:
                copy.start()
        out_copy = pltpu.make_async_copy(wo_ref, o_buf, sems.at[0, 3])
        out_copy.start()
        pltpu.make_async_copy(context_ref.at[slot], x_ref, x_sem).wait()

        normed = root_scale(x_ref[...], gain_ref[...]).astype(BF16)
        cosine, sine = cos_ref[...], sin_ref[...]
        cosine_query, sine_query = cosine * 0.125, sine * 0.125
        lane = lax.broadcasted_iota(jnp.int32, (BLOCK, LANES), 1)
        lower = (lane % ENC_HD) < ENC_HD // 2
        first = lane < ENC_HD

        def rotate(values, cosine, sine):
            swapped = jnp.where(
                lower,
                pltpu.roll(values, LANES - ENC_HD // 2, 1),
                pltpu.roll(values, ENC_HD // 2, 1),
            )
            return (values * cosine + swapped * sine).astype(BF16)

        for part in range(PARTS):
            columns = slice(part * PART, (part + 1) * PART)
            for copy in copies[part]:
                copy.wait()
            query = jnp.dot(normed, q_buf[:, columns], preferred_element_type=F32)
            key = jnp.dot(normed, k_buf[:, columns], preferred_element_type=F32)
            value = jnp.dot(normed, v_buf[:, columns], preferred_element_type=F32).astype(BF16)
            for pair in range(PART // LANES):
                cut = slice(pair * LANES, (pair + 1) * LANES)
                query_pair = rotate(query[:, cut], cosine_query, sine_query)
                key_pair = rotate(key[:, cut], cosine, sine)
                value_pair = value[:, cut]
                mixed = []
                for head in range(2):
                    own = first if head == 0 else jnp.logical_not(first)
                    scores = lax.dot_general(
                        jnp.where(own, query_pair, jnp.zeros_like(query_pair)), key_pair,
                        (((1,), (1,)), ((), ())), preferred_element_type=F32,
                    )
                    weights = jnp.exp(scores - jnp.max(scores, axis=-1, keepdims=True))
                    weights = weights * (1.0 / jnp.sum(weights, axis=-1, keepdims=True))
                    mixed.append(jnp.dot(weights.astype(BF16), value_pair, preferred_element_type=F32))
                start = part * PART + pair * LANES
                mixed_ref[:, start : start + LANES] = jnp.where(first, mixed[0], mixed[1]).astype(BF16)
        out_copy.wait()
        residual = x_ref[...].astype(F32) + jnp.dot(mixed_ref[...], o_buf[...], preferred_element_type=F32)
        out_ref[...] = root_scale(residual, fgain_ref[...]).astype(BF16)


def encode(slot, counts, context, taken, weights):
    square = pltpu.VMEM((D_ENC, D_ENC), BF16)
    return pl.pallas_call(
        functools.partial(encoder_kernel, slot),
        out_shape=jax.ShapeDtypeStruct((BLOCK, D_ENC), BF16),
        in_specs=[SMEM] + [ANY] * 6 + [VMEM] * 4,
        out_specs=VMEM,
        scratch_shapes=[
            pltpu.VMEM((BLOCK, D_ENC), BF16), pltpu.VMEM((BLOCK, D_ENC), BF16),
            square, square, square, square,
            pltpu.SemaphoreType.DMA((PARTS, 4)), pltpu.SemaphoreType.DMA,
        ],
        compiler_params=pltpu.CompilerParams(vmem_limit_bytes=48 * 2**20),
        cost_estimate=pl.CostEstimate(flops=6 * 10**9, bytes_accessed=9 * 2**20, transcendentals=2**20),
    )(counts, context, taken, *weights)


def three_parts(values):
    high = values.astype(BF16).astype(F32)
    middle = (values - high).astype(BF16).astype(F32)
    return high, middle, values - high - middle


def ring_chips(me):
    z, y = me // 4, lax.rem(me // 2, 2)
    place = jnp.where(z == 3, 2, jnp.where(z == 2, 3, z))
    chips = []
    for step in range(4):
        at = lax.rem(place + 4 - step, 4)
        z = jnp.where(at == 2, 3, jnp.where(at == 3, 2, at))
        chips.append((2 * z + y, 2 * z + 1 - y))
    return chips


def cross_kernel(counts_ref, *refs):
    tokens, loads, rows = refs[:6], refs[6:14], refs[14:18]
    out_ref, token_buf, weight_buf, query_buf, total_ref, top_ref, sum_ref, sems, token_sems, row_sems = refs[18:]
    me = lax.axis_index("ctx")
    core = lax.rem(me, 2)
    own_live, other_live, _ = live_counts(counts_ref)
    chips = ring_chips(me)
    copies = []
    for step in range(4):
        for side in range(2):
            start = pl.multiple_of(chips[step][side] * LANES, LANES)
            copies.append(pltpu.make_async_copy(
                loads[2 * step + side], weight_buf.at[:, pl.ds(start, LANES)], sems.at[2 * step + side]))
    for step in range(4):
        for side in range(2):
            for at, part in ((0, core), (1, 1 - core)):
                start = pl.multiple_of((2 * chips[step][side] + part) * LINES, LINES)
                copies.append(pltpu.make_async_copy(
                    rows[step].at[side, at], query_buf.at[:, pl.ds(start, LINES), :],
                    row_sems.at[4 * step + 2 * side + at]))

    def token_copy(at):
        return pltpu.make_async_copy(tokens[at], token_buf.at[at], token_sems.at[at])

    def live(at):
        return (own_live > at) if at < CAP else (other_live > at - CAP)

    for copy in copies:
        copy.start()
    for at in range(2 * CAP):
        @pl.when(live(at))
        def _():
            token_copy(at).start()
    total_ref[...] = jnp.zeros_like(total_ref)
    sum_ref[...] = jnp.zeros_like(sum_ref)
    top_ref[...] = jnp.full_like(top_ref, -jnp.inf)
    for copy in copies:
        copy.wait()

    for at in range(2 * CAP):
        @pl.when(live(at))
        def _():
            token_copy(at).wait()
            both = jnp.dot(token_buf[at], weight_buf[...], preferred_element_type=F32).astype(BF16)
            for head in range(HALF_HEADS):
                key = both[:, head * LANES : (head + 1) * LANES]
                value = both[:, (HALF_HEADS + head) * LANES : (HALF_HEADS + head + 1) * LANES]
                scores = lax.dot_general(
                    query_buf[head], key, (((1,), (1,)), ((), ())), preferred_element_type=F32
                ) * (1.0 / math.sqrt(HEAD_DIM))
                old_top = top_ref[head]
                new_top = jnp.maximum(old_top, jnp.max(scores, axis=-1, keepdims=True))
                weights = jnp.exp(scores - new_top[:, :1])
                shrink = jnp.exp(old_top - new_top)
                top_ref[head] = new_top
                sum_ref[head] = sum_ref[head] * shrink + jnp.sum(weights, axis=-1, keepdims=True)
                total_ref[head] = total_ref[head] * shrink + jnp.dot(
                    weights.astype(BF16), value, preferred_element_type=F32)

    lines = total_ref.shape[1]
    places = out_ref.shape[0] * 2
    lane = lax.broadcasted_iota(jnp.int32, (lines, LANES), 1)
    notes = jnp.zeros((lines, LANES), F32)
    for head in range(HALF_HEADS):
        pieces = three_parts(top_ref[head]) + three_parts(sum_ref[head])
        for at, piece in enumerate(pieces):
            notes = jnp.where(lane == 6 * head + at, piece, notes)
        out_ref[:, :, head] = total_ref[head].astype(BF16).reshape(places // 2, 2, LINES, LANES)
    out_ref[:, :, HALF_HEADS] = notes.astype(BF16).reshape(places // 2, 2, LINES, LANES)


def cross(counts, tokens, loads, rows):
    lines = 2 * CHIPS * LINES
    sums = pltpu.VMEM((HALF_HEADS, lines, LANES), F32)
    return pl.pallas_call(
        cross_kernel,
        out_shape=jax.ShapeDtypeStruct((CHIPS, 2, HALF_HEADS + 1, LINES, LANES), BF16),
        in_specs=[SMEM] + [ANY] * 18,
        out_specs=VMEM,
        scratch_shapes=[
            pltpu.VMEM((2 * CAP, BLOCK, D_ENC), BF16),
            pltpu.VMEM((D_ENC, KV_HEADS * LANES), BF16),
            pltpu.VMEM((HALF_HEADS, lines, LANES), BF16),
            sums, sums, sums,
            pltpu.SemaphoreType.DMA((8,)), pltpu.SemaphoreType.DMA((2 * CAP,)), pltpu.SemaphoreType.DMA((16,)),
        ],
        compiler_params=pltpu.CompilerParams(vmem_limit_bytes=40 * 2**20),
        cost_estimate=pl.CostEstimate(flops=6 * 10**9, bytes_accessed=8 * 2**20, transcendentals=2**20),
    )(counts, *tokens, *loads, *rows)


def combine_kernel(*refs):
    own_ref, arrived, (keep_ref, give_ref) = refs[0], refs[1:CHIPS], refs[CHIPS:]
    me = lax.axis_index("ctx")
    core, chip = lax.rem(me, 2), me // 2
    for out_ref, part in ((keep_ref, core), (give_ref, 1 - core)):
        pieces = [own_ref.at[chip, part]] + [ref.at[part] for ref in arrived]
        notes = [piece[HALF_HEADS].astype(F32) for piece in pieces]
        for head in range(HALF_HEADS):
            at = 6 * head
            tops = [n[:, at : at + 1] + n[:, at + 1 : at + 2] + n[:, at + 2 : at + 3] for n in notes]
            sums = [n[:, at + 3 : at + 4] + n[:, at + 4 : at + 5] + n[:, at + 5 : at + 6] for n in notes]
            top = functools.reduce(jnp.maximum, tops)
            numerator, denominator = 0.0, 0.0
            for share, amount, piece in zip([jnp.exp(t - top) for t in tops], sums, pieces):
                numerator += share * piece[head].astype(F32)
                denominator += share * amount
            out_ref[head] = (numerator / denominator).astype(BF16)


def combine(own, arrived):
    shape = jax.ShapeDtypeStruct((HALF_HEADS, LINES, LANES), BF16)
    return pl.pallas_call(
        combine_kernel, out_shape=(shape, shape), in_specs=[VMEM] * CHIPS, out_specs=(VMEM, VMEM),
    )(own, *arrived)


def place_kernel(keep_ref, got_ref, out_ref):
    core = lax.rem(lax.axis_index("ctx"), 2)
    for head in range(KV_HEADS):
        mine = core == head % 2
        lines = jnp.where(mine, keep_ref[head // 2].astype(F32), got_ref[head // 2].astype(F32))
        for g in range(GROUP):
            start = (head * GROUP + g) * LANES
            out_ref[:, start : start + LANES] = lines[g * ROWS : (g + 1) * ROWS].astype(BF16)


def put_in_place(keep, got):
    return pl.pallas_call(
        place_kernel, out_shape=jax.ShapeDtypeStruct((ROWS, QW), BF16), in_specs=[VMEM] * 2, out_specs=VMEM,
    )(keep, got)


NEXT_Z = (1, 3, 0, 2)


def exchange(values, bits):
    return lax.ppermute(values, "ctx", [(i, i ^ bits) for i in range(2 * CHIPS)])


def round_z(values):
    return lax.ppermute(values, "ctx", [(i, 4 * NEXT_Z[i // 4] + i % 4) for i in range(2 * CHIPS)])


def after(values, *others):
    return lax.optimization_barrier((values,) + others)[0]


def local(context, counts, queries, norm_gain, w_query, w_key, w_value, w_out, final_gain, w_kv):
    me = lax.axis_index("ctx")
    load0 = w_kv
    load1 = round_z(load0)
    beside0 = exchange(load0, 2)
    taken = exchange(context[2], 1)
    keep, give = split_queries(queries)
    row_chip = jnp.stack([keep, exchange(give, 1)])

    cosine, sine = rotary_lanes()
    weights = (w_query, w_key, w_value, w_out, norm_gain[None], final_gain[None], cosine, sine)
    token0 = encode(0, counts, context, context, weights)
    load1, row_chip, token0, taken = lax.optimization_barrier((load1, row_chip, token0, taken))
    load2 = round_z(load1)
    beside1 = exchange(load1, 2)
    far0 = exchange(token0, 1)
    row_beside = exchange(row_chip, 2)
    token1 = encode(1, counts, context, taken, weights)
    load2, token1, row_beside = lax.optimization_barrier((load2, token1, row_beside))
    load3 = round_z(load2)
    beside2 = exchange(load2, 2)
    far1 = exchange(token1, 1)
    rows0 = jnp.stack([row_chip, row_beside])
    rows1 = round_z(rows0)
    token2 = encode(2, counts, context, context, weights)
    load3, token2, rows1 = lax.optimization_barrier((load3, token2, rows1))
    beside3 = exchange(load3, 2)
    far2 = exchange(token2, 1)
    rows2 = round_z(rows1)
    rows3 = round_z(rows2)

    parts = cross(
        counts, (token0, token1, token2, far0, far1, far2),
        (load0, beside0, load1, beside1, load2, beside2, load3, beside3),
        (rows0, rows1, rows2, rows3),
    )
    arrived = [
        exchange(lax.dynamic_index_in_dim(parts, (me // 2) ^ chip, keepdims=False), 2 * chip)
        for chip in range(1, CHIPS)
    ]
    keep, give = combine(parts, arrived)
    return put_in_place(keep, exchange(give, 1))


def rotary_tables(length, head_width):
    position = jnp.arange(length).astype(jnp.float32)[:, None]
    frequency = jnp.exp(
        jnp.arange(head_width // 2).astype(jnp.float32) * (-2.0 * math.log(10000.0) / head_width)
    )
    phase_angle = position * frequency[None, :]
    return (jnp.cos(phase_angle)[:, None, :], jnp.sin(phase_angle)[:, None, :])


def rotate(values, cosine_table, sine_table):
    half_width = values.shape[-1] // 2
    lower_half = values[..., :half_width]
    upper_half = values[..., half_width:]
    return jnp.concatenate(
        [
            lower_half * cosine_table - upper_half * sine_table,
            upper_half * cosine_table + lower_half * sine_table,
        ],
        axis=-1,
    )


def weighted_sums(cross_scores, top_scores, key_alive, cross_values):
    cross_weights = jnp.where(key_alive, jnp.exp(cross_scores - top_scores[..., None]), 0.0)
    total_rows = cross_scores.shape[0]
    denominator = jnp.sum(cross_weights, axis=-1).reshape(total_rows, Q_HEADS)
    numerator = jnp.einsum(
        "rkgt,tkd->rkgd",
        cross_weights.astype(jnp.bfloat16),
        cross_values,
        preferred_element_type=jnp.float32,
    )
    return (numerator.reshape(total_rows, QW), denominator)


def local_any(context, counts, queries, norm_gain, w_query, w_key, w_value, w_out, final_gain, w_kv):
    places = lax.axis_size("ctx")
    device_index = lax.axis_index("ctx")
    device_number = jnp.arange(places)
    own_count = jnp.sum(jnp.where(device_number == device_index, counts, 0))
    alive_slot = jnp.arange(CAP) < own_count
    slot_count = context.shape[0]
    row_count = slot_count * BLOCK
    normed = root_scale(context, norm_gain).astype(jnp.bfloat16).reshape(row_count, D_ENC)
    cosine_table, sine_table = rotary_tables(BLOCK, ENC_HD)

    def project(weight):
        return jnp.dot(normed, weight, preferred_element_type=jnp.float32).reshape(
            slot_count, BLOCK, ENC_HEADS, ENC_HD
        )

    query_rows = rotate(project(w_query), cosine_table, sine_table).astype(jnp.bfloat16)
    key_rows = rotate(project(w_key), cosine_table, sine_table).astype(jnp.bfloat16)
    value_rows = project(w_value).astype(jnp.bfloat16)
    scores = jnp.einsum(
        "sqhd,skhd->shqk", query_rows, key_rows, preferred_element_type=jnp.float32
    ) / math.sqrt(ENC_HD)
    weights = jax.nn.softmax(scores, axis=-1).astype(jnp.bfloat16)
    mixed_rows = jnp.einsum(
        "shqk,skhd->sqhd", weights, value_rows, preferred_element_type=jnp.float32
    )
    mixed_rows = mixed_rows.astype(jnp.bfloat16).reshape(row_count, D_ENC)
    residual = context.reshape(row_count, D_ENC).astype(jnp.float32) + jnp.dot(
        mixed_rows, w_out, preferred_element_type=jnp.float32
    )
    final_norm = root_scale(residual, final_gain).astype(jnp.bfloat16)
    key_value = jnp.dot(
        final_norm,
        lax.all_gather(w_kv, "ctx", axis=1, tiled=True),
        preferred_element_type=jnp.float32,
    ).astype(jnp.bfloat16)
    cross_keys = key_value[:, : KV_HEADS * HEAD_DIM].reshape(row_count, KV_HEADS, HEAD_DIM)
    cross_values = key_value[:, KV_HEADS * HEAD_DIM :].reshape(row_count, KV_HEADS, HEAD_DIM)
    every_query = lax.all_gather(queries, "ctx", axis=0, tiled=True)
    total_rows = every_query.shape[0]
    grouped = every_query.reshape(total_rows, KV_HEADS, GROUP, HEAD_DIM)
    cross_scores = jnp.einsum(
        "rkgd,tkd->rkgt", grouped, cross_keys, preferred_element_type=jnp.float32
    ) / math.sqrt(HEAD_DIM)
    key_alive = jnp.repeat(alive_slot, BLOCK)
    local_top = jnp.max(jnp.where(key_alive, cross_scores, -jnp.inf), axis=-1)
    row_top = lax.pmax(local_top.astype(jnp.bfloat16), "ctx").astype(local_top.dtype)
    numerator, denominator = weighted_sums(cross_scores, row_top, key_alive, cross_values)
    own_numerator, own_denominator = (
        lax.psum_scatter(numerator, "ctx", scatter_dimension=0, tiled=True),
        lax.psum_scatter(denominator, "ctx", scatter_dimension=0, tiled=True),
    )
    own_rows = own_numerator.shape[0]
    result = own_numerator.reshape(own_rows, Q_HEADS, HEAD_DIM) / own_denominator[..., None]
    return result.reshape(own_rows, QW).astype(jnp.bfloat16)


def solution(mesh):
    in_specs = (
        P(("groups", "ctx"), None, None),
        P("groups"),
        P(("groups", "ctx"), None),
        P(),
        P(),
        P(),
        P(),
        P(),
        P(),
        P(None, "ctx"),
    )
    out_specs = P(("groups", "ctx"), None)
    small = mesh.shape["ctx"] == 2 * CHIPS
    return jax.shard_map(local if small else local_any, mesh=mesh, in_specs=in_specs, out_specs=out_specs, check_vma=False)
```

```python
import functools
import math

import jax
import jax.numpy as jnp
import numpy as np
from jax import lax
from jax.experimental import pallas as pl
from jax.experimental.pallas import tpu as pltpu
from jax.sharding import PartitionSpec as P

D_ENC = 1024
ENC_HEADS = 16
ENC_HD = 64
BLOCK = 256
KV_HEADS = 8
HEAD_DIM = 128
Q_HEADS = 32
GROUP = 4
QW = 4096
CAP = 3
HALF_HEADS = KV_HEADS // 2
LANES = 128
CHIPS = 8
ROWS = 4
LINES = ROWS * GROUP
F32 = jnp.float32
BF16 = jnp.bfloat16
VMEM = pl.BlockSpec(memory_space=pltpu.VMEM)
SMEM = pl.BlockSpec(memory_space=pltpu.SMEM)
HBM = pl.BlockSpec(memory_space=pltpu.HBM)
PARTS = 4
PART = D_ENC // PARTS


def root_scale(values, gain):
    values = values.astype(F32)
    return (
        values
        * lax.rsqrt(jnp.mean(values * values, axis=-1, keepdims=True) + 1e-05)
        * gain.astype(F32)
    )


def rotary_lanes():
    position = np.arange(BLOCK, dtype=np.float64)[:, None]
    frequency = 10000.0 ** (-2.0 * np.arange(ENC_HD // 2) / ENC_HD)
    angle = position * frequency[None, :]
    cosine, sine = np.cos(angle), np.sin(angle)
    return (
        jnp.asarray(np.concatenate([cosine, cosine, cosine, cosine], axis=1), F32),
        jnp.asarray(np.concatenate([-sine, sine, -sine, sine], axis=1), F32),
    )


def live_counts(counts_ref):
    me = lax.axis_index("ctx")
    own, other = counts_ref[me], counts_ref[me + 1 - 2 * lax.rem(me, 2)]
    gives = jnp.where((own == 3) & (other == 1), 1, 0)
    takes = jnp.where((own == 1) & (other == 3), 1, 0)
    return own - gives + takes, other + gives - takes, takes


def query_kernel(query_ref, keep_ref, give_ref):
    core = lax.rem(lax.axis_index("ctx"), 2)
    width = GROUP * HEAD_DIM
    for out_ref, parity in ((keep_ref, core), (give_ref, 1 - core)):
        for head in range(HALF_HEADS):
            start = pl.multiple_of((2 * head + parity) * width, width)
            rows = query_ref[:, pl.ds(start, width)].astype(F32)
            out_ref[head] = jnp.concatenate(
                [rows[:, g * LANES : (g + 1) * LANES] for g in range(GROUP)], axis=0
            ).astype(BF16)


def split_queries(queries):
    shape = jax.ShapeDtypeStruct((HALF_HEADS, LINES, LANES), BF16)
    return pl.pallas_call(
        query_kernel, out_shape=(shape, shape), in_specs=[VMEM], out_specs=(VMEM, VMEM),
    )(queries)


def encoder_kernel(slot, counts_ref, context_ref, taken_ref, wq_ref, wk_ref, wv_ref, wo_ref, gain_ref, fgain_ref,
                   cos_ref, sin_ref, out_ref, mixed_ref, x_ref, q_buf, k_buf, v_buf, o_buf, sems, x_sem):
    live, _, takes = live_counts(counts_ref)

    @pl.when(live > slot)
    def _():
        if slot == 1:
            @pl.when(takes != 0)
            def _():
                pltpu.make_async_copy(taken_ref, x_ref, x_sem).start()

            @pl.when(takes == 0)
            def _():
                pltpu.make_async_copy(context_ref.at[slot], x_ref, x_sem).start()
        else:
            pltpu.make_async_copy(context_ref.at[slot], x_ref, x_sem).start()

        copies = []
        for part in range(PARTS):
            columns = slice(part * PART, (part + 1) * PART)
            copies.append([
                pltpu.make_async_copy(hbm.at[:, columns], buf.at[:, columns], sems.at[part, at])
                for at, (hbm, buf) in enumerate(((wq_ref, q_buf), (wk_ref, k_buf), (wv_ref, v_buf)))
            ])
        for group in copies:
            for copy in group:
                copy.start()
        out_copy = pltpu.make_async_copy(wo_ref, o_buf, sems.at[0, 3])
        out_copy.start()
        pltpu.make_async_copy(context_ref.at[slot], x_ref, x_sem).wait()

        normed = root_scale(x_ref[...], gain_ref[...]).astype(BF16)
        cosine, sine = cos_ref[...], sin_ref[...]
        cosine_query, sine_query = cosine * 0.125, sine * 0.125
        lane = lax.broadcasted_iota(jnp.int32, (BLOCK, LANES), 1)
        lower = (lane % ENC_HD) < ENC_HD // 2
        first = lane < ENC_HD

        def rotate(values, cosine, sine):
            swapped = jnp.where(
                lower,
                pltpu.roll(values, LANES - ENC_HD // 2, 1),
                pltpu.roll(values, ENC_HD // 2, 1),
            )
            return (values * cosine + swapped * sine).astype(BF16)

        for part in range(PARTS):
            columns = slice(part * PART, (part + 1) * PART)
            for copy in copies[part]:
                copy.wait()
            query = jnp.dot(normed, q_buf[:, columns], preferred_element_type=F32)
            key = jnp.dot(normed, k_buf[:, columns], preferred_element_type=F32)
            value = jnp.dot(normed, v_buf[:, columns], preferred_element_type=F32).astype(BF16)
            for pair in range(PART // LANES):
                cut = slice(pair * LANES, (pair + 1) * LANES)
                query_pair = rotate(query[:, cut], cosine_query, sine_query)
                key_pair = rotate(key[:, cut], cosine, sine)
                value_pair = value[:, cut]
                mixed = []
                for head in range(2):
                    own = first if head == 0 else jnp.logical_not(first)
                    scores = lax.dot_general(
                        jnp.where(own, query_pair, jnp.zeros_like(query_pair)), key_pair,
                        (((1,), (1,)), ((), ())), preferred_element_type=F32,
                    )
                    weights = jnp.exp(scores - jnp.max(scores, axis=-1, keepdims=True))
                    weights = weights * (1.0 / jnp.sum(weights, axis=-1, keepdims=True))
                    mixed.append(jnp.dot(weights.astype(BF16), value_pair, preferred_element_type=F32))
                start = part * PART + pair * LANES
                mixed_ref[:, start : start + LANES] = jnp.where(first, mixed[0], mixed[1]).astype(BF16)
        out_copy.wait()
        residual = x_ref[...].astype(F32) + jnp.dot(mixed_ref[...], o_buf[...], preferred_element_type=F32)
        out_ref[...] = root_scale(residual, fgain_ref[...]).astype(BF16)


def encode(slot, counts, context, taken, weights):
    square = pltpu.VMEM((D_ENC, D_ENC), BF16)
    return pl.pallas_call(
        functools.partial(encoder_kernel, slot),
        out_shape=jax.ShapeDtypeStruct((BLOCK, D_ENC), BF16),
        in_specs=[SMEM] + [HBM] * 6 + [VMEM] * 4,
        out_specs=VMEM,
        scratch_shapes=[
            pltpu.VMEM((BLOCK, D_ENC), BF16), pltpu.VMEM((BLOCK, D_ENC), BF16),
            square, square, square, square,
            pltpu.SemaphoreType.DMA((PARTS, 4)), pltpu.SemaphoreType.DMA,
        ],
        compiler_params=pltpu.CompilerParams(vmem_limit_bytes=63 * 2**20),
        cost_estimate=pl.CostEstimate(flops=6 * 10**9, bytes_accessed=9 * 2**20, transcendentals=2**20),
    )(counts, context, taken, *weights)


def three_parts(values):
    high = values.astype(BF16).astype(F32)
    middle = (values - high).astype(BF16).astype(F32)
    return high, middle, values - high - middle


def ring_chips(me):
    z, y = me // 4, lax.rem(me // 2, 2)
    place = jnp.where(z == 3, 2, jnp.where(z == 2, 3, z))
    chips = []
    for step in range(4):
        at = lax.rem(place + 4 - step, 4)
        z = jnp.where(at == 2, 3, jnp.where(at == 3, 2, at))
        chips.append((2 * z + y, 2 * z + 1 - y))
    return chips


def cross_kernel(counts_ref, *refs):
    tokens, loads, rows = refs[:6], refs[6:14], refs[14:18]
    out_ref, token_buf, weight_buf, query_buf, total_ref, top_ref, sum_ref, sems, token_sems, row_sems = refs[18:]
    me = lax.axis_index("ctx")
    core = lax.rem(me, 2)
    own_live, other_live, _ = live_counts(counts_ref)
    chips = ring_chips(me)
    copies = []
    for step in range(4):
        for side in range(2):
            start = pl.multiple_of(chips[step][side] * LANES, LANES)
            copies.append(pltpu.make_async_copy(
                loads[2 * step + side], weight_buf.at[:, pl.ds(start, LANES)], sems.at[2 * step + side]))
    for step in range(4):
        for side in range(2):
            for at, part in ((0, core), (1, 1 - core)):
                start = pl.multiple_of((2 * chips[step][side] + part) * LINES, LINES)
                copies.append(pltpu.make_async_copy(
                    rows[step].at[side, at], query_buf.at[:, pl.ds(start, LINES), :],
                    row_sems.at[4 * step + 2 * side + at]))

    def token_copy(at):
        return pltpu.make_async_copy(tokens[at], token_buf.at[at], token_sems.at[at])

    def live(at):
        return (own_live > at) if at < CAP else (other_live > at - CAP)

    for copy in copies:
        copy.start()
    for at in range(2 * CAP):
        @pl.when(live(at))
        def _():
            token_copy(at).start()
    total_ref[...] = jnp.zeros_like(total_ref)
    sum_ref[...] = jnp.zeros_like(sum_ref)
    top_ref[...] = jnp.full_like(top_ref, -jnp.inf)
    for copy in copies:
        copy.wait()

    for at in range(2 * CAP):
        @pl.when(live(at))
        def _():
            token_copy(at).wait()
            both = jnp.dot(token_buf[at], weight_buf[...], preferred_element_type=F32).astype(BF16)
            for head in range(HALF_HEADS):
                key = both[:, head * LANES : (head + 1) * LANES]
                value = both[:, (HALF_HEADS + head) * LANES : (HALF_HEADS + head + 1) * LANES]
                scores = lax.dot_general(
                    query_buf[head], key, (((1,), (1,)), ((), ())), preferred_element_type=F32
                ) * (1.0 / math.sqrt(HEAD_DIM))
                old_top = top_ref[head]
                new_top = jnp.maximum(old_top, jnp.max(scores, axis=-1, keepdims=True))
                weights = jnp.exp(scores - new_top[:, :1])
                shrink = jnp.exp(old_top - new_top)
                top_ref[head] = new_top
                sum_ref[head] = sum_ref[head] * shrink + jnp.sum(weights, axis=-1, keepdims=True)
                total_ref[head] = total_ref[head] * shrink + jnp.dot(
                    weights.astype(BF16), value, preferred_element_type=F32)

    lines = total_ref.shape[1]
    places = out_ref.shape[0] * 2
    lane = lax.broadcasted_iota(jnp.int32, (lines, LANES), 1)
    notes = jnp.zeros((lines, LANES), F32)
    for head in range(HALF_HEADS):
        pieces = three_parts(top_ref[head]) + three_parts(sum_ref[head])
        for at, piece in enumerate(pieces):
            notes = jnp.where(lane == 6 * head + at, piece, notes)
        out_ref[:, :, head] = total_ref[head].astype(BF16).reshape(places // 2, 2, LINES, LANES)
    out_ref[:, :, HALF_HEADS] = notes.astype(BF16).reshape(places // 2, 2, LINES, LANES)


def cross(counts, tokens, loads, rows):
    lines = 2 * CHIPS * LINES
    sums = pltpu.VMEM((HALF_HEADS, lines, LANES), F32)
    return pl.pallas_call(
        cross_kernel,
        out_shape=jax.ShapeDtypeStruct((CHIPS, 2, HALF_HEADS + 1, LINES, LANES), BF16),
        in_specs=[SMEM] + [HBM] * 18,
        out_specs=VMEM,
        scratch_shapes=[
            pltpu.VMEM((2 * CAP, BLOCK, D_ENC), BF16),
            pltpu.VMEM((D_ENC, KV_HEADS * LANES), BF16),
            pltpu.VMEM((HALF_HEADS, lines, LANES), BF16),
            sums, sums, sums,
            pltpu.SemaphoreType.DMA((8,)), pltpu.SemaphoreType.DMA((2 * CAP,)), pltpu.SemaphoreType.DMA((16,)),
        ],
        compiler_params=pltpu.CompilerParams(vmem_limit_bytes=63 * 2**20),
        cost_estimate=pl.CostEstimate(flops=6 * 10**9, bytes_accessed=8 * 2**20, transcendentals=2**20),
    )(counts, *tokens, *loads, *rows)


def combine_kernel(*refs):
    own_ref, arrived, (keep_ref, give_ref) = refs[0], refs[1:CHIPS], refs[CHIPS:]
    me = lax.axis_index("ctx")
    core, chip = lax.rem(me, 2), me // 2
    for out_ref, part in ((keep_ref, core), (give_ref, 1 - core)):
        pieces = [own_ref.at[chip, part]] + [ref.at[part] for ref in arrived]
        notes = [piece[HALF_HEADS].astype(F32) for piece in pieces]
        for head in range(HALF_HEADS):
            at = 6 * head
            tops = [n[:, at : at + 1] + n[:, at + 1 : at + 2] + n[:, at + 2 : at + 3] for n in notes]
            sums = [n[:, at + 3 : at + 4] + n[:, at + 4 : at + 5] + n[:, at + 5 : at + 6] for n in notes]
            top = functools.reduce(jnp.maximum, tops)
            numerator, denominator = 0.0, 0.0
            for share, amount, piece in zip([jnp.exp(t - top) for t in tops], sums, pieces):
                numerator += share * piece[head].astype(F32)
                denominator += share * amount
            out_ref[head] = (numerator / denominator).astype(BF16)


def combine(own, arrived):
    shape = jax.ShapeDtypeStruct((HALF_HEADS, LINES, LANES), BF16)
    return pl.pallas_call(
        combine_kernel, out_shape=(shape, shape), in_specs=[VMEM] * CHIPS, out_specs=(VMEM, VMEM),
    )(own, *arrived)


def place_kernel(keep_ref, got_ref, out_ref):
    core = lax.rem(lax.axis_index("ctx"), 2)
    for head in range(KV_HEADS):
        mine = core == head % 2
        lines = jnp.where(mine, keep_ref[head // 2].astype(F32), got_ref[head // 2].astype(F32))
        for g in range(GROUP):
            start = (head * GROUP + g) * LANES
            out_ref[:, start : start + LANES] = lines[g * ROWS : (g + 1) * ROWS].astype(BF16)


def put_in_place(keep, got):
    return pl.pallas_call(
        place_kernel, out_shape=jax.ShapeDtypeStruct((ROWS, QW), BF16), in_specs=[VMEM] * 2, out_specs=VMEM,
    )(keep, got)


NEXT_Z = (1, 3, 0, 2)


def exchange(values, bits):
    return lax.ppermute(values, "ctx", [(i, i ^ bits) for i in range(2 * CHIPS)])


def round_z(values):
    return lax.ppermute(values, "ctx", [(i, 4 * NEXT_Z[i // 4] + i % 4) for i in range(2 * CHIPS)])


def after(values, *others):
    return lax.optimization_barrier((values,) + others)[0]


def local(context, counts, queries, norm_gain, w_query, w_key, w_value, w_out, final_gain, w_kv):
    me = lax.axis_index("ctx")
    load0 = w_kv
    load1 = round_z(load0)
    beside0 = exchange(load0, 2)
    taken = exchange(context[2], 1)
    keep, give = split_queries(queries)
    row_chip = jnp.stack([keep, exchange(give, 1)])

    cosine, sine = rotary_lanes()
    weights = (w_query, w_key, w_value, w_out, norm_gain[None], final_gain[None], cosine, sine)
    token0 = encode(0, counts, context, context, weights)
    load1, row_chip, token0, taken = lax.optimization_barrier((load1, row_chip, token0, taken))
    load2 = round_z(load1)
    beside1 = exchange(load1, 2)
    far0 = exchange(token0, 1)
    row_beside = exchange(row_chip, 2)
    token1 = encode(1, after(counts, beside0), context, taken, weights)
    load2, token1, row_beside = lax.optimization_barrier((load2, token1, row_beside))
    load3 = round_z(load2)
    beside2 = exchange(load2, 2)
    far1 = exchange(token1, 1)
    rows0 = jnp.stack([row_chip, row_beside])
    rows1 = round_z(rows0)
    token2 = encode(2, after(counts, beside1, far0), context, context, weights)
    load3, token2, rows1 = lax.optimization_barrier((load3, token2, rows1))
    beside3 = exchange(load3, 2)
    far2 = exchange(token2, 1)
    rows2 = round_z(rows1)
    rows3 = round_z(rows2)

    parts = cross(
        counts, (token0, token1, token2, far0, far1, far2),
        (load0, beside0, load1, beside1, load2, beside2, load3, beside3),
        (rows0, rows1, rows2, rows3),
    )
    arrived = [
        exchange(lax.dynamic_index_in_dim(parts, (me // 2) ^ chip, keepdims=False), 2 * chip)
        for chip in range(1, CHIPS)
    ]
    keep, give = combine(parts, arrived)
    return put_in_place(keep, exchange(give, 1))


def rotary_tables(length, head_width):
    position = jnp.arange(length).astype(jnp.float32)[:, None]
    frequency = jnp.exp(
        jnp.arange(head_width // 2).astype(jnp.float32) * (-2.0 * math.log(10000.0) / head_width)
    )
    phase_angle = position * frequency[None, :]
    return (jnp.cos(phase_angle)[:, None, :], jnp.sin(phase_angle)[:, None, :])


def rotate(values, cosine_table, sine_table):
    half_width = values.shape[-1] // 2
    lower_half = values[..., :half_width]
    upper_half = values[..., half_width:]
    return jnp.concatenate(
        [
            lower_half * cosine_table - upper_half * sine_table,
            upper_half * cosine_table + lower_half * sine_table,
        ],
        axis=-1,
    )


def weighted_sums(cross_scores, top_scores, key_alive, cross_values):
    cross_weights = jnp.where(key_alive, jnp.exp(cross_scores - top_scores[..., None]), 0.0)
    total_rows = cross_scores.shape[0]
    denominator = jnp.sum(cross_weights, axis=-1).reshape(total_rows, Q_HEADS)
    numerator = jnp.einsum(
        "rkgt,tkd->rkgd",
        cross_weights.astype(jnp.bfloat16),
        cross_values,
        preferred_element_type=jnp.float32,
    )
    return (numerator.reshape(total_rows, QW), denominator)


def local_any(context, counts, queries, norm_gain, w_query, w_key, w_value, w_out, final_gain, w_kv):
    places = lax.axis_size("ctx")
    device_index = lax.axis_index("ctx")
    device_number = jnp.arange(places)
    own_count = jnp.sum(jnp.where(device_number == device_index, counts, 0))
    alive_slot = jnp.arange(CAP) < own_count
    slot_count = context.shape[0]
    row_count = slot_count * BLOCK
    normed = root_scale(context, norm_gain).astype(jnp.bfloat16).reshape(row_count, D_ENC)
    cosine_table, sine_table = rotary_tables(BLOCK, ENC_HD)

    def project(weight):
        return jnp.dot(normed, weight, preferred_element_type=jnp.float32).reshape(
            slot_count, BLOCK, ENC_HEADS, ENC_HD
        )

    query_rows = rotate(project(w_query), cosine_table, sine_table).astype(jnp.bfloat16)
    key_rows = rotate(project(w_key), cosine_table, sine_table).astype(jnp.bfloat16)
    value_rows = project(w_value).astype(jnp.bfloat16)
    scores = jnp.einsum(
        "sqhd,skhd->shqk", query_rows, key_rows, preferred_element_type=jnp.float32
    ) / math.sqrt(ENC_HD)
    weights = jax.nn.softmax(scores, axis=-1).astype(jnp.bfloat16)
    mixed_rows = jnp.einsum(
        "shqk,skhd->sqhd", weights, value_rows, preferred_element_type=jnp.float32
    )
    mixed_rows = mixed_rows.astype(jnp.bfloat16).reshape(row_count, D_ENC)
    residual = context.reshape(row_count, D_ENC).astype(jnp.float32) + jnp.dot(
        mixed_rows, w_out, preferred_element_type=jnp.float32
    )
    final_norm = root_scale(residual, final_gain).astype(jnp.bfloat16)
    key_value = jnp.dot(
        final_norm,
        lax.all_gather(w_kv, "ctx", axis=1, tiled=True),
        preferred_element_type=jnp.float32,
    ).astype(jnp.bfloat16)
    cross_keys = key_value[:, : KV_HEADS * HEAD_DIM].reshape(row_count, KV_HEADS, HEAD_DIM)
    cross_values = key_value[:, KV_HEADS * HEAD_DIM :].reshape(row_count, KV_HEADS, HEAD_DIM)
    every_query = lax.all_gather(queries, "ctx", axis=0, tiled=True)
    total_rows = every_query.shape[0]
    grouped = every_query.reshape(total_rows, KV_HEADS, GROUP, HEAD_DIM)
    cross_scores = jnp.einsum(
        "rkgd,tkd->rkgt", grouped, cross_keys, preferred_element_type=jnp.float32
    ) / math.sqrt(HEAD_DIM)
    key_alive = jnp.repeat(alive_slot, BLOCK)
    local_top = jnp.max(jnp.where(key_alive, cross_scores, -jnp.inf), axis=-1)
    row_top = lax.pmax(local_top.astype(jnp.bfloat16), "ctx").astype(local_top.dtype)
    numerator, denominator = weighted_sums(cross_scores, row_top, key_alive, cross_values)
    own_numerator, own_denominator = (
        lax.psum_scatter(numerator, "ctx", scatter_dimension=0, tiled=True),
        lax.psum_scatter(denominator, "ctx", scatter_dimension=0, tiled=True),
    )
    own_rows = own_numerator.shape[0]
    result = own_numerator.reshape(own_rows, Q_HEADS, HEAD_DIM) / own_denominator[..., None]
    return result.reshape(own_rows, QW).astype(jnp.bfloat16)


def solution(mesh):
    in_specs = (
        P(("groups", "ctx"), None, None),
        P("groups"),
        P(("groups", "ctx"), None),
        P(),
        P(),
        P(),
        P(),
        P(),
        P(),
        P(None, "ctx"),
    )
    out_specs = P(("groups", "ctx"), None)
    small = mesh.shape["ctx"] == 2 * CHIPS
    return jax.shard_map(local if small else local_any, mesh=mesh, in_specs=in_specs, out_specs=out_specs, check_vma=False)
```

```python
import functools
import math

import jax
import jax.numpy as jnp
import numpy as np
from jax import lax
from jax.experimental import pallas as pl
from jax.experimental.pallas import tpu as pltpu
from jax.sharding import PartitionSpec as P

D_ENC = 1024
ENC_HEADS = 16
ENC_HD = 64
BLOCK = 256
KV_HEADS = 8
HEAD_DIM = 128
Q_HEADS = 32
GROUP = 4
QW = 4096
CAP = 3
HALF_HEADS = KV_HEADS // 2
LANES = 128
CHIPS = 8
ROWS = 4
LINES = ROWS * GROUP
F32 = jnp.float32
BF16 = jnp.bfloat16
VMEM = pl.BlockSpec(memory_space=pltpu.VMEM)
SMEM = pl.BlockSpec(memory_space=pltpu.SMEM)
HBM = pl.BlockSpec(memory_space=pltpu.HBM)
PARTS = 4
PART = D_ENC // PARTS


def root_scale(values, gain):
    values = values.astype(F32)
    return (
        values
        * lax.rsqrt(jnp.mean(values * values, axis=-1, keepdims=True) + 1e-05)
        * gain.astype(F32)
    )


def rotary_lanes():
    position = np.arange(BLOCK, dtype=np.float64)[:, None]
    frequency = 10000.0 ** (-2.0 * np.arange(ENC_HD // 2) / ENC_HD)
    angle = position * frequency[None, :]
    cosine, sine = np.cos(angle), np.sin(angle)
    return jnp.asarray(np.stack([
        np.concatenate([cosine, cosine, cosine, cosine], axis=1),
        np.concatenate([-sine, sine, -sine, sine], axis=1),
    ]), F32)


def live_counts(counts_ref):
    me = lax.axis_index("ctx")
    own, other = counts_ref[me], counts_ref[me + 1 - 2 * lax.rem(me, 2)]
    gives = jnp.where((own == 3) & (other == 1), 1, 0)
    takes = jnp.where((own == 1) & (other == 3), 1, 0)
    return own - gives + takes, other + gives - takes, takes


def split_rows(query_ref, keep_ref, give_ref):
    core = lax.rem(lax.axis_index("ctx"), 2)
    width = GROUP * HEAD_DIM
    for out_ref, parity in ((keep_ref, core), (give_ref, 1 - core)):
        for head in range(HALF_HEADS):
            start = pl.multiple_of((2 * head + parity) * width, width)
            rows = query_ref[:, pl.ds(start, width)].astype(F32)
            out_ref[head] = jnp.concatenate(
                [rows[:, g * LANES : (g + 1) * LANES] for g in range(GROUP)], axis=0
            ).astype(BF16)


def encoder_kernel(slot, counts_ref, context_ref, taken_ref, wq_ref, wk_ref, wv_ref, wo_ref, table_ref, gain_ref,
                   fgain_ref, *refs):
    rows_in, refs = refs[: 2 if slot else 1], refs[2 if slot else 1 :]
    out_ref, refs = refs[0], refs[1:]
    rows_out, refs = refs[: 1 if slot else 2], refs[1 if slot else 2 :]
    mixed_ref, x_ref, q_ref, k_ref, v_ref, final_ref, table_buf, q_buf, k_buf, v_buf, o_buf, sems = refs
    live, _, takes = live_counts(counts_ref)
    copies = [
        pltpu.make_async_copy(hbm, buf, sems.at[at])
        for at, (hbm, buf) in enumerate(
            ((context_ref.at[slot], x_ref), (wq_ref, q_buf), (table_ref, table_buf), (wk_ref, k_buf),
             (wv_ref, v_buf), (wo_ref, o_buf)))
    ]

    @pl.when(live > slot)
    def _():
        if slot == 1:
            @pl.when(takes != 0)
            def _():
                pltpu.make_async_copy(taken_ref.at[CAP - 1], x_ref, sems.at[0]).start()

            @pl.when(takes == 0)
            def _():
                copies[0].start()
        else:
            copies[0].start()
        for copy in copies[1:]:
            copy.start()

    if slot == 0:
        split_rows(rows_in[0], rows_out[0], rows_out[1])
    else:
        rows_out[0][0] = rows_in[0][...]
        rows_out[0][1] = rows_in[1][...]

    @pl.when(live > slot)
    def _():
        copies[0].wait()
        normed = root_scale(x_ref[...], gain_ref[...]).astype(BF16)
        copies[1].wait()
        copies[2].wait()
        cosine, sine = table_buf[0], table_buf[1]
        lane = lax.broadcasted_iota(jnp.int32, (BLOCK, LANES), 1)
        lower = (lane % ENC_HD) < ENC_HD // 2
        first = lane < ENC_HD

        def project(buf, to_ref, cosine, sine):
            for part in range(PARTS):
                values = jnp.dot(normed, buf[:, part * PART : (part + 1) * PART], preferred_element_type=F32)
                for at in range(PART // LANES):
                    cut = values[:, at * LANES : (at + 1) * LANES]
                    swapped = jnp.where(
                        lower, pltpu.roll(cut, LANES - ENC_HD // 2, 1), pltpu.roll(cut, ENC_HD // 2, 1))
                    start = part * PART + at * LANES
                    to_ref[:, start : start + LANES] = (cut * cosine + swapped * sine).astype(BF16)

        project(q_buf, q_ref, cosine * 0.125, sine * 0.125)
        copies[3].wait()
        project(k_buf, k_ref, cosine, sine)
        copies[4].wait()
        v_ref[...] = jnp.dot(normed, v_buf[...], preferred_element_type=F32).astype(BF16)
        for pair in range(ENC_HEADS // 2):
            cut = slice(pair * LANES, (pair + 1) * LANES)
            query, key, value = q_ref[:, cut], k_ref[:, cut], v_ref[:, cut]
            mixed = []
            for own in (first, jnp.logical_not(first)):
                scores = lax.dot_general(
                    key, jnp.where(own, query, jnp.zeros_like(query)),
                    (((1,), (1,)), ((), ())), preferred_element_type=F32)
                weights = jnp.exp(scores - jnp.max(scores, axis=0, keepdims=True))
                weights = (weights * (1.0 / jnp.sum(weights, axis=0, keepdims=True))).astype(BF16)
                mixed.append(lax.dot_general(
                    weights, value, (((0,), (0,)), ((), ())), preferred_element_type=F32))
            mixed_ref[:, cut] = jnp.where(first, mixed[0], mixed[1]).astype(BF16)
        copies[5].wait()
        residual = x_ref[...].astype(F32) + jnp.dot(mixed_ref[...], o_buf[...], preferred_element_type=F32)
        final_ref[...] = root_scale(residual, fgain_ref[...]).astype(BF16)
        copy = pltpu.make_async_copy(final_ref, out_ref, sems.at[6])
        copy.start()
        copy.wait()


def encode(slot, counts, context, taken, weights, *rows):
    square, block = pltpu.VMEM((D_ENC, D_ENC), BF16), pltpu.VMEM((BLOCK, D_ENC), BF16)
    piece = rows[0].shape if slot else (HALF_HEADS, LINES, LANES)
    rows_out = (
        [jax.ShapeDtypeStruct((2,) + piece, BF16)] if slot else [jax.ShapeDtypeStruct(piece, BF16)] * 2)
    return pl.pallas_call(
        functools.partial(encoder_kernel, slot),
        out_shape=[jax.ShapeDtypeStruct((BLOCK, D_ENC), BF16)] + rows_out,
        in_specs=[SMEM] + [HBM] * 7 + [VMEM] * (2 + len(rows)),
        out_specs=[HBM] + [VMEM] * len(rows_out),
        scratch_shapes=[block] * 6 + [pltpu.VMEM((2, BLOCK, LANES), F32)] + [square] * 4
        + [pltpu.SemaphoreType.DMA((7,))],
        compiler_params=pltpu.CompilerParams(vmem_limit_bytes=63 * 2**20),
        cost_estimate=pl.CostEstimate(flops=6 * 10**9, bytes_accessed=9 * 2**20, transcendentals=2**20),
    )(counts, context, taken, *weights, *rows)


def three_parts(values):
    high = values.astype(BF16).astype(F32)
    middle = (values - high).astype(BF16).astype(F32)
    return high, middle, values - high - middle


def ring_chips(me):
    z, y = me // 4, lax.rem(me // 2, 2)
    place = jnp.where(z == 3, 2, jnp.where(z == 2, 3, z))
    chips = []
    for step in range(4):
        at = lax.rem(place + 4 - step, 4)
        z = jnp.where(at == 2, 3, jnp.where(at == 3, 2, at))
        chips.append((2 * z + y, 2 * z + 1 - y))
    return chips


def cross_kernel(counts_ref, *refs):
    tokens, loads, rows = refs[:6], refs[6:14], refs[14:18]
    out_ref, token_buf, weight_buf, query_buf, score_ref, value_ref, total_ref, top_ref, sum_ref = refs[18:27]
    sems, token_sems, row_sems = refs[27:]
    me = lax.axis_index("ctx")
    core = lax.rem(me, 2)
    own_live, other_live, _ = live_counts(counts_ref)
    chips = ring_chips(me)
    copies = []
    for step in range(4):
        for side in range(2):
            start = pl.multiple_of(chips[step][side] * LANES, LANES)
            copies.append(pltpu.make_async_copy(
                loads[2 * step + side], weight_buf.at[:, pl.ds(start, LANES)], sems.at[2 * step + side]))
    for step in range(4):
        for side in range(2):
            for at, part in ((0, core), (1, 1 - core)):
                start = pl.multiple_of((2 * chips[step][side] + part) * LINES, LINES)
                copies.append(pltpu.make_async_copy(
                    rows[step].at[side, at], query_buf.at[:, pl.ds(start, LINES), :],
                    row_sems.at[4 * step + 2 * side + at]))

    def token_copy(at):
        return pltpu.make_async_copy(tokens[at], token_buf.at[at], token_sems.at[at])

    def live(at):
        return (own_live > at) if at < CAP else (other_live > at - CAP)

    for copy in copies:
        copy.start()
    for at in range(2 * CAP):
        @pl.when(live(at))
        def _():
            token_copy(at).start()
    total_ref[...] = jnp.zeros_like(total_ref)
    sum_ref[...] = jnp.zeros_like(sum_ref)
    top_ref[...] = jnp.full_like(top_ref, -jnp.inf)
    for copy in copies:
        copy.wait()

    for at in range(2 * CAP):
        @pl.when(live(at))
        def _():
            token_copy(at).wait()
            both = jnp.dot(token_buf[at], weight_buf[...], preferred_element_type=F32).astype(BF16)
            value_ref[at] = both[:, HALF_HEADS * LANES :]
            for head in range(HALF_HEADS):
                scores = lax.dot_general(
                    both[:, head * LANES : (head + 1) * LANES], query_buf[head],
                    (((1,), (1,)), ((), ())), preferred_element_type=F32,
                ) * (1.0 / math.sqrt(HEAD_DIM))
                score_ref[at, head] = scores
                top_ref[head] = jnp.maximum(top_ref[head], jnp.max(scores, axis=0, keepdims=True))

    for at in range(2 * CAP):
        @pl.when(live(at))
        def _():
            for head in range(HALF_HEADS):
                weights = jnp.exp(score_ref[at, head] - top_ref[head])
                sum_ref[head] += jnp.sum(weights, axis=0, keepdims=True)
                total_ref[head] += lax.dot_general(
                    weights.astype(BF16), value_ref[at, :, head * LANES : (head + 1) * LANES],
                    (((0,), (0,)), ((), ())), preferred_element_type=F32)

    lines = total_ref.shape[1]
    notes = []
    for head in range(HALF_HEADS):
        notes += list(three_parts(top_ref[head])) + list(three_parts(sum_ref[head]))
        out_ref[:, :, head] = total_ref[head].astype(BF16).reshape(CHIPS, 2, LINES, LANES)
    notes = jnp.concatenate(notes + [jnp.zeros((LANES - len(notes), lines), F32)], axis=0).T
    out_ref[:, :, HALF_HEADS] = notes.astype(BF16).reshape(CHIPS, 2, LINES, LANES)


def cross(counts, tokens, loads, rows):
    lines = 2 * CHIPS * LINES
    line = pltpu.VMEM((HALF_HEADS, 1, lines), F32)
    return pl.pallas_call(
        cross_kernel,
        out_shape=jax.ShapeDtypeStruct((CHIPS, 2, HALF_HEADS + 1, LINES, LANES), BF16),
        in_specs=[SMEM] + [HBM] * 18,
        out_specs=VMEM,
        scratch_shapes=[
            pltpu.VMEM((2 * CAP, BLOCK, D_ENC), BF16),
            pltpu.VMEM((D_ENC, KV_HEADS * LANES), BF16),
            pltpu.VMEM((HALF_HEADS, lines, LANES), BF16),
            pltpu.VMEM((2 * CAP, HALF_HEADS, BLOCK, lines), F32),
            pltpu.VMEM((2 * CAP, BLOCK, HALF_HEADS * LANES), BF16),
            pltpu.VMEM((HALF_HEADS, lines, LANES), F32),
            line, line,
            pltpu.SemaphoreType.DMA((8,)), pltpu.SemaphoreType.DMA((2 * CAP,)), pltpu.SemaphoreType.DMA((16,)),
        ],
        compiler_params=pltpu.CompilerParams(vmem_limit_bytes=63 * 2**20),
        cost_estimate=pl.CostEstimate(flops=6 * 10**9, bytes_accessed=8 * 2**20, transcendentals=2**20),
    )(counts, *tokens, *loads, *rows)


def combine_kernel(*refs):
    own_ref, arrived, (keep_ref, give_ref) = refs[0], refs[1:CHIPS], refs[CHIPS:]
    me = lax.axis_index("ctx")
    core, chip = lax.rem(me, 2), me // 2
    for out_ref, part in ((keep_ref, core), (give_ref, 1 - core)):
        pieces = [own_ref.at[chip, part]] + [ref.at[part] for ref in arrived]
        notes = [piece[HALF_HEADS].astype(F32) for piece in pieces]
        for head in range(HALF_HEADS):
            at = 6 * head
            tops = [n[:, at : at + 1] + n[:, at + 1 : at + 2] + n[:, at + 2 : at + 3] for n in notes]
            sums = [n[:, at + 3 : at + 4] + n[:, at + 4 : at + 5] + n[:, at + 5 : at + 6] for n in notes]
            top = functools.reduce(jnp.maximum, tops)
            numerator, denominator = 0.0, 0.0
            for share, amount, piece in zip([jnp.exp(t - top) for t in tops], sums, pieces):
                numerator += share * piece[head].astype(F32)
                denominator += share * amount
            out_ref[head] = (numerator / denominator).astype(BF16)


def combine(own, arrived):
    shape = jax.ShapeDtypeStruct((HALF_HEADS, LINES, LANES), BF16)
    return pl.pallas_call(
        combine_kernel, out_shape=(shape, shape), in_specs=[VMEM] * CHIPS, out_specs=(VMEM, VMEM),
    )(own, *arrived)


def place_kernel(keep_ref, got_ref, out_ref):
    core = lax.rem(lax.axis_index("ctx"), 2)
    for head in range(KV_HEADS):
        mine = core == head % 2
        lines = jnp.where(mine, keep_ref[head // 2].astype(F32), got_ref[head // 2].astype(F32))
        for g in range(GROUP):
            start = (head * GROUP + g) * LANES
            out_ref[:, start : start + LANES] = lines[g * ROWS : (g + 1) * ROWS].astype(BF16)


def put_in_place(keep, got):
    return pl.pallas_call(
        place_kernel, out_shape=jax.ShapeDtypeStruct((ROWS, QW), BF16), in_specs=[VMEM] * 2, out_specs=VMEM,
    )(keep, got)


NEXT_Z = (1, 3, 0, 2)


def exchange(values, bits):
    return lax.ppermute(values, "ctx", [(i, i ^ bits) for i in range(2 * CHIPS)])


def round_z(values, steps=1):
    ring = []
    for i in range(2 * CHIPS):
        z = i // 4
        for _ in range(steps):
            z = NEXT_Z[z]
        ring.append((i, 4 * z + i % 4))
    return lax.ppermute(values, "ctx", ring)


def after(values, *others):
    return lax.optimization_barrier((values,) + others)[0]


def local(context, counts, queries, norm_gain, w_query, w_key, w_value, w_out, final_gain, w_kv):
    me = lax.axis_index("ctx")
    load0 = w_kv
    load1 = round_z(load0)
    beside0 = exchange(load0, 2)
    taken = exchange(context, 1)
    weights = (w_query, w_key, w_value, w_out, rotary_lanes(), norm_gain, final_gain)
    token0, keep, give = encode(0, counts, context, context, weights, queries)
    load1, token0, keep, give, taken = lax.optimization_barrier((load1, token0, keep, give, taken))
    load2 = round_z(load1)
    beside1 = exchange(load1, 2)
    got = exchange(give, 1)
    far0 = exchange(token0, 1)
    token1, row_chip = encode(1, after(counts, beside0), context, taken, weights, keep, got)
    load2, token1, row_chip = lax.optimization_barrier((load2, token1, row_chip))
    load3 = round_z(load2)
    row_beside = exchange(row_chip, 2)
    beside2 = exchange(load2, 2)
    far1 = exchange(token1, 1)
    token2, rows0 = encode(2, after(counts, beside1, far0), context, context, weights, row_chip, row_beside)
    load3, token2, rows0 = lax.optimization_barrier((load3, token2, rows0))
    beside3 = exchange(load3, 2)
    rows = [rows0] + [round_z(rows0, steps) for steps in (1, 2, 3)]
    far2 = exchange(token2, 1)

    parts = cross(
        counts, (token0, token1, token2, far0, far1, far2),
        (load0, beside0, load1, beside1, load2, beside2, load3, beside3), rows,
    )
    arrived = [
        exchange(lax.dynamic_index_in_dim(parts, (me // 2) ^ chip, keepdims=False), 2 * chip)
        for chip in range(1, CHIPS)
    ]
    keep, give = combine(parts, arrived)
    return put_in_place(keep, exchange(give, 1))


def rotary_tables(length, head_width):
    position = jnp.arange(length).astype(jnp.float32)[:, None]
    frequency = jnp.exp(
        jnp.arange(head_width // 2).astype(jnp.float32) * (-2.0 * math.log(10000.0) / head_width)
    )
    phase_angle = position * frequency[None, :]
    return (jnp.cos(phase_angle)[:, None, :], jnp.sin(phase_angle)[:, None, :])


def rotate(values, cosine_table, sine_table):
    half_width = values.shape[-1] // 2
    lower_half = values[..., :half_width]
    upper_half = values[..., half_width:]
    return jnp.concatenate(
        [
            lower_half * cosine_table - upper_half * sine_table,
            upper_half * cosine_table + lower_half * sine_table,
        ],
        axis=-1,
    )


def weighted_sums(cross_scores, top_scores, key_alive, cross_values):
    cross_weights = jnp.where(key_alive, jnp.exp(cross_scores - top_scores[..., None]), 0.0)
    total_rows = cross_scores.shape[0]
    denominator = jnp.sum(cross_weights, axis=-1).reshape(total_rows, Q_HEADS)
    numerator = jnp.einsum(
        "rkgt,tkd->rkgd",
        cross_weights.astype(jnp.bfloat16),
        cross_values,
        preferred_element_type=jnp.float32,
    )
    return (numerator.reshape(total_rows, QW), denominator)


def local_any(context, counts, queries, norm_gain, w_query, w_key, w_value, w_out, final_gain, w_kv):
    places = lax.axis_size("ctx")
    device_index = lax.axis_index("ctx")
    device_number = jnp.arange(places)
    own_count = jnp.sum(jnp.where(device_number == device_index, counts, 0))
    alive_slot = jnp.arange(CAP) < own_count
    slot_count = context.shape[0]
    row_count = slot_count * BLOCK
    normed = root_scale(context, norm_gain).astype(jnp.bfloat16).reshape(row_count, D_ENC)
    cosine_table, sine_table = rotary_tables(BLOCK, ENC_HD)

    def project(weight):
        return jnp.dot(normed, weight, preferred_element_type=jnp.float32).reshape(
            slot_count, BLOCK, ENC_HEADS, ENC_HD
        )

    query_rows = rotate(project(w_query), cosine_table, sine_table).astype(jnp.bfloat16)
    key_rows = rotate(project(w_key), cosine_table, sine_table).astype(jnp.bfloat16)
    value_rows = project(w_value).astype(jnp.bfloat16)
    scores = jnp.einsum(
        "sqhd,skhd->shqk", query_rows, key_rows, preferred_element_type=jnp.float32
    ) / math.sqrt(ENC_HD)
    weights = jax.nn.softmax(scores, axis=-1).astype(jnp.bfloat16)
    mixed_rows = jnp.einsum(
        "shqk,skhd->sqhd", weights, value_rows, preferred_element_type=jnp.float32
    )
    mixed_rows = mixed_rows.astype(jnp.bfloat16).reshape(row_count, D_ENC)
    residual = context.reshape(row_count, D_ENC).astype(jnp.float32) + jnp.dot(
        mixed_rows, w_out, preferred_element_type=jnp.float32
    )
    final_norm = root_scale(residual, final_gain).astype(jnp.bfloat16)
    key_value = jnp.dot(
        final_norm,
        lax.all_gather(w_kv, "ctx", axis=1, tiled=True),
        preferred_element_type=jnp.float32,
    ).astype(jnp.bfloat16)
    cross_keys = key_value[:, : KV_HEADS * HEAD_DIM].reshape(row_count, KV_HEADS, HEAD_DIM)
    cross_values = key_value[:, KV_HEADS * HEAD_DIM :].reshape(row_count, KV_HEADS, HEAD_DIM)
    every_query = lax.all_gather(queries, "ctx", axis=0, tiled=True)
    total_rows = every_query.shape[0]
    grouped = every_query.reshape(total_rows, KV_HEADS, GROUP, HEAD_DIM)
    cross_scores = jnp.einsum(
        "rkgd,tkd->rkgt", grouped, cross_keys, preferred_element_type=jnp.float32
    ) / math.sqrt(HEAD_DIM)
    key_alive = jnp.repeat(alive_slot, BLOCK)
    local_top = jnp.max(jnp.where(key_alive, cross_scores, -jnp.inf), axis=-1)
    row_top = lax.pmax(local_top.astype(jnp.bfloat16), "ctx").astype(local_top.dtype)
    numerator, denominator = weighted_sums(cross_scores, row_top, key_alive, cross_values)
    own_numerator, own_denominator = (
        lax.psum_scatter(numerator, "ctx", scatter_dimension=0, tiled=True),
        lax.psum_scatter(denominator, "ctx", scatter_dimension=0, tiled=True),
    )
    own_rows = own_numerator.shape[0]
    result = own_numerator.reshape(own_rows, Q_HEADS, HEAD_DIM) / own_denominator[..., None]
    return result.reshape(own_rows, QW).astype(jnp.bfloat16)


def solution(mesh):
    in_specs = (
        P(("groups", "ctx"), None, None),
        P("groups"),
        P(("groups", "ctx"), None),
        P(),
        P(),
        P(),
        P(),
        P(),
        P(),
        P(None, "ctx"),
    )
    out_specs = P(("groups", "ctx"), None)
    small = mesh.shape["ctx"] == 2 * CHIPS
    return jax.shard_map(local if small else local_any, mesh=mesh, in_specs=in_specs, out_specs=out_specs, check_vma=False)
```

```python
import functools
import math

import jax
import jax.numpy as jnp
import numpy as np
from jax import lax
from jax.experimental import pallas as pl
from jax.experimental.pallas import tpu as pltpu
from jax.sharding import PartitionSpec as P

D_ENC = 1024
ENC_HEADS = 16
ENC_HD = 64
BLOCK = 256
KV_HEADS = 8
HEAD_DIM = 128
Q_HEADS = 32
GROUP = 4
QW = 4096
CAP = 3
HALF_HEADS = KV_HEADS // 2
LANES = 128
CHIPS = 8
ROWS = 4
LINES = ROWS * GROUP
F32 = jnp.float32
BF16 = jnp.bfloat16
VMEM = pl.BlockSpec(memory_space=pltpu.VMEM)
SMEM = pl.BlockSpec(memory_space=pltpu.SMEM)
HBM = pl.BlockSpec(memory_space=pltpu.HBM)
PARTS = 4
PART = D_ENC // PARTS


def root_scale(values, gain):
    values = values.astype(F32)
    return (
        values
        * lax.rsqrt(jnp.mean(values * values, axis=-1, keepdims=True) + 1e-05)
        * gain.astype(F32)
    )


def rotary_lanes():
    position = np.arange(BLOCK, dtype=np.float64)[:, None]
    frequency = 10000.0 ** (-2.0 * np.arange(ENC_HD // 2) / ENC_HD)
    angle = position * frequency[None, :]
    cosine, sine = np.cos(angle), np.sin(angle)
    return jnp.asarray(np.stack([
        np.concatenate([cosine, cosine, cosine, cosine], axis=1),
        np.concatenate([-sine, sine, -sine, sine], axis=1),
    ]), F32)


def live_counts(counts_ref):
    me = lax.axis_index("ctx")
    own, other = counts_ref[me], counts_ref[me + 1 - 2 * lax.rem(me, 2)]
    gives = jnp.where((own == 3) & (other == 1), 1, 0)
    takes = jnp.where((own == 1) & (other == 3), 1, 0)
    return own - gives + takes, other + gives - takes, takes


def split_rows(query_ref, keep_ref, give_ref):
    core = lax.rem(lax.axis_index("ctx"), 2)
    width = GROUP * HEAD_DIM
    for out_ref, parity in ((keep_ref, core), (give_ref, 1 - core)):
        for head in range(HALF_HEADS):
            start = pl.multiple_of((2 * head + parity) * width, width)
            rows = query_ref[:, pl.ds(start, width)].astype(F32)
            out_ref[head] = jnp.concatenate(
                [rows[:, g * LANES : (g + 1) * LANES] for g in range(GROUP)], axis=0
            ).astype(BF16)


def start_block(slot, context_ref, taken_ref, takes, x_ref, sem):
    if slot == 1:
        @pl.when(takes != 0)
        def _():
            pltpu.make_async_copy(taken_ref.at[CAP - 1], x_ref, sem).start()

        @pl.when(takes == 0)
        def _():
            pltpu.make_async_copy(context_ref.at[slot], x_ref, sem).start()
    else:
        pltpu.make_async_copy(context_ref.at[slot], x_ref, sem).start()


def project_block(x_ref, copies, table_buf, gain_ref, q_buf, k_buf, v_buf, q_ref, k_ref, v_ref):
    normed = root_scale(x_ref[...], gain_ref[...]).astype(BF16)
    copies[0].wait()
    copies[1].wait()
    cosine, sine = table_buf[0], table_buf[1]
    lane = lax.broadcasted_iota(jnp.int32, (BLOCK, LANES), 1)
    lower = (lane % ENC_HD) < ENC_HD // 2

    def project(buf, to_ref, cosine, sine):
        for part in range(PARTS):
            values = jnp.dot(normed, buf[:, part * PART : (part + 1) * PART], preferred_element_type=F32)
            for at in range(PART // LANES):
                cut = values[:, at * LANES : (at + 1) * LANES]
                swapped = jnp.where(
                    lower, pltpu.roll(cut, LANES - ENC_HD // 2, 1), pltpu.roll(cut, ENC_HD // 2, 1))
                start = part * PART + at * LANES
                to_ref[:, start : start + LANES] = (cut * cosine + swapped * sine).astype(BF16)

    project(q_buf, q_ref, cosine * 0.125, sine * 0.125)
    copies[2].wait()
    project(k_buf, k_ref, cosine, sine)
    copies[3].wait()
    v_ref[...] = jnp.dot(normed, v_buf[...], preferred_element_type=F32).astype(BF16)


def attend_block(x_ref, copy, q_ref, k_ref, v_ref, o_buf, fgain_ref, mixed_ref, final_ref):
    first = lax.broadcasted_iota(jnp.int32, (BLOCK, LANES), 1) < ENC_HD
    for pair in range(ENC_HEADS // 2):
        cut = slice(pair * LANES, (pair + 1) * LANES)
        query, key, value = q_ref[:, cut], k_ref[:, cut], v_ref[:, cut]
        mixed = []
        for own in (first, jnp.logical_not(first)):
            scores = lax.dot_general(
                key, jnp.where(own, query, jnp.zeros_like(query)),
                (((1,), (1,)), ((), ())), preferred_element_type=F32)
            weights = jnp.exp(scores - jnp.max(scores, axis=0, keepdims=True))
            weights = (weights * (1.0 / jnp.sum(weights, axis=0, keepdims=True))).astype(BF16)
            mixed.append(lax.dot_general(
                weights, value, (((0,), (0,)), ((), ())), preferred_element_type=F32))
        mixed_ref[:, cut] = jnp.where(first, mixed[0], mixed[1]).astype(BF16)
    copy.wait()
    residual = x_ref[...].astype(F32) + jnp.dot(mixed_ref[...], o_buf[...], preferred_element_type=F32)
    final_ref[...] = root_scale(residual, fgain_ref[...]).astype(BF16)


def first_half_kernel(context_ref, wq_ref, wk_ref, wv_ref, table_ref, gain_ref, query_ref,
                      out_ref, keep_ref, give_ref, x_ref, table_buf, q_buf, k_buf, v_buf, q_ref, k_ref, v_ref, sems):
    copies = [
        pltpu.make_async_copy(hbm, buf, sems.at[at])
        for at, (hbm, buf) in enumerate(
            ((context_ref.at[0], x_ref), (wq_ref, q_buf), (table_ref, table_buf), (wk_ref, k_buf), (wv_ref, v_buf)))
    ]
    for copy in copies:
        copy.start()
    split_rows(query_ref, keep_ref, give_ref)
    copies[0].wait()
    project_block(x_ref, copies[1:], table_buf, gain_ref, q_buf, k_buf, v_buf, q_ref, k_ref, v_ref)
    writes = [
        pltpu.make_async_copy(buf, out_ref.at[at], sems.at[5 + at]) for at, buf in enumerate((q_ref, k_ref, v_ref))]
    for copy in writes:
        copy.start()
    for copy in writes:
        copy.wait()


def second_half_kernel(context_ref, half_ref, wo_ref, fgain_ref, keep_ref, got_ref, out_ref, rows_ref,
                       x_ref, o_buf, q_ref, k_ref, v_ref, mixed_ref, final_ref, sems):
    copies = [
        pltpu.make_async_copy(hbm, buf, sems.at[at])
        for at, (hbm, buf) in enumerate(
            ((half_ref.at[0], q_ref), (half_ref.at[1], k_ref), (half_ref.at[2], v_ref), (context_ref.at[0], x_ref),
             (wo_ref, o_buf)))
    ]
    for copy in copies:
        copy.start()
    rows_ref[0] = keep_ref[...]
    rows_ref[1] = got_ref[...]
    for copy in copies[:4]:
        copy.wait()
    attend_block(x_ref, copies[4], q_ref, k_ref, v_ref, o_buf, fgain_ref, mixed_ref, final_ref)
    copy = pltpu.make_async_copy(final_ref, out_ref, sems.at[5])
    copy.start()
    copy.wait()


def encoder_kernel(slot, counts_ref, context_ref, taken_ref, wq_ref, wk_ref, wv_ref, wo_ref, table_ref, gain_ref,
                   fgain_ref, *refs):
    if slot == 1:
        (rows_in0, rows_in1, out_ref, rows_out), refs = refs[:4], refs[4:]
    else:
        (out_ref,), refs = refs[:1], refs[1:]
    mixed_ref, x_ref, q_ref, k_ref, v_ref, final_ref, table_buf, q_buf, k_buf, v_buf, o_buf, sems = refs
    live, _, takes = live_counts(counts_ref)
    copies = [
        pltpu.make_async_copy(hbm, buf, sems.at[1 + at])
        for at, (hbm, buf) in enumerate(
            ((wq_ref, q_buf), (table_ref, table_buf), (wk_ref, k_buf), (wv_ref, v_buf), (wo_ref, o_buf)))
    ]

    @pl.when(live > slot)
    def _():
        start_block(slot, context_ref, taken_ref, takes, x_ref, sems.at[0])
        for copy in copies:
            copy.start()

    if slot == 1:
        rows_out[0] = rows_in0[...]
        rows_out[1] = rows_in1[...]

    @pl.when(live > slot)
    def _():
        pltpu.make_async_copy(context_ref.at[slot], x_ref, sems.at[0]).wait()
        project_block(x_ref, copies, table_buf, gain_ref, q_buf, k_buf, v_buf, q_ref, k_ref, v_ref)
        attend_block(x_ref, copies[4], q_ref, k_ref, v_ref, o_buf, fgain_ref, mixed_ref, final_ref)
        copy = pltpu.make_async_copy(final_ref, out_ref, sems.at[6])
        copy.start()
        copy.wait()


SQUARE, WHOLE = pltpu.VMEM((D_ENC, D_ENC), BF16), pltpu.VMEM((BLOCK, D_ENC), BF16)
TABLES = pltpu.VMEM((2, BLOCK, LANES), F32)
TOKENS = jax.ShapeDtypeStruct((BLOCK, D_ENC), BF16)
PIECE = (HALF_HEADS, LINES, LANES)


def vmem(mebibytes):
    return pltpu.CompilerParams(vmem_limit_bytes=mebibytes * 2**20)


def cost(flops):
    return pl.CostEstimate(flops=flops, bytes_accessed=9 * 2**20, transcendentals=2**20)


def first_half(context, weights, queries):
    w_query, w_key, w_value, _, tables, gain, _ = weights
    return pl.pallas_call(
        first_half_kernel,
        out_shape=[jax.ShapeDtypeStruct((3, BLOCK, D_ENC), BF16)] + [jax.ShapeDtypeStruct(PIECE, BF16)] * 2,
        in_specs=[HBM] * 5 + [VMEM] * 2,
        out_specs=[HBM, VMEM, VMEM],
        scratch_shapes=[WHOLE, TABLES] + [SQUARE] * 3 + [WHOLE] * 3 + [pltpu.SemaphoreType.DMA((8,))],
        compiler_params=vmem(63), cost_estimate=cost(5 * 10**9),
    )(context, w_query, w_key, w_value, tables, gain, queries)


def second_half(context, half, weights, keep, got):
    return pl.pallas_call(
        second_half_kernel,
        out_shape=[TOKENS, jax.ShapeDtypeStruct((2,) + PIECE, BF16)],
        in_specs=[HBM] * 3 + [VMEM] * 3,
        out_specs=[HBM, VMEM],
        scratch_shapes=[WHOLE, SQUARE] + [WHOLE] * 5 + [pltpu.SemaphoreType.DMA((6,))],
        compiler_params=vmem(63), cost_estimate=cost(5 * 10**9),
    )(context, half, weights[3], weights[6], keep, got)


def encode(slot, counts, context, taken, weights, *rows):
    rows_out = [jax.ShapeDtypeStruct((2,) + rows[0].shape, BF16)] if rows else []
    return pl.pallas_call(
        functools.partial(encoder_kernel, slot),
        out_shape=[TOKENS] + rows_out,
        in_specs=[SMEM] + [HBM] * 7 + [VMEM] * (2 + len(rows)),
        out_specs=[HBM] + [VMEM] * len(rows_out),
        scratch_shapes=[WHOLE] * 6 + [TABLES] + [SQUARE] * 4 + [pltpu.SemaphoreType.DMA((7,))],
        compiler_params=vmem(63), cost_estimate=cost(8 * 10**9),
    )(counts, context, taken, *weights, *rows)


def three_parts(values):
    high = values.astype(BF16).astype(F32)
    middle = (values - high).astype(BF16).astype(F32)
    return high, middle, values - high - middle


def ring_chips(me):
    z, y = me // 4, lax.rem(me // 2, 2)
    place = jnp.where(z == 3, 2, jnp.where(z == 2, 3, z))
    chips = []
    for step in range(4):
        at = lax.rem(place + 4 - step, 4)
        z = jnp.where(at == 2, 3, jnp.where(at == 3, 2, at))
        chips.append((2 * z + y, 2 * z + 1 - y))
    return chips


def cross_kernel(counts_ref, *refs):
    tokens, loads, rows = refs[:6], refs[6:14], refs[14:18]
    out_ref, token_buf, weight_buf, query_buf, score_ref, value_ref, total_ref, top_ref, sum_ref = refs[18:27]
    sems, token_sems, row_sems = refs[27:]
    me = lax.axis_index("ctx")
    core = lax.rem(me, 2)
    own_live, other_live, _ = live_counts(counts_ref)
    chips = ring_chips(me)
    copies = []
    for step in range(4):
        for side in range(2):
            start = pl.multiple_of(chips[step][side] * LANES, LANES)
            copies.append(pltpu.make_async_copy(
                loads[2 * step + side], weight_buf.at[:, pl.ds(start, LANES)], sems.at[2 * step + side]))
    for step in range(4):
        for side in range(2):
            for at, part in ((0, core), (1, 1 - core)):
                start = pl.multiple_of((2 * chips[step][side] + part) * LINES, LINES)
                copies.append(pltpu.make_async_copy(
                    rows[step].at[side, at], query_buf.at[:, pl.ds(start, LINES), :],
                    row_sems.at[4 * step + 2 * side + at]))

    def token_copy(at):
        return pltpu.make_async_copy(tokens[at], token_buf.at[at], token_sems.at[at])

    def live(at):
        return (own_live > at) if at < CAP else (other_live > at - CAP)

    for copy in copies:
        copy.start()
    for at in range(2 * CAP):
        @pl.when(live(at))
        def _():
            token_copy(at).start()
    total_ref[...] = jnp.zeros_like(total_ref)
    sum_ref[...] = jnp.zeros_like(sum_ref)
    top_ref[...] = jnp.full_like(top_ref, -jnp.inf)
    for copy in copies:
        copy.wait()

    for at in range(2 * CAP):
        @pl.when(live(at))
        def _():
            token_copy(at).wait()
            both = jnp.dot(token_buf[at], weight_buf[...], preferred_element_type=F32).astype(BF16)
            value_ref[at] = both[:, HALF_HEADS * LANES :]
            for head in range(HALF_HEADS):
                scores = lax.dot_general(
                    both[:, head * LANES : (head + 1) * LANES], query_buf[head],
                    (((1,), (1,)), ((), ())), preferred_element_type=F32,
                ) * (1.0 / math.sqrt(HEAD_DIM))
                score_ref[at, head] = scores
                top_ref[head] = jnp.maximum(top_ref[head], jnp.max(scores, axis=0, keepdims=True))

    for at in range(2 * CAP):
        @pl.when(live(at))
        def _():
            for head in range(HALF_HEADS):
                weights = jnp.exp(score_ref[at, head] - top_ref[head])
                sum_ref[head] += jnp.sum(weights, axis=0, keepdims=True)
                total_ref[head] += lax.dot_general(
                    weights.astype(BF16), value_ref[at, :, head * LANES : (head + 1) * LANES],
                    (((0,), (0,)), ((), ())), preferred_element_type=F32)

    lines = total_ref.shape[1]
    notes = []
    for head in range(HALF_HEADS):
        notes += list(three_parts(top_ref[head])) + list(three_parts(sum_ref[head]))
        out_ref[:, head] = total_ref[head].astype(BF16).reshape(2 * CHIPS, LINES, LANES)
    notes = jnp.concatenate(notes + [jnp.zeros((LANES - len(notes), lines), F32)], axis=0).T
    out_ref[:, HALF_HEADS] = notes.astype(BF16).reshape(2 * CHIPS, LINES, LANES)


def cross(counts, tokens, loads, rows):
    lines = 2 * CHIPS * LINES
    line = pltpu.VMEM((HALF_HEADS, 1, lines), F32)
    return pl.pallas_call(
        cross_kernel,
        out_shape=jax.ShapeDtypeStruct((2 * CHIPS, HALF_HEADS + 1, LINES, LANES), BF16),
        in_specs=[SMEM] + [HBM] * 18,
        out_specs=VMEM,
        scratch_shapes=[
            pltpu.VMEM((2 * CAP, BLOCK, D_ENC), BF16),
            pltpu.VMEM((D_ENC, KV_HEADS * LANES), BF16),
            pltpu.VMEM((HALF_HEADS, lines, LANES), BF16),
            pltpu.VMEM((2 * CAP, HALF_HEADS, BLOCK, lines), F32),
            pltpu.VMEM((2 * CAP, BLOCK, HALF_HEADS * LANES), BF16),
            pltpu.VMEM((HALF_HEADS, lines, LANES), F32),
            line, line,
            pltpu.SemaphoreType.DMA((8,)), pltpu.SemaphoreType.DMA((2 * CAP,)), pltpu.SemaphoreType.DMA((16,)),
        ],
        compiler_params=vmem(63),
        cost_estimate=pl.CostEstimate(flops=6 * 10**9, bytes_accessed=8 * 2**20, transcendentals=2**20),
    )(counts, *tokens, *loads, *rows)


def combine_kernel(parts_ref, out_ref):
    for core in range(2):
        pieces = [parts_ref.at[2 * chip + core] for chip in range(CHIPS)]
        notes = [piece[HALF_HEADS].astype(F32) for piece in pieces]
        for at in range(HALF_HEADS):
            lane = 6 * at
            tops = [n[:, lane : lane + 1] + n[:, lane + 1 : lane + 2] + n[:, lane + 2 : lane + 3] for n in notes]
            sums = [n[:, lane + 3 : lane + 4] + n[:, lane + 4 : lane + 5] + n[:, lane + 5 : lane + 6] for n in notes]
            top = functools.reduce(jnp.maximum, tops)
            numerator, denominator = 0.0, 0.0
            for share, amount, piece in zip([jnp.exp(t - top) for t in tops], sums, pieces):
                numerator += share * piece[at].astype(F32)
                denominator += share * amount
            lines = numerator / denominator
            for g in range(GROUP):
                start = ((2 * at + core) * GROUP + g) * LANES
                out_ref[:, start : start + LANES] = lines[g * ROWS : (g + 1) * ROWS].astype(BF16)


def combine(parts):
    return pl.pallas_call(
        combine_kernel, out_shape=jax.ShapeDtypeStruct((ROWS, QW), BF16), in_specs=[VMEM], out_specs=VMEM,
        compiler_params=vmem(8),
    )(parts)


NEXT_Z = (1, 3, 0, 2)


def exchange(values, bits):
    return lax.ppermute(values, "ctx", [(i, i ^ bits) for i in range(2 * CHIPS)])


def round_z(values, steps=1):
    ring = []
    for i in range(2 * CHIPS):
        z = i // 4
        for _ in range(steps):
            z = NEXT_Z[z]
        ring.append((i, 4 * z + i % 4))
    return lax.ppermute(values, "ctx", ring)


def after(values, *others):
    return lax.optimization_barrier((values,) + others)[0]


def local(context, counts, queries, norm_gain, w_query, w_key, w_value, w_out, final_gain, w_kv):
    load0 = w_kv
    load1 = round_z(load0)
    beside0 = exchange(load0, 2)
    taken = exchange(context, 1)
    weights = (w_query, w_key, w_value, w_out, rotary_lanes(), norm_gain, final_gain)
    half, keep, give = first_half(context, weights, queries)
    load1, half, give, taken, beside0 = lax.optimization_barrier((load1, half, give, taken, beside0))
    load2 = round_z(load1)
    beside1 = exchange(load1, 2)
    got = exchange(give, 1)
    token0, row_chip = second_half(context, half, weights, keep, got)
    load2, token0, row_chip, beside1 = lax.optimization_barrier((load2, token0, row_chip, beside1))
    load3 = round_z(load2)
    beside2 = exchange(load2, 2)
    row_beside = exchange(row_chip, 2)
    far0 = exchange(token0, 1)
    token1, rows0 = encode(1, counts, context, taken, weights, row_chip, row_beside)
    load3, token1, rows0, beside2, far0 = lax.optimization_barrier((load3, token1, rows0, beside2, far0))
    beside3 = exchange(load3, 2)
    far1 = exchange(token1, 1)
    rows = [rows0] + [round_z(rows0, steps) for steps in (1, 2, 3)]
    (token2,) = encode(2, after(counts, beside2), context, context, weights)
    far2 = exchange(token2, 1)

    parts = cross(
        counts, (token0, token1, token2, far0, far1, far2),
        (load0, beside0, load1, beside1, load2, beside2, load3, beside3), rows,
    )
    return combine(lax.all_to_all(parts, "ctx", 0, 0, tiled=True))


def rotary_tables(length, head_width):
    position = jnp.arange(length).astype(jnp.float32)[:, None]
    frequency = jnp.exp(
        jnp.arange(head_width // 2).astype(jnp.float32) * (-2.0 * math.log(10000.0) / head_width)
    )
    phase_angle = position * frequency[None, :]
    return (jnp.cos(phase_angle)[:, None, :], jnp.sin(phase_angle)[:, None, :])


def rotate(values, cosine_table, sine_table):
    half_width = values.shape[-1] // 2
    lower_half = values[..., :half_width]
    upper_half = values[..., half_width:]
    return jnp.concatenate(
        [
            lower_half * cosine_table - upper_half * sine_table,
            upper_half * cosine_table + lower_half * sine_table,
        ],
        axis=-1,
    )


def weighted_sums(cross_scores, top_scores, key_alive, cross_values):
    cross_weights = jnp.where(key_alive, jnp.exp(cross_scores - top_scores[..., None]), 0.0)
    total_rows = cross_scores.shape[0]
    denominator = jnp.sum(cross_weights, axis=-1).reshape(total_rows, Q_HEADS)
    numerator = jnp.einsum(
        "rkgt,tkd->rkgd",
        cross_weights.astype(jnp.bfloat16),
        cross_values,
        preferred_element_type=jnp.float32,
    )
    return (numerator.reshape(total_rows, QW), denominator)


def local_any(context, counts, queries, norm_gain, w_query, w_key, w_value, w_out, final_gain, w_kv):
    places = lax.axis_size("ctx")
    device_index = lax.axis_index("ctx")
    device_number = jnp.arange(places)
    own_count = jnp.sum(jnp.where(device_number == device_index, counts, 0))
    alive_slot = jnp.arange(CAP) < own_count
    slot_count = context.shape[0]
    row_count = slot_count * BLOCK
    normed = root_scale(context, norm_gain).astype(jnp.bfloat16).reshape(row_count, D_ENC)
    cosine_table, sine_table = rotary_tables(BLOCK, ENC_HD)

    def project(weight):
        return jnp.dot(normed, weight, preferred_element_type=jnp.float32).reshape(
            slot_count, BLOCK, ENC_HEADS, ENC_HD
        )

    query_rows = rotate(project(w_query), cosine_table, sine_table).astype(jnp.bfloat16)
    key_rows = rotate(project(w_key), cosine_table, sine_table).astype(jnp.bfloat16)
    value_rows = project(w_value).astype(jnp.bfloat16)
    scores = jnp.einsum(
        "sqhd,skhd->shqk", query_rows, key_rows, preferred_element_type=jnp.float32
    ) / math.sqrt(ENC_HD)
    weights = jax.nn.softmax(scores, axis=-1).astype(jnp.bfloat16)
    mixed_rows = jnp.einsum(
        "shqk,skhd->sqhd", weights, value_rows, preferred_element_type=jnp.float32
    )
    mixed_rows = mixed_rows.astype(jnp.bfloat16).reshape(row_count, D_ENC)
    residual = context.reshape(row_count, D_ENC).astype(jnp.float32) + jnp.dot(
        mixed_rows, w_out, preferred_element_type=jnp.float32
    )
    final_norm = root_scale(residual, final_gain).astype(jnp.bfloat16)
    key_value = jnp.dot(
        final_norm,
        lax.all_gather(w_kv, "ctx", axis=1, tiled=True),
        preferred_element_type=jnp.float32,
    ).astype(jnp.bfloat16)
    cross_keys = key_value[:, : KV_HEADS * HEAD_DIM].reshape(row_count, KV_HEADS, HEAD_DIM)
    cross_values = key_value[:, KV_HEADS * HEAD_DIM :].reshape(row_count, KV_HEADS, HEAD_DIM)
    every_query = lax.all_gather(queries, "ctx", axis=0, tiled=True)
    total_rows = every_query.shape[0]
    grouped = every_query.reshape(total_rows, KV_HEADS, GROUP, HEAD_DIM)
    cross_scores = jnp.einsum(
        "rkgd,tkd->rkgt", grouped, cross_keys, preferred_element_type=jnp.float32
    ) / math.sqrt(HEAD_DIM)
    key_alive = jnp.repeat(alive_slot, BLOCK)
    local_top = jnp.max(jnp.where(key_alive, cross_scores, -jnp.inf), axis=-1)
    row_top = lax.pmax(local_top.astype(jnp.bfloat16), "ctx").astype(local_top.dtype)
    numerator, denominator = weighted_sums(cross_scores, row_top, key_alive, cross_values)
    own_numerator, own_denominator = (
        lax.psum_scatter(numerator, "ctx", scatter_dimension=0, tiled=True),
        lax.psum_scatter(denominator, "ctx", scatter_dimension=0, tiled=True),
    )
    own_rows = own_numerator.shape[0]
    result = own_numerator.reshape(own_rows, Q_HEADS, HEAD_DIM) / own_denominator[..., None]
    return result.reshape(own_rows, QW).astype(jnp.bfloat16)


def solution(mesh):
    in_specs = (
        P(("groups", "ctx"), None, None),
        P("groups"),
        P(("groups", "ctx"), None),
        P(),
        P(),
        P(),
        P(),
        P(),
        P(),
        P(None, "ctx"),
    )
    out_specs = P(("groups", "ctx"), None)
    small = mesh.shape["ctx"] == 2 * CHIPS
    return jax.shard_map(local if small else local_any, mesh=mesh, in_specs=in_specs, out_specs=out_specs, check_vma=False)
```

```python
import functools
import math

import jax
import jax.numpy as jnp
import numpy as np
from jax import lax
from jax.experimental import pallas as pl
from jax.experimental.pallas import tpu as pltpu
from jax.sharding import PartitionSpec as P

D_ENC = 1024
ENC_HEADS = 16
ENC_HD = 64
BLOCK = 256
KV_HEADS = 8
HEAD_DIM = 128
Q_HEADS = 32
GROUP = 4
QW = 4096
CAP = 3
HALF_HEADS = KV_HEADS // 2
LANES = 128
CHIPS = 8
ROWS = 4
LINES = ROWS * GROUP
F32 = jnp.float32
BF16 = jnp.bfloat16
VMEM = pl.BlockSpec(memory_space=pltpu.VMEM)
SMEM = pl.BlockSpec(memory_space=pltpu.SMEM)
HBM = pl.BlockSpec(memory_space=pltpu.HBM)
ANY = pl.BlockSpec(memory_space=pl.ANY)
PARTS = 4
PART = D_ENC // PARTS
HALF = D_ENC // 2
QUERY_LINES = KV_HEADS * LINES
STEPS = 4
SPLIT = (STEPS - 1) * HALF


def root_scale(values, gain):
    values = values.astype(F32)
    return (
        values
        * lax.rsqrt(jnp.mean(values * values, axis=-1, keepdims=True) + 1e-05)
        * gain.astype(F32)
    )


def rotary_lanes():
    position = np.arange(BLOCK, dtype=np.float64)[:, None]
    frequency = 10000.0 ** (-2.0 * np.arange(ENC_HD // 2) / ENC_HD)
    angle = position * frequency[None, :]
    cosine, sine = np.cos(angle), np.sin(angle)
    return jnp.asarray(np.stack([
        np.concatenate([cosine, cosine, cosine, cosine], axis=1),
        np.concatenate([-sine, sine, -sine, sine], axis=1),
    ]), F32)


def live_counts(counts_ref):
    me = lax.axis_index("ctx")
    own, other = counts_ref[me], counts_ref[me + 1 - 2 * lax.rem(me, 2)]
    gives = jnp.where((own == 3) & (other == 1), 1, 0)
    takes = jnp.where((own == 1) & (other == 3), 1, 0)
    return own - gives + takes, other + gives - takes, takes


def prepare_kernel(w_kv_ref, query_ref, out_ref, sem):
    start = pl.multiple_of(lax.axis_index("groups") * HALF, HALF)
    copy = pltpu.make_async_copy(w_kv_ref.at[pl.ds(start, HALF), :], out_ref.at[pl.ds(0, HALF), :], sem)
    copy.start()
    rows = query_ref[...].astype(F32)
    for head in range(KV_HEADS):
        first = head * GROUP
        out_ref[HALF + head * LINES : HALF + (head + 1) * LINES, :] = jnp.concatenate(
            [rows[:, (first + g) * LANES : (first + g + 1) * LANES] for g in range(GROUP)], axis=0
        ).astype(BF16)
    copy.wait()


def prepare(w_kv, queries):
    return pl.pallas_call(
        prepare_kernel,
        out_shape=jax.ShapeDtypeStruct((HALF + QUERY_LINES, LANES), BF16),
        in_specs=[HBM, VMEM], out_specs=VMEM, scratch_shapes=[pltpu.SemaphoreType.DMA],
        compiler_params=vmem(8),
    )(w_kv, queries)


def copy_all(pairs, sems):
    copies = [pltpu.make_async_copy(source, target, sems.at[at]) for at, (source, target) in enumerate(pairs)]
    for copy in copies:
        copy.start()
    for copy in copies:
        copy.wait()


def collect_kernel(own_ref, z0_ref, z1_ref, z2_ref, x_ref, y_ref, sems):
    pairs = []
    for at, ref in enumerate((z0_ref, z1_ref, z2_ref)):
        columns = ref.at[pl.ds(0, HALF), :]
        pairs.append((columns, x_ref.at[pl.ds(at * HALF, HALF), :]))
        pairs.append((columns, y_ref.at[pl.ds(at * HALF, HALF), :]))
    for at, ref in enumerate((z0_ref, z1_ref, z2_ref, own_ref)):
        pairs.append((
            ref.at[pl.ds(HALF, QUERY_LINES), :], y_ref.at[pl.ds(SPLIT + at * QUERY_LINES, QUERY_LINES), :]))
    copy_all(pairs, sems)


def collect(own, z_loads):
    return pl.pallas_call(
        collect_kernel,
        out_shape=[
            jax.ShapeDtypeStruct((SPLIT, LANES), BF16),
            jax.ShapeDtypeStruct((SPLIT + STEPS * QUERY_LINES, LANES), BF16),
        ],
        in_specs=[ANY] * 4, out_specs=[ANY] * 2, scratch_shapes=[pltpu.SemaphoreType.DMA((10,))],
        compiler_params=vmem(8),
    )(own, *z_loads)


def gather_rows_kernel(own_ref, z0_ref, z1_ref, z2_ref, y_ref, last_ref, near_ref, sems):
    pairs = [(y_ref.at[pl.ds(0, SPLIT), :], last_ref)]
    for at, ref in enumerate((own_ref, z0_ref, z1_ref, z2_ref)):
        pairs.append((ref.at[pl.ds(HALF, QUERY_LINES), :], near_ref.at[2 * at]))
        start = SPLIT + (at + STEPS - 1) % STEPS * QUERY_LINES
        pairs.append((y_ref.at[pl.ds(start, QUERY_LINES), :], near_ref.at[2 * at + 1]))
    copy_all(pairs, sems)


def gather_rows(own, z_loads, y_load):
    return pl.pallas_call(
        gather_rows_kernel,
        out_shape=[
            jax.ShapeDtypeStruct((SPLIT, LANES), BF16),
            jax.ShapeDtypeStruct((2 * STEPS, QUERY_LINES, LANES), BF16),
        ],
        in_specs=[ANY] * 5, out_specs=[ANY] * 2, scratch_shapes=[pltpu.SemaphoreType.DMA((9,))],
        compiler_params=vmem(8),
    )(own, *z_loads, y_load)


def project_block(x_ref, copies, table_buf, gain_ref, q_buf, k_buf, v_buf, q_ref, k_ref, v_ref):
    normed = root_scale(x_ref[...], gain_ref[...]).astype(BF16)
    for copy in copies[:2]:
        copy.wait()
    cosine, sine = table_buf[0], table_buf[1]
    lane = lax.broadcasted_iota(jnp.int32, (BLOCK, LANES), 1)
    lower = (lane % ENC_HD) < ENC_HD // 2

    def project(buf, to_ref, cosine, sine):
        for part in range(PARTS):
            values = jnp.dot(normed, buf[:, part * PART : (part + 1) * PART], preferred_element_type=F32)
            for at in range(PART // LANES):
                cut = values[:, at * LANES : (at + 1) * LANES]
                swapped = jnp.where(
                    lower, pltpu.roll(cut, LANES - ENC_HD // 2, 1), pltpu.roll(cut, ENC_HD // 2, 1))
                start = part * PART + at * LANES
                to_ref[:, start : start + LANES] = (cut * cosine + swapped * sine).astype(BF16)

    project(q_buf, q_ref, cosine * 0.125, sine * 0.125)
    for copy in copies[2:3]:
        copy.wait()
    project(k_buf, k_ref, cosine, sine)
    for copy in copies[3:4]:
        copy.wait()
    v_ref[...] = jnp.dot(normed, v_buf[...], preferred_element_type=F32).astype(BF16)


def attend_block(x_ref, copies, q_ref, k_ref, v_ref, o_buf, fgain_ref, mixed_ref, final_ref):
    first = lax.broadcasted_iota(jnp.int32, (BLOCK, LANES), 1) < ENC_HD
    for pair in range(ENC_HEADS // 2):
        cut = slice(pair * LANES, (pair + 1) * LANES)
        query, key, value = q_ref[:, cut], k_ref[:, cut], v_ref[:, cut]
        mixed = []
        for own in (first, jnp.logical_not(first)):
            scores = lax.dot_general(
                key, jnp.where(own, query, jnp.zeros_like(query)),
                (((1,), (1,)), ((), ())), preferred_element_type=F32)
            weights = jnp.exp(scores - jnp.max(scores, axis=0, keepdims=True))
            weights = (weights * (1.0 / jnp.sum(weights, axis=0, keepdims=True))).astype(BF16)
            mixed.append(lax.dot_general(
                weights, value, (((0,), (0,)), ((), ())), preferred_element_type=F32))
        mixed_ref[:, cut] = jnp.where(first, mixed[0], mixed[1]).astype(BF16)
    for copy in copies[4:]:
        copy.wait()
    residual = x_ref[...].astype(F32) + jnp.dot(mixed_ref[...], o_buf[...], preferred_element_type=F32)
    final_ref[...] = root_scale(residual, fgain_ref[...]).astype(BF16)


def encoder_kernel(first_slot, slots, counts_ref, context_ref, taken_ref, wq_ref, wk_ref, wv_ref, wo_ref, table_ref,
                   gain_ref, fgain_ref, out_ref, mixed_ref, x_buf, q_ref, k_ref, v_ref, final_buf, table_buf,
                   q_buf, k_buf, v_buf, o_buf, sems, x_sems, out_sems):
    live, _, takes = live_counts(counts_ref)
    copies = [
        pltpu.make_async_copy(hbm, buf, sems.at[at])
        for at, (hbm, buf) in enumerate(
            ((wq_ref, q_buf), (table_ref, table_buf), (wk_ref, k_buf), (wv_ref, v_buf), (wo_ref, o_buf)))
    ]

    def read(slot):
        at = slot - first_slot
        return pltpu.make_async_copy(context_ref.at[slot], x_buf.at[at], x_sems.at[at])

    def write(slot):
        at = slot - first_slot
        return pltpu.make_async_copy(final_buf.at[at], out_ref.at[at], out_sems.at[at])

    @pl.when(live > first_slot)
    def _():
        if first_slot == 1:
            @pl.when(takes != 0)
            def _():
                pltpu.make_async_copy(taken_ref.at[CAP - 1], x_buf.at[0], x_sems.at[0]).start()

            @pl.when(takes == 0)
            def _():
                read(1).start()
        else:
            read(first_slot).start()
        for copy in copies:
            copy.start()

    for slot in slots:
        @pl.when(live > slot)
        def _():
            at = slot - first_slot
            pending = copies if slot == first_slot else []
            if slot > first_slot:
                read(slot).start()
            read(slot).wait()
            project_block(
                x_buf.at[at], pending, table_buf, gain_ref, q_buf, k_buf, v_buf, q_ref, k_ref, v_ref)
            attend_block(
                x_buf.at[at], pending, q_ref, k_ref, v_ref, o_buf, fgain_ref, mixed_ref, final_buf.at[at])
            write(slot).start()
            write(slot).wait()


SQUARE, WHOLE = pltpu.VMEM((D_ENC, D_ENC), BF16), pltpu.VMEM((BLOCK, D_ENC), BF16)
TABLES = pltpu.VMEM((2, BLOCK, LANES), F32)


def vmem(mebibytes):
    return pltpu.CompilerParams(vmem_limit_bytes=mebibytes * 2**20)


def cost(flops):
    return pl.CostEstimate(flops=flops, bytes_accessed=9 * 2**20, transcendentals=2**20)


def encode(slots, counts, context, taken, weights):
    blocks = pltpu.VMEM((len(slots), BLOCK, D_ENC), BF16)
    return pl.pallas_call(
        functools.partial(encoder_kernel, slots[0], slots),
        out_shape=jax.ShapeDtypeStruct((len(slots), BLOCK, D_ENC), BF16),
        in_specs=[SMEM] + [HBM] * 7 + [VMEM] * 2,
        out_specs=HBM,
        scratch_shapes=[WHOLE, blocks, WHOLE, WHOLE, WHOLE, blocks, TABLES] + [SQUARE] * 4
        + [pltpu.SemaphoreType.DMA((5,)), pltpu.SemaphoreType.DMA((2,)), pltpu.SemaphoreType.DMA((2,))],
        compiler_params=vmem(63), cost_estimate=cost(9 * 10**9),
    )(counts, context, taken, *weights)


def three_parts(values):
    high = values.astype(BF16).astype(F32)
    middle = (values - high).astype(BF16).astype(F32)
    return high, middle, values - high - middle


def ring_chips(me):
    z, y = me // 4, lax.rem(me // 2, 2)
    place = jnp.where(z == 3, 2, jnp.where(z == 2, 3, z))
    chips = []
    for step in range(4):
        at = lax.rem(place + 4 - step, 4)
        z = jnp.where(at == 2, 3, jnp.where(at == 3, 2, at))
        chips.append((2 * z + y, 2 * z + 1 - y))
    return chips


def cross_kernel(counts_ref, *refs):
    token0, token12, far0, far12, own_ref, beside_ref = refs[:6]
    z_refs, (x_ref, y_ref, last_ref), (near_ref, far_ref) = refs[6:9], refs[9:12], refs[12:14]
    out_ref, token_buf, weight_buf, query_buf, score_ref, value_ref, total_ref, top_ref, sum_ref = refs[14:23]
    sems, token_sems, row_sems = refs[23:]
    tokens = (token0.at[0], token12.at[0], token12.at[1], far0.at[0], far12.at[0], far12.at[1])
    me = lax.axis_index("ctx")
    core = lax.rem(me, 2)
    own_live, other_live, _ = live_counts(counts_ref)
    chips = ring_chips(me)
    mine = pl.multiple_of(lax.axis_index("groups") * HALF, HALF)
    theirs = pl.multiple_of(HALF - mine, HALF)
    copies = []

    def fetch(source, row, rows, step, side):
        column = pl.multiple_of(chips[step][side] * LANES, LANES)
        copies.append(pltpu.make_async_copy(
            source, weight_buf.at[pl.ds(row, rows), pl.ds(column, LANES)], sems.at[len(copies)]))

    fetch(own_ref, 0, D_ENC, 0, 0)
    fetch(beside_ref, 0, D_ENC, 0, 1)
    for step in range(1, STEPS):
        piece = slice((step - 1) * HALF, step * HALF)
        fetch(z_refs[step - 1].at[:HALF, :], mine, HALF, step, 0)
        fetch(x_ref.at[piece, :], theirs, HALF, step, 0)
        fetch(y_ref.at[piece, :], mine, HALF, step, 1)
        fetch(last_ref.at[piece, :], theirs, HALF, step, 1)
    for step in range(STEPS):
        for side in range(2):
            for at, (source, part) in enumerate(((near_ref, core), (far_ref, 1 - core))):
                start = pl.multiple_of((2 * chips[step][side] + part) * LINES, LINES)
                copies.append(pltpu.make_async_copy(
                    source.at[2 * step + side, :, core], query_buf.at[:, pl.ds(start, LINES), :],
                    row_sems.at[4 * step + 2 * side + at]))

    def token_copy(at):
        return pltpu.make_async_copy(tokens[at], token_buf.at[at], token_sems.at[at])

    def live(at):
        return (own_live > at) if at < CAP else (other_live > at - CAP)

    for copy in copies:
        copy.start()
    for at in range(2 * CAP):
        @pl.when(live(at))
        def _():
            token_copy(at).start()
    total_ref[...] = jnp.zeros_like(total_ref)
    sum_ref[...] = jnp.zeros_like(sum_ref)
    top_ref[...] = jnp.full_like(top_ref, -jnp.inf)
    for copy in copies:
        copy.wait()

    for at in range(2 * CAP):
        @pl.when(live(at))
        def _():
            token_copy(at).wait()
            both = jnp.dot(token_buf[at], weight_buf[...], preferred_element_type=F32).astype(BF16)
            value_ref[at] = both[:, HALF_HEADS * LANES :]
            for head in range(HALF_HEADS):
                scores = lax.dot_general(
                    both[:, head * LANES : (head + 1) * LANES], query_buf[head],
                    (((1,), (1,)), ((), ())), preferred_element_type=F32,
                ) * (1.0 / math.sqrt(HEAD_DIM))
                score_ref[at, head] = scores
                top_ref[head] = jnp.maximum(top_ref[head], jnp.max(scores, axis=0, keepdims=True))

    for at in range(2 * CAP):
        @pl.when(live(at))
        def _():
            for head in range(HALF_HEADS):
                weights = jnp.exp(score_ref[at, head] - top_ref[head])
                sum_ref[head] += jnp.sum(weights, axis=0, keepdims=True)
                total_ref[head] += lax.dot_general(
                    weights.astype(BF16), value_ref[at, :, head * LANES : (head + 1) * LANES],
                    (((0,), (0,)), ((), ())), preferred_element_type=F32)

    lines = total_ref.shape[1]
    notes = []
    for head in range(HALF_HEADS):
        notes += list(three_parts(top_ref[head])) + list(three_parts(sum_ref[head]))
        out_ref[:, head] = total_ref[head].astype(BF16).reshape(2 * CHIPS, LINES, LANES)
    notes = jnp.concatenate(notes + [jnp.zeros((LANES - len(notes), lines), F32)], axis=0).T
    out_ref[:, HALF_HEADS] = notes.astype(BF16).reshape(2 * CHIPS, LINES, LANES)


def cross(counts, *arrays):
    lines = 2 * CHIPS * LINES
    line = pltpu.VMEM((HALF_HEADS, 1, lines), F32)
    return pl.pallas_call(
        cross_kernel,
        out_shape=jax.ShapeDtypeStruct((2 * CHIPS, HALF_HEADS + 1, LINES, LANES), BF16),
        in_specs=[SMEM] + [HBM] * 14,
        out_specs=VMEM,
        scratch_shapes=[
            pltpu.VMEM((2 * CAP, BLOCK, D_ENC), BF16),
            pltpu.VMEM((D_ENC, KV_HEADS * LANES), BF16),
            pltpu.VMEM((HALF_HEADS, lines, LANES), BF16),
            pltpu.VMEM((2 * CAP, HALF_HEADS, BLOCK, lines), F32),
            pltpu.VMEM((2 * CAP, BLOCK, HALF_HEADS * LANES), BF16),
            pltpu.VMEM((HALF_HEADS, lines, LANES), F32),
            line, line,
            pltpu.SemaphoreType.DMA((14,)), pltpu.SemaphoreType.DMA((2 * CAP,)), pltpu.SemaphoreType.DMA((16,)),
        ],
        compiler_params=vmem(63),
        cost_estimate=pl.CostEstimate(flops=6 * 10**9, bytes_accessed=8 * 2**20, transcendentals=2**20),
    )(counts, *arrays)


def combine_kernel(parts_ref, out_ref):
    for core in range(2):
        pieces = [parts_ref.at[2 * chip + core] for chip in range(CHIPS)]
        notes = [piece[HALF_HEADS].astype(F32) for piece in pieces]
        for at in range(HALF_HEADS):
            lane = 6 * at
            tops = [n[:, lane : lane + 1] + n[:, lane + 1 : lane + 2] + n[:, lane + 2 : lane + 3] for n in notes]
            sums = [n[:, lane + 3 : lane + 4] + n[:, lane + 4 : lane + 5] + n[:, lane + 5 : lane + 6] for n in notes]
            top = functools.reduce(jnp.maximum, tops)
            numerator, denominator = 0.0, 0.0
            for share, amount, piece in zip([jnp.exp(t - top) for t in tops], sums, pieces):
                numerator += share * piece[at].astype(F32)
                denominator += share * amount
            lines = numerator / denominator
            for g in range(GROUP):
                start = ((2 * at + core) * GROUP + g) * LANES
                out_ref[:, start : start + LANES] = lines[g * ROWS : (g + 1) * ROWS].astype(BF16)


def combine(parts):
    return pl.pallas_call(
        combine_kernel, out_shape=jax.ShapeDtypeStruct((ROWS, QW), BF16), in_specs=[VMEM], out_specs=VMEM,
        compiler_params=vmem(8),
    )(parts)


NEXT_Z = (1, 3, 0, 2)


def exchange(values, bits):
    return lax.ppermute(values, "ctx", [(i, i ^ bits) for i in range(2 * CHIPS)])


def round_z(values, steps=1):
    ring = []
    for i in range(2 * CHIPS):
        z = i // 4
        for _ in range(steps):
            z = NEXT_Z[z]
        ring.append((i, 4 * z + i % 4))
    return lax.ppermute(values, "ctx", ring)


def swap_x(values):
    return lax.ppermute(values, "groups", [(0, 1), (1, 0)])


def local(context, counts, queries, norm_gain, w_query, w_key, w_value, w_out, final_gain, w_kv):
    own = prepare(w_kv, queries)
    z_loads = [round_z(own, steps) for steps in range(1, STEPS)]
    beside0 = exchange(w_kv, 2)
    taken = exchange(context, 1)
    weights = (w_query, w_key, w_value, w_out, rotary_lanes(), norm_gain, final_gain)
    token0 = encode((0,), counts, context, context, weights)
    *z_loads, token0, beside0, taken = lax.optimization_barrier((*z_loads, token0, beside0, taken))
    columns, side = collect(own, z_loads)
    x_load = swap_x(columns)
    y_load = exchange(side, 2)
    far0 = exchange(token0, 1)
    token12 = encode((1, 2), counts, context, taken, weights)
    x_load, y_load, far0, token12 = lax.optimization_barrier((x_load, y_load, far0, token12))
    last, near = gather_rows(own, z_loads, y_load)
    last = swap_x(last)
    near = near.reshape(2 * STEPS, HALF_HEADS, 2, LINES, LANES)
    far12 = exchange(token12, 1)
    parts = cross(
        counts, token0, token12, far0, far12, w_kv, beside0, *z_loads, x_load, y_load, last, near, exchange(near, 1))
    return combine(lax.all_to_all(parts, "ctx", 0, 0, tiled=True))


def rotary_tables(length, head_width):
    position = jnp.arange(length).astype(jnp.float32)[:, None]
    frequency = jnp.exp(
        jnp.arange(head_width // 2).astype(jnp.float32) * (-2.0 * math.log(10000.0) / head_width)
    )
    phase_angle = position * frequency[None, :]
    return (jnp.cos(phase_angle)[:, None, :], jnp.sin(phase_angle)[:, None, :])


def rotate(values, cosine_table, sine_table):
    half_width = values.shape[-1] // 2
    lower_half = values[..., :half_width]
    upper_half = values[..., half_width:]
    return jnp.concatenate(
        [
            lower_half * cosine_table - upper_half * sine_table,
            upper_half * cosine_table + lower_half * sine_table,
        ],
        axis=-1,
    )


def weighted_sums(cross_scores, top_scores, key_alive, cross_values):
    cross_weights = jnp.where(key_alive, jnp.exp(cross_scores - top_scores[..., None]), 0.0)
    total_rows = cross_scores.shape[0]
    denominator = jnp.sum(cross_weights, axis=-1).reshape(total_rows, Q_HEADS)
    numerator = jnp.einsum(
        "rkgt,tkd->rkgd",
        cross_weights.astype(jnp.bfloat16),
        cross_values,
        preferred_element_type=jnp.float32,
    )
    return (numerator.reshape(total_rows, QW), denominator)


def local_any(context, counts, queries, norm_gain, w_query, w_key, w_value, w_out, final_gain, w_kv):
    places = lax.axis_size("ctx")
    device_index = lax.axis_index("ctx")
    device_number = jnp.arange(places)
    own_count = jnp.sum(jnp.where(device_number == device_index, counts, 0))
    alive_slot = jnp.arange(CAP) < own_count
    slot_count = context.shape[0]
    row_count = slot_count * BLOCK
    normed = root_scale(context, norm_gain).astype(jnp.bfloat16).reshape(row_count, D_ENC)
    cosine_table, sine_table = rotary_tables(BLOCK, ENC_HD)

    def project(weight):
        return jnp.dot(normed, weight, preferred_element_type=jnp.float32).reshape(
            slot_count, BLOCK, ENC_HEADS, ENC_HD
        )

    query_rows = rotate(project(w_query), cosine_table, sine_table).astype(jnp.bfloat16)
    key_rows = rotate(project(w_key), cosine_table, sine_table).astype(jnp.bfloat16)
    value_rows = project(w_value).astype(jnp.bfloat16)
    scores = jnp.einsum(
        "sqhd,skhd->shqk", query_rows, key_rows, preferred_element_type=jnp.float32
    ) / math.sqrt(ENC_HD)
    weights = jax.nn.softmax(scores, axis=-1).astype(jnp.bfloat16)
    mixed_rows = jnp.einsum(
        "shqk,skhd->sqhd", weights, value_rows, preferred_element_type=jnp.float32
    )
    mixed_rows = mixed_rows.astype(jnp.bfloat16).reshape(row_count, D_ENC)
    residual = context.reshape(row_count, D_ENC).astype(jnp.float32) + jnp.dot(
        mixed_rows, w_out, preferred_element_type=jnp.float32
    )
    final_norm = root_scale(residual, final_gain).astype(jnp.bfloat16)
    key_value = jnp.dot(
        final_norm,
        lax.all_gather(w_kv, "ctx", axis=1, tiled=True),
        preferred_element_type=jnp.float32,
    ).astype(jnp.bfloat16)
    cross_keys = key_value[:, : KV_HEADS * HEAD_DIM].reshape(row_count, KV_HEADS, HEAD_DIM)
    cross_values = key_value[:, KV_HEADS * HEAD_DIM :].reshape(row_count, KV_HEADS, HEAD_DIM)
    every_query = lax.all_gather(queries, "ctx", axis=0, tiled=True)
    total_rows = every_query.shape[0]
    grouped = every_query.reshape(total_rows, KV_HEADS, GROUP, HEAD_DIM)
    cross_scores = jnp.einsum(
        "rkgd,tkd->rkgt", grouped, cross_keys, preferred_element_type=jnp.float32
    ) / math.sqrt(HEAD_DIM)
    key_alive = jnp.repeat(alive_slot, BLOCK)
    local_top = jnp.max(jnp.where(key_alive, cross_scores, -jnp.inf), axis=-1)
    row_top = lax.pmax(local_top.astype(jnp.bfloat16), "ctx").astype(local_top.dtype)
    numerator, denominator = weighted_sums(cross_scores, row_top, key_alive, cross_values)
    own_numerator, own_denominator = (
        lax.psum_scatter(numerator, "ctx", scatter_dimension=0, tiled=True),
        lax.psum_scatter(denominator, "ctx", scatter_dimension=0, tiled=True),
    )
    own_rows = own_numerator.shape[0]
    result = own_numerator.reshape(own_rows, Q_HEADS, HEAD_DIM) / own_denominator[..., None]
    return result.reshape(own_rows, QW).astype(jnp.bfloat16)


def solution(mesh):
    in_specs = (
        P(("groups", "ctx"), None, None),
        P("groups"),
        P(("groups", "ctx"), None),
        P(),
        P(),
        P(),
        P(),
        P(),
        P(),
        P(None, "ctx"),
    )
    out_specs = P(("groups", "ctx"), None)
    small = mesh.shape["ctx"] == 2 * CHIPS
    return jax.shard_map(local if small else local_any, mesh=mesh, in_specs=in_specs, out_specs=out_specs, check_vma=False)
```

```python
import functools
import math

import jax
import jax.numpy as jnp
import numpy as np
from jax import lax
from jax.experimental import pallas as pl
from jax.experimental.pallas import tpu as pltpu
from jax.sharding import PartitionSpec as P

D_ENC = 1024
ENC_HEADS = 16
ENC_HD = 64
BLOCK = 256
KV_HEADS = 8
HEAD_DIM = 128
Q_HEADS = 32
GROUP = 4
QW = 4096
CAP = 3
HALF_HEADS = KV_HEADS // 2
LANES = 128
CHIPS = 8
ROWS = 4
LINES = ROWS * GROUP
F32 = jnp.float32
BF16 = jnp.bfloat16
VMEM = pl.BlockSpec(memory_space=pltpu.VMEM)
SMEM = pl.BlockSpec(memory_space=pltpu.SMEM)
HBM = pl.BlockSpec(memory_space=pltpu.HBM)
ANY = pl.BlockSpec(memory_space=pl.ANY)
PARTS = 4
PART = D_ENC // PARTS
QUERY_LINES = KV_HEADS * LINES


def root_scale(values, gain):
    values = values.astype(F32)
    return (
        values
        * lax.rsqrt(jnp.mean(values * values, axis=-1, keepdims=True) + 1e-05)
        * gain.astype(F32)
    )


def rotary_lanes():
    position = np.arange(BLOCK, dtype=np.float64)[:, None]
    frequency = 10000.0 ** (-2.0 * np.arange(ENC_HD // 2) / ENC_HD)
    angle = position * frequency[None, :]
    cosine, sine = np.cos(angle), np.sin(angle)
    return jnp.asarray(np.stack([
        np.concatenate([cosine, cosine, cosine, cosine], axis=1),
        np.concatenate([-sine, sine, -sine, sine], axis=1),
    ]), F32)


def live_counts(counts_ref):
    me = lax.axis_index("ctx")
    own, other = counts_ref[me], counts_ref[me + 1 - 2 * lax.rem(me, 2)]
    gives = jnp.where((own == 3) & (other == 1), 1, 0)
    takes = jnp.where((own == 1) & (other == 3), 1, 0)
    return own - gives + takes, other + gives - takes, takes


def prepare_kernel(w_kv_ref, query_ref, out_ref, query_buf, sems):
    copies = [
        pltpu.make_async_copy(query_ref, query_buf, sems.at[0]),
        pltpu.make_async_copy(w_kv_ref, out_ref.at[pl.ds(0, D_ENC), :], sems.at[1]),
    ]
    for copy in copies:
        copy.start()
    copies[0].wait()
    rows = query_buf[...].astype(F32)
    for head in range(KV_HEADS):
        first = head * GROUP
        out_ref[D_ENC + head * LINES : D_ENC + (head + 1) * LINES, :] = jnp.concatenate(
            [rows[:, (first + g) * LANES : (first + g + 1) * LANES] for g in range(GROUP)], axis=0
        ).astype(BF16)
    copies[1].wait()


def prepare(w_kv, queries):
    return pl.pallas_call(
        prepare_kernel,
        out_shape=jax.ShapeDtypeStruct((D_ENC + QUERY_LINES, LANES), BF16),
        in_specs=[HBM] * 2, out_specs=VMEM,
        scratch_shapes=[pltpu.VMEM((ROWS, QW), BF16), pltpu.SemaphoreType.DMA((2,))],
        compiler_params=vmem(63),
    )(w_kv, queries)


def copy_all(pairs, sems):
    copies = [pltpu.make_async_copy(source, target, sems.at[at]) for at, (source, target) in enumerate(pairs)]
    for copy in copies:
        copy.start()
    for copy in copies:
        copy.wait()


def gather_rows_kernel(*refs):
    loads, (early_ref, late_ref, sems) = refs[:7], refs[7:]
    rows = [ref.at[pl.ds(D_ENC, QUERY_LINES), :] for ref in loads]
    copy_all([(row, early_ref.at[at]) for at, row in enumerate(rows[:6])] + [(rows[6], late_ref)], sems)


def gather_rows(*loads):
    early, late = pl.pallas_call(
        gather_rows_kernel,
        out_shape=[
            jax.ShapeDtypeStruct((6, QUERY_LINES, LANES), BF16),
            jax.ShapeDtypeStruct((QUERY_LINES, LANES), BF16),
        ],
        in_specs=[ANY] * 7, out_specs=[ANY] * 2, scratch_shapes=[pltpu.SemaphoreType.DMA((7,))],
        compiler_params=vmem(8),
    )(*loads)
    return early.reshape(6, HALF_HEADS, 2, LINES, LANES), late.reshape(HALF_HEADS, 2, LINES, LANES)


def project_block(x_ref, copies, table_buf, gain_ref, q_buf, k_buf, v_buf, q_ref, k_ref, v_ref):
    normed = root_scale(x_ref[...], gain_ref[...]).astype(BF16)
    for copy in copies[:2]:
        copy.wait()
    cosine, sine = table_buf[0], table_buf[1]
    lane = lax.broadcasted_iota(jnp.int32, (BLOCK, LANES), 1)
    lower = (lane % ENC_HD) < ENC_HD // 2

    def project(buf, to_ref, cosine, sine):
        for part in range(PARTS):
            values = jnp.dot(normed, buf[:, part * PART : (part + 1) * PART], preferred_element_type=F32)
            for at in range(PART // LANES):
                cut = values[:, at * LANES : (at + 1) * LANES]
                swapped = jnp.where(
                    lower, pltpu.roll(cut, LANES - ENC_HD // 2, 1), pltpu.roll(cut, ENC_HD // 2, 1))
                start = part * PART + at * LANES
                to_ref[:, start : start + LANES] = (cut * cosine + swapped * sine).astype(BF16)

    project(q_buf, q_ref, cosine * 0.125, sine * 0.125)
    for copy in copies[2:3]:
        copy.wait()
    project(k_buf, k_ref, cosine, sine)
    for copy in copies[3:4]:
        copy.wait()
    v_ref[...] = jnp.dot(normed, v_buf[...], preferred_element_type=F32).astype(BF16)


def attend_block(x_ref, copies, q_ref, k_ref, v_ref, o_buf, fgain_ref, mixed_ref, final_ref):
    first = lax.broadcasted_iota(jnp.int32, (BLOCK, LANES), 1) < ENC_HD
    for pair in range(ENC_HEADS // 2):
        cut = slice(pair * LANES, (pair + 1) * LANES)
        query, key, value = q_ref[:, cut], k_ref[:, cut], v_ref[:, cut]
        mixed = []
        for own in (first, jnp.logical_not(first)):
            scores = lax.dot_general(
                key, jnp.where(own, query, jnp.zeros_like(query)),
                (((1,), (1,)), ((), ())), preferred_element_type=F32)
            weights = jnp.exp(scores - jnp.max(scores, axis=0, keepdims=True))
            weights = (weights * (1.0 / jnp.sum(weights, axis=0, keepdims=True))).astype(BF16)
            mixed.append(lax.dot_general(
                weights, value, (((0,), (0,)), ((), ())), preferred_element_type=F32))
        mixed_ref[:, cut] = jnp.where(first, mixed[0], mixed[1]).astype(BF16)
    for copy in copies[4:]:
        copy.wait()
    residual = x_ref[...].astype(F32) + jnp.dot(mixed_ref[...], o_buf[...], preferred_element_type=F32)
    final_ref[...] = root_scale(residual, fgain_ref[...]).astype(BF16)


def first_half_kernel(context_ref, wq_ref, wk_ref, wv_ref, table_ref, gain_ref, out_ref,
                      x_ref, table_buf, q_buf, k_buf, v_buf, q_ref, k_ref, v_ref, sems):
    copies = [
        pltpu.make_async_copy(hbm, buf, sems.at[at])
        for at, (hbm, buf) in enumerate(
            ((context_ref.at[0], x_ref), (wq_ref, q_buf), (table_ref, table_buf), (wk_ref, k_buf), (wv_ref, v_buf)))
    ]
    for copy in copies:
        copy.start()
    copies[0].wait()
    project_block(x_ref, copies[1:], table_buf, gain_ref, q_buf, k_buf, v_buf, q_ref, k_ref, v_ref)
    writes = [
        pltpu.make_async_copy(buf, out_ref.at[at], sems.at[5 + at]) for at, buf in enumerate((q_ref, k_ref, v_ref))]
    for copy in writes:
        copy.start()
    for copy in writes:
        copy.wait()


def second_half_kernel(context_ref, half_ref, wo_ref, fgain_ref, out_ref,
                       x_ref, o_buf, q_ref, k_ref, v_ref, mixed_ref, final_ref, sems):
    copies = [
        pltpu.make_async_copy(hbm, buf, sems.at[at])
        for at, (hbm, buf) in enumerate(
            ((half_ref.at[0], q_ref), (half_ref.at[1], k_ref), (half_ref.at[2], v_ref), (context_ref.at[0], x_ref),
             (wo_ref, o_buf)))
    ]
    for copy in copies:
        copy.start()
    for copy in copies[:4]:
        copy.wait()
    attend_block(x_ref, copies, q_ref, k_ref, v_ref, o_buf, fgain_ref, mixed_ref, final_ref)
    copy = pltpu.make_async_copy(final_ref, out_ref.at[0], sems.at[5])
    copy.start()
    copy.wait()


def encoder_kernel(first_slot, slots, counts_ref, context_ref, taken_ref, wq_ref, wk_ref, wv_ref, wo_ref, table_ref,
                   gain_ref, fgain_ref, out_ref, mixed_ref, x_buf, q_ref, k_ref, v_ref, final_buf, table_buf,
                   q_buf, k_buf, v_buf, o_buf, sems, x_sems, out_sems):
    live, _, takes = live_counts(counts_ref)
    copies = [
        pltpu.make_async_copy(hbm, buf, sems.at[at])
        for at, (hbm, buf) in enumerate(
            ((wq_ref, q_buf), (table_ref, table_buf), (wk_ref, k_buf), (wv_ref, v_buf), (wo_ref, o_buf)))
    ]

    def read(slot):
        at = slot - first_slot
        return pltpu.make_async_copy(context_ref.at[slot], x_buf.at[at], x_sems.at[at])

    def write(slot):
        at = slot - first_slot
        return pltpu.make_async_copy(final_buf.at[at], out_ref.at[at], out_sems.at[at])

    @pl.when(live > first_slot)
    def _():
        if first_slot == 1:
            @pl.when(takes != 0)
            def _():
                pltpu.make_async_copy(taken_ref.at[CAP - 1], x_buf.at[0], x_sems.at[0]).start()

            @pl.when(takes == 0)
            def _():
                read(1).start()
        else:
            read(first_slot).start()
        for copy in copies:
            copy.start()

    for slot in slots:
        @pl.when(live > slot)
        def _():
            at = slot - first_slot
            pending = copies if slot == first_slot else []
            if slot > first_slot:
                read(slot).start()
            read(slot).wait()
            project_block(
                x_buf.at[at], pending, table_buf, gain_ref, q_buf, k_buf, v_buf, q_ref, k_ref, v_ref)
            attend_block(
                x_buf.at[at], pending, q_ref, k_ref, v_ref, o_buf, fgain_ref, mixed_ref, final_buf.at[at])
            write(slot).start()
            write(slot).wait()


SQUARE, WHOLE = pltpu.VMEM((D_ENC, D_ENC), BF16), pltpu.VMEM((BLOCK, D_ENC), BF16)
TABLES = pltpu.VMEM((2, BLOCK, LANES), F32)


def vmem(mebibytes):
    return pltpu.CompilerParams(vmem_limit_bytes=mebibytes * 2**20)


def cost(flops):
    return pl.CostEstimate(flops=flops, bytes_accessed=9 * 2**20, transcendentals=2**20)


def encode(slots, counts, context, taken, weights):
    blocks = pltpu.VMEM((len(slots), BLOCK, D_ENC), BF16)
    return pl.pallas_call(
        functools.partial(encoder_kernel, slots[0], slots),
        out_shape=jax.ShapeDtypeStruct((len(slots), BLOCK, D_ENC), BF16),
        in_specs=[SMEM] + [HBM] * 7 + [VMEM] * 2,
        out_specs=HBM,
        scratch_shapes=[WHOLE, blocks, WHOLE, WHOLE, WHOLE, blocks, TABLES] + [SQUARE] * 4
        + [pltpu.SemaphoreType.DMA((5,)), pltpu.SemaphoreType.DMA((2,)), pltpu.SemaphoreType.DMA((2,))],
        compiler_params=vmem(63), cost_estimate=cost(9 * 10**9),
    )(counts, context, taken, *weights)


def first_half(context, weights):
    w_query, w_key, w_value, _, tables, gain, _ = weights
    return pl.pallas_call(
        first_half_kernel,
        out_shape=jax.ShapeDtypeStruct((3, BLOCK, D_ENC), BF16),
        in_specs=[HBM] * 5 + [VMEM],
        out_specs=HBM,
        scratch_shapes=[WHOLE, TABLES] + [SQUARE] * 3 + [WHOLE] * 3 + [pltpu.SemaphoreType.DMA((8,))],
        compiler_params=vmem(63), cost_estimate=cost(5 * 10**9),
    )(context, w_query, w_key, w_value, tables, gain)


def second_half(context, half, weights):
    return pl.pallas_call(
        second_half_kernel,
        out_shape=jax.ShapeDtypeStruct((1, BLOCK, D_ENC), BF16),
        in_specs=[HBM] * 3 + [VMEM],
        out_specs=HBM,
        scratch_shapes=[WHOLE, SQUARE] + [WHOLE] * 5 + [pltpu.SemaphoreType.DMA((6,))],
        compiler_params=vmem(63), cost_estimate=cost(5 * 10**9),
    )(context, half, weights[3], weights[6])


def three_parts(values):
    high = values.astype(BF16).astype(F32)
    middle = (values - high).astype(BF16).astype(F32)
    return high, middle, values - high - middle


def ring_chips(me):
    z, y = me // 4, lax.rem(me // 2, 2)
    place = jnp.where(z == 3, 2, jnp.where(z == 2, 3, z))
    chips = []
    for step in range(CHIPS // 2):
        at = lax.rem(place + 4 - step, 4)
        z = jnp.where(at == 2, 3, jnp.where(at == 3, 2, at))
        chips.append((2 * z + y, 2 * z + 1 - y))
    return chips


def cross_kernel(counts_ref, *refs):
    token0, token12, far0, far12 = refs[:4]
    loads, (early_ref, late_ref, far_early_ref, far_late_ref, far_last_ref) = refs[4:12], refs[12:17]
    out_ref, token_buf, weight_buf, query_buf, score_ref, value_ref, total_ref, top_ref, sum_ref = refs[17:26]
    sems, token_sems, row_sems = refs[26:]
    tokens = (token0.at[0], token12.at[0], token12.at[1], far0.at[0], far12.at[0], far12.at[1])
    me = lax.axis_index("ctx")
    core = lax.rem(me, 2)
    own_live, other_live, _ = live_counts(counts_ref)
    chips = [chip for pair in ring_chips(me) for chip in pair]
    copies = []
    for at in range(CHIPS):
        column = pl.multiple_of(chips[at] * LANES, LANES)
        copies.append(pltpu.make_async_copy(
            loads[at].at[pl.ds(0, D_ENC), :], weight_buf.at[:, pl.ds(column, LANES)], sems.at[at]))

    def fetch(at, part, source, heads):
        start = pl.multiple_of((2 * chips[at] + part) * LINES, LINES)
        copies.append(pltpu.make_async_copy(
            source, query_buf.at[heads, pl.ds(start, LINES), :], row_sems.at[len(copies) - CHIPS]))

    every = slice(0, HALF_HEADS)
    for at in range(CHIPS - 2):
        fetch(at, core, early_ref.at[at, :, core], every)
        fetch(at, 1 - core, far_early_ref.at[at, :, core], every)
    fetch(CHIPS - 2, core, late_ref.at[:, core], every)
    fetch(CHIPS - 2, 1 - core, far_late_ref.at[:, core], every)
    fetch(CHIPS - 1, 1 - core, far_last_ref.at[:, core], every)
    for head in range(HALF_HEADS):
        start = pl.multiple_of(D_ENC + (2 * head + core) * LINES, LINES)
        fetch(CHIPS - 1, core, loads[CHIPS - 1].at[pl.ds(start, LINES), :], head)

    def token_copy(at):
        return pltpu.make_async_copy(tokens[at], token_buf.at[at], token_sems.at[at])

    def live(at):
        return (own_live > at) if at < CAP else (other_live > at - CAP)

    for copy in copies:
        copy.start()
    for at in range(2 * CAP):
        @pl.when(live(at))
        def _():
            token_copy(at).start()
    total_ref[...] = jnp.zeros_like(total_ref)
    sum_ref[...] = jnp.zeros_like(sum_ref)
    top_ref[...] = jnp.full_like(top_ref, -jnp.inf)
    for copy in copies:
        copy.wait()

    for at in range(2 * CAP):
        @pl.when(live(at))
        def _():
            token_copy(at).wait()
            both = jnp.dot(token_buf[at], weight_buf[...], preferred_element_type=F32).astype(BF16)
            value_ref[at] = both[:, HALF_HEADS * LANES :]
            for head in range(HALF_HEADS):
                scores = lax.dot_general(
                    both[:, head * LANES : (head + 1) * LANES], query_buf[head],
                    (((1,), (1,)), ((), ())), preferred_element_type=F32,
                ) * (1.0 / math.sqrt(HEAD_DIM))
                score_ref[at, head] = scores
                top_ref[head] = jnp.maximum(top_ref[head], jnp.max(scores, axis=0, keepdims=True))

    for at in range(2 * CAP):
        @pl.when(live(at))
        def _():
            for head in range(HALF_HEADS):
                weights = jnp.exp(score_ref[at, head] - top_ref[head])
                sum_ref[head] += jnp.sum(weights, axis=0, keepdims=True)
                total_ref[head] += lax.dot_general(
                    weights.astype(BF16), value_ref[at, :, head * LANES : (head + 1) * LANES],
                    (((0,), (0,)), ((), ())), preferred_element_type=F32)

    lines = total_ref.shape[1]
    notes = []
    for head in range(HALF_HEADS):
        notes += list(three_parts(top_ref[head])) + list(three_parts(sum_ref[head]))
        out_ref[:, head] = total_ref[head].astype(BF16).reshape(2 * CHIPS, LINES, LANES)
    notes = jnp.concatenate(notes + [jnp.zeros((LANES - len(notes), lines), F32)], axis=0).T
    out_ref[:, HALF_HEADS] = notes.astype(BF16).reshape(2 * CHIPS, LINES, LANES)


def cross(counts, *arrays):
    lines = 2 * CHIPS * LINES
    line = pltpu.VMEM((HALF_HEADS, 1, lines), F32)
    return pl.pallas_call(
        cross_kernel,
        out_shape=jax.ShapeDtypeStruct((2 * CHIPS, HALF_HEADS + 1, LINES, LANES), BF16),
        in_specs=[SMEM] + [HBM] * 17,
        out_specs=VMEM,
        scratch_shapes=[
            pltpu.VMEM((2 * CAP, BLOCK, D_ENC), BF16),
            pltpu.VMEM((D_ENC, KV_HEADS * LANES), BF16),
            pltpu.VMEM((HALF_HEADS, lines, LANES), BF16),
            pltpu.VMEM((2 * CAP, HALF_HEADS, BLOCK, lines), F32),
            pltpu.VMEM((2 * CAP, BLOCK, HALF_HEADS * LANES), BF16),
            pltpu.VMEM((HALF_HEADS, lines, LANES), F32),
            line, line,
            pltpu.SemaphoreType.DMA((CHIPS,)), pltpu.SemaphoreType.DMA((2 * CAP,)), pltpu.SemaphoreType.DMA((19,)),
        ],
        compiler_params=vmem(63),
        cost_estimate=pl.CostEstimate(flops=6 * 10**9, bytes_accessed=8 * 2**20, transcendentals=2**20),
    )(counts, *arrays)


def combine_kernel(parts_ref, out_ref):
    for core in range(2):
        pieces = [parts_ref.at[2 * chip + core] for chip in range(CHIPS)]
        notes = [piece[HALF_HEADS].astype(F32) for piece in pieces]
        for at in range(HALF_HEADS):
            lane = 6 * at
            tops = [n[:, lane : lane + 1] + n[:, lane + 1 : lane + 2] + n[:, lane + 2 : lane + 3] for n in notes]
            sums = [n[:, lane + 3 : lane + 4] + n[:, lane + 4 : lane + 5] + n[:, lane + 5 : lane + 6] for n in notes]
            top = functools.reduce(jnp.maximum, tops)
            numerator, denominator = 0.0, 0.0
            for share, amount, piece in zip([jnp.exp(t - top) for t in tops], sums, pieces):
                numerator += share * piece[at].astype(F32)
                denominator += share * amount
            lines = numerator / denominator
            for g in range(GROUP):
                start = ((2 * at + core) * GROUP + g) * LANES
                out_ref[:, start : start + LANES] = lines[g * ROWS : (g + 1) * ROWS].astype(BF16)


def combine(parts):
    return pl.pallas_call(
        combine_kernel, out_shape=jax.ShapeDtypeStruct((ROWS, QW), BF16), in_specs=[VMEM], out_specs=VMEM,
        compiler_params=vmem(8),
    )(parts)


NEXT_Z = (1, 3, 0, 2)


def exchange(values, bits):
    return lax.ppermute(values, "ctx", [(i, i ^ bits) for i in range(2 * CHIPS)])


def round_z(values, steps=1):
    ring = []
    for i in range(2 * CHIPS):
        z = i // 4
        for _ in range(steps):
            z = NEXT_Z[z]
        ring.append((i, 4 * z + i % 4))
    return lax.ppermute(values, "ctx", ring)


def local(context, counts, queries, norm_gain, w_query, w_key, w_value, w_out, final_gain, w_kv):
    weights = (w_query, w_key, w_value, w_out, rotary_lanes(), norm_gain, final_gain)
    load0 = prepare(w_kv, queries)
    load1, beside0, taken = round_z(load0), exchange(load0, 2), exchange(context, 1)
    half = first_half(context, weights)
    load1, beside0, taken, half = lax.optimization_barrier((load1, beside0, taken, half))
    load2, beside1 = round_z(load1), exchange(load1, 2)
    token0 = second_half(context, half, weights)
    load2, beside1, token0 = lax.optimization_barrier((load2, beside1, token0))
    load3, beside2, far0 = round_z(load2), exchange(load2, 2), exchange(token0, 1)
    token12 = encode((1, 2), counts, context, taken, weights)
    load3, beside2, far0, token12 = lax.optimization_barrier((load3, beside2, far0, token12))
    beside3, far12 = exchange(load3, 2), exchange(token12, 1)
    early, late = gather_rows(load0, beside0, load1, beside1, load2, beside2, load3)
    far_early, far_late = exchange(early, 1), exchange(late, 1)
    parts = cross(
        counts, token0, token12, far0, far12, load0, beside0, load1, beside1, load2, beside2, load3, beside3,
        early, late, far_early, far_late, exchange(far_late, 2))
    return combine(lax.all_to_all(parts, "ctx", 0, 0, tiled=True))


def rotary_tables(length, head_width):
    position = jnp.arange(length).astype(jnp.float32)[:, None]
    frequency = jnp.exp(
        jnp.arange(head_width // 2).astype(jnp.float32) * (-2.0 * math.log(10000.0) / head_width)
    )
    phase_angle = position * frequency[None, :]
    return (jnp.cos(phase_angle)[:, None, :], jnp.sin(phase_angle)[:, None, :])


def rotate(values, cosine_table, sine_table):
    half_width = values.shape[-1] // 2
    lower_half = values[..., :half_width]
    upper_half = values[..., half_width:]
    return jnp.concatenate(
        [
            lower_half * cosine_table - upper_half * sine_table,
            upper_half * cosine_table + lower_half * sine_table,
        ],
        axis=-1,
    )


def weighted_sums(cross_scores, top_scores, key_alive, cross_values):
    cross_weights = jnp.where(key_alive, jnp.exp(cross_scores - top_scores[..., None]), 0.0)
    total_rows = cross_scores.shape[0]
    denominator = jnp.sum(cross_weights, axis=-1).reshape(total_rows, Q_HEADS)
    numerator = jnp.einsum(
        "rkgt,tkd->rkgd",
        cross_weights.astype(jnp.bfloat16),
        cross_values,
        preferred_element_type=jnp.float32,
    )
    return (numerator.reshape(total_rows, QW), denominator)


def local_any(context, counts, queries, norm_gain, w_query, w_key, w_value, w_out, final_gain, w_kv):
    places = lax.axis_size("ctx")
    device_index = lax.axis_index("ctx")
    device_number = jnp.arange(places)
    own_count = jnp.sum(jnp.where(device_number == device_index, counts, 0))
    alive_slot = jnp.arange(CAP) < own_count
    slot_count = context.shape[0]
    row_count = slot_count * BLOCK
    normed = root_scale(context, norm_gain).astype(jnp.bfloat16).reshape(row_count, D_ENC)
    cosine_table, sine_table = rotary_tables(BLOCK, ENC_HD)

    def project(weight):
        return jnp.dot(normed, weight, preferred_element_type=jnp.float32).reshape(
            slot_count, BLOCK, ENC_HEADS, ENC_HD
        )

    query_rows = rotate(project(w_query), cosine_table, sine_table).astype(jnp.bfloat16)
    key_rows = rotate(project(w_key), cosine_table, sine_table).astype(jnp.bfloat16)
    value_rows = project(w_value).astype(jnp.bfloat16)
    scores = jnp.einsum(
        "sqhd,skhd->shqk", query_rows, key_rows, preferred_element_type=jnp.float32
    ) / math.sqrt(ENC_HD)
    weights = jax.nn.softmax(scores, axis=-1).astype(jnp.bfloat16)
    mixed_rows = jnp.einsum(
        "shqk,skhd->sqhd", weights, value_rows, preferred_element_type=jnp.float32
    )
    mixed_rows = mixed_rows.astype(jnp.bfloat16).reshape(row_count, D_ENC)
    residual = context.reshape(row_count, D_ENC).astype(jnp.float32) + jnp.dot(
        mixed_rows, w_out, preferred_element_type=jnp.float32
    )
    final_norm = root_scale(residual, final_gain).astype(jnp.bfloat16)
    key_value = jnp.dot(
        final_norm,
        lax.all_gather(w_kv, "ctx", axis=1, tiled=True),
        preferred_element_type=jnp.float32,
    ).astype(jnp.bfloat16)
    cross_keys = key_value[:, : KV_HEADS * HEAD_DIM].reshape(row_count, KV_HEADS, HEAD_DIM)
    cross_values = key_value[:, KV_HEADS * HEAD_DIM :].reshape(row_count, KV_HEADS, HEAD_DIM)
    every_query = lax.all_gather(queries, "ctx", axis=0, tiled=True)
    total_rows = every_query.shape[0]
    grouped = every_query.reshape(total_rows, KV_HEADS, GROUP, HEAD_DIM)
    cross_scores = jnp.einsum(
        "rkgd,tkd->rkgt", grouped, cross_keys, preferred_element_type=jnp.float32
    ) / math.sqrt(HEAD_DIM)
    key_alive = jnp.repeat(alive_slot, BLOCK)
    local_top = jnp.max(jnp.where(key_alive, cross_scores, -jnp.inf), axis=-1)
    row_top = lax.pmax(local_top.astype(jnp.bfloat16), "ctx").astype(local_top.dtype)
    numerator, denominator = weighted_sums(cross_scores, row_top, key_alive, cross_values)
    own_numerator, own_denominator = (
        lax.psum_scatter(numerator, "ctx", scatter_dimension=0, tiled=True),
        lax.psum_scatter(denominator, "ctx", scatter_dimension=0, tiled=True),
    )
    own_rows = own_numerator.shape[0]
    result = own_numerator.reshape(own_rows, Q_HEADS, HEAD_DIM) / own_denominator[..., None]
    return result.reshape(own_rows, QW).astype(jnp.bfloat16)


def solution(mesh):
    in_specs = (
        P(("groups", "ctx"), None, None),
        P("groups"),
        P(("groups", "ctx"), None),
        P(),
        P(),
        P(),
        P(),
        P(),
        P(),
        P(None, "ctx"),
    )
    out_specs = P(("groups", "ctx"), None)
    small = mesh.shape["ctx"] == 2 * CHIPS
    return jax.shard_map(local if small else local_any, mesh=mesh, in_specs=in_specs, out_specs=out_specs, check_vma=False)
```

```python
import functools
import math

import jax
import jax.numpy as jnp
import numpy as np
from jax import lax
from jax.experimental import pallas as pl
from jax.experimental.pallas import tpu as pltpu
from jax.sharding import PartitionSpec as P

D_ENC = 1024
ENC_HEADS = 16
ENC_HD = 64
BLOCK = 256
KV_HEADS = 8
HEAD_DIM = 128
Q_HEADS = 32
GROUP = 4
QW = 4096
CAP = 3
HALF_HEADS = KV_HEADS // 2
LANES = 128
CHIPS = 8
ROWS = 4
LINES = ROWS * GROUP
F32 = jnp.float32
BF16 = jnp.bfloat16
VMEM = pl.BlockSpec(memory_space=pltpu.VMEM)
SMEM = pl.BlockSpec(memory_space=pltpu.SMEM)
HBM = pl.BlockSpec(memory_space=pltpu.HBM)
ANY = pl.BlockSpec(memory_space=pl.ANY)
PARTS = 4
PART = D_ENC // PARTS
QUERY_LINES = KV_HEADS * LINES


def root_scale(values, gain):
    values = values.astype(F32)
    return (
        values
        * lax.rsqrt(jnp.mean(values * values, axis=-1, keepdims=True) + 1e-05)
        * gain.astype(F32)
    )


def rotary_lanes():
    position = np.arange(BLOCK, dtype=np.float64)[:, None]
    frequency = 10000.0 ** (-2.0 * np.arange(ENC_HD // 2) / ENC_HD)
    angle = position * frequency[None, :]
    cosine, sine = np.cos(angle), np.sin(angle)
    return jnp.asarray(np.stack([
        np.concatenate([cosine, cosine, cosine, cosine], axis=1),
        np.concatenate([-sine, sine, -sine, sine], axis=1),
    ]), F32)


def live_counts(counts_ref):
    me = lax.axis_index("ctx")
    own, other = counts_ref[me], counts_ref[me + 1 - 2 * lax.rem(me, 2)]
    gives = jnp.where((own == 3) & (other == 1), 1, 0)
    takes = jnp.where((own == 1) & (other == 3), 1, 0)
    return own - gives + takes, other + gives - takes, takes


def prepare_kernel(query_ref, out_ref):
    rows = query_ref[...].astype(F32)
    for head in range(KV_HEADS):
        first = head * GROUP
        out_ref[head * LINES : (head + 1) * LINES, :] = jnp.concatenate(
            [rows[:, (first + g) * LANES : (first + g + 1) * LANES] for g in range(GROUP)], axis=0
        ).astype(BF16)


def prepare(queries):
    return pl.pallas_call(
        prepare_kernel,
        out_shape=jax.ShapeDtypeStruct((QUERY_LINES, LANES), BF16),
        in_specs=[VMEM], out_specs=VMEM, compiler_params=vmem(63),
    )(queries)


def copy_all(pairs, sems):
    copies = [pltpu.make_async_copy(source, target, sems.at[at]) for at, (source, target) in enumerate(pairs)]
    for copy in copies:
        copy.start()
    for copy in copies:
        copy.wait()


def stack_kernel(*refs):
    *pieces, out_ref, sems = refs
    copy_all([(piece, out_ref.at[at]) for at, piece in enumerate(pieces)], sems)


def stack(*pieces):
    return pl.pallas_call(
        stack_kernel,
        out_shape=jax.ShapeDtypeStruct((len(pieces), QUERY_LINES, LANES), BF16),
        in_specs=[HBM] * len(pieces), out_specs=HBM,
        scratch_shapes=[pltpu.SemaphoreType.DMA((len(pieces),))], compiler_params=vmem(63),
    )(*pieces).reshape(len(pieces), HALF_HEADS, 2, LINES, LANES)


def project_block(x_ref, copies, table_buf, gain_ref, q_buf, k_buf, v_buf, q_ref, k_ref, v_ref):
    normed = root_scale(x_ref[...], gain_ref[...]).astype(BF16)
    for copy in copies[:2]:
        copy.wait()
    cosine, sine = table_buf[0], table_buf[1]
    lane = lax.broadcasted_iota(jnp.int32, (BLOCK, LANES), 1)
    lower = (lane % ENC_HD) < ENC_HD // 2

    def project(buf, to_ref, cosine, sine):
        for part in range(PARTS):
            values = jnp.dot(normed, buf[:, part * PART : (part + 1) * PART], preferred_element_type=F32)
            for at in range(PART // LANES):
                cut = values[:, at * LANES : (at + 1) * LANES]
                swapped = jnp.where(
                    lower, pltpu.roll(cut, LANES - ENC_HD // 2, 1), pltpu.roll(cut, ENC_HD // 2, 1))
                start = part * PART + at * LANES
                to_ref[:, start : start + LANES] = (cut * cosine + swapped * sine).astype(BF16)

    project(q_buf, q_ref, cosine * 0.125, sine * 0.125)
    for copy in copies[2:3]:
        copy.wait()
    project(k_buf, k_ref, cosine, sine)
    for copy in copies[3:4]:
        copy.wait()
    v_ref[...] = jnp.dot(normed, v_buf[...], preferred_element_type=F32).astype(BF16)


def attend_block(x_ref, copies, q_ref, k_ref, v_ref, o_buf, fgain_ref, mixed_ref, final_ref):
    first = lax.broadcasted_iota(jnp.int32, (BLOCK, LANES), 1) < ENC_HD
    for pair in range(ENC_HEADS // 2):
        cut = slice(pair * LANES, (pair + 1) * LANES)
        query, key, value = q_ref[:, cut], k_ref[:, cut], v_ref[:, cut]
        mixed = []
        for own in (first, jnp.logical_not(first)):
            scores = lax.dot_general(
                key, jnp.where(own, query, jnp.zeros_like(query)),
                (((1,), (1,)), ((), ())), preferred_element_type=F32)
            weights = jnp.exp(scores - jnp.max(scores, axis=0, keepdims=True))
            weights = (weights * (1.0 / jnp.sum(weights, axis=0, keepdims=True))).astype(BF16)
            mixed.append(lax.dot_general(
                weights, value, (((0,), (0,)), ((), ())), preferred_element_type=F32))
        mixed_ref[:, cut] = jnp.where(first, mixed[0], mixed[1]).astype(BF16)
    for copy in copies[4:]:
        copy.wait()
    residual = x_ref[...].astype(F32) + jnp.dot(mixed_ref[...], o_buf[...], preferred_element_type=F32)
    final_ref[...] = root_scale(residual, fgain_ref[...]).astype(BF16)


def first_half_kernel(context_ref, wq_ref, wk_ref, wv_ref, table_ref, gain_ref, out_ref,
                      x_ref, table_buf, q_buf, k_buf, v_buf, q_ref, k_ref, v_ref, sems):
    copies = [
        pltpu.make_async_copy(hbm, buf, sems.at[at])
        for at, (hbm, buf) in enumerate(
            ((context_ref.at[0], x_ref), (wq_ref, q_buf), (table_ref, table_buf), (wk_ref, k_buf), (wv_ref, v_buf)))
    ]
    for copy in copies:
        copy.start()
    copies[0].wait()
    project_block(x_ref, copies[1:], table_buf, gain_ref, q_buf, k_buf, v_buf, q_ref, k_ref, v_ref)
    writes = [
        pltpu.make_async_copy(buf, out_ref.at[at], sems.at[5 + at]) for at, buf in enumerate((q_ref, k_ref, v_ref))]
    for copy in writes:
        copy.start()
    for copy in writes:
        copy.wait()


def second_half_kernel(context_ref, half_ref, wo_ref, fgain_ref, out_ref,
                       x_ref, o_buf, q_ref, k_ref, v_ref, mixed_ref, final_ref, sems):
    copies = [
        pltpu.make_async_copy(hbm, buf, sems.at[at])
        for at, (hbm, buf) in enumerate(
            ((half_ref.at[0], q_ref), (half_ref.at[1], k_ref), (half_ref.at[2], v_ref), (context_ref.at[0], x_ref),
             (wo_ref, o_buf)))
    ]
    for copy in copies:
        copy.start()
    for copy in copies[:4]:
        copy.wait()
    attend_block(x_ref, copies, q_ref, k_ref, v_ref, o_buf, fgain_ref, mixed_ref, final_ref)
    copy = pltpu.make_async_copy(final_ref, out_ref.at[0], sems.at[5])
    copy.start()
    copy.wait()


def encoder_kernel(first_slot, slots, counts_ref, context_ref, taken_ref, wq_ref, wk_ref, wv_ref, wo_ref, table_ref,
                   gain_ref, fgain_ref, out_ref, mixed_ref, x_buf, q_ref, k_ref, v_ref, final_buf, table_buf,
                   q_buf, k_buf, v_buf, o_buf, sems, x_sems, out_sems):
    live, _, takes = live_counts(counts_ref)
    copies = [
        pltpu.make_async_copy(hbm, buf, sems.at[at])
        for at, (hbm, buf) in enumerate(
            ((wq_ref, q_buf), (table_ref, table_buf), (wk_ref, k_buf), (wv_ref, v_buf), (wo_ref, o_buf)))
    ]

    def read(slot):
        at = slot - first_slot
        return pltpu.make_async_copy(context_ref.at[slot], x_buf.at[at], x_sems.at[at])

    def write(slot):
        at = slot - first_slot
        return pltpu.make_async_copy(final_buf.at[at], out_ref.at[at], out_sems.at[at])

    @pl.when(live > first_slot)
    def _():
        if first_slot == 1:
            @pl.when(takes != 0)
            def _():
                pltpu.make_async_copy(taken_ref.at[CAP - 1], x_buf.at[0], x_sems.at[0]).start()

            @pl.when(takes == 0)
            def _():
                read(1).start()
        else:
            read(first_slot).start()
        for copy in copies:
            copy.start()

    for slot in slots:
        @pl.when(live > slot)
        def _():
            at = slot - first_slot
            pending = copies if slot == first_slot else []
            if slot > first_slot:
                read(slot).start()
            read(slot).wait()
            project_block(
                x_buf.at[at], pending, table_buf, gain_ref, q_buf, k_buf, v_buf, q_ref, k_ref, v_ref)
            attend_block(
                x_buf.at[at], pending, q_ref, k_ref, v_ref, o_buf, fgain_ref, mixed_ref, final_buf.at[at])
            write(slot).start()
            write(slot).wait()


SQUARE, WHOLE = pltpu.VMEM((D_ENC, D_ENC), BF16), pltpu.VMEM((BLOCK, D_ENC), BF16)
TABLES = pltpu.VMEM((2, BLOCK, LANES), F32)


def vmem(mebibytes):
    return pltpu.CompilerParams(vmem_limit_bytes=mebibytes * 2**20)


def cost(flops):
    return pl.CostEstimate(flops=flops, bytes_accessed=9 * 2**20, transcendentals=2**20)


def encode(slots, counts, context, taken, weights):
    blocks = pltpu.VMEM((len(slots), BLOCK, D_ENC), BF16)
    return pl.pallas_call(
        functools.partial(encoder_kernel, slots[0], slots),
        out_shape=jax.ShapeDtypeStruct((len(slots), BLOCK, D_ENC), BF16),
        in_specs=[SMEM] + [HBM] * 7 + [VMEM] * 2,
        out_specs=HBM,
        scratch_shapes=[WHOLE, blocks, WHOLE, WHOLE, WHOLE, blocks, TABLES] + [SQUARE] * 4
        + [pltpu.SemaphoreType.DMA((5,)), pltpu.SemaphoreType.DMA((2,)), pltpu.SemaphoreType.DMA((2,))],
        compiler_params=vmem(63), cost_estimate=cost(9 * 10**9),
    )(counts, context, taken, *weights)


def first_half(context, weights):
    w_query, w_key, w_value, _, tables, gain, _ = weights
    return pl.pallas_call(
        first_half_kernel,
        out_shape=jax.ShapeDtypeStruct((3, BLOCK, D_ENC), BF16),
        in_specs=[HBM] * 5 + [VMEM],
        out_specs=HBM,
        scratch_shapes=[WHOLE, TABLES] + [SQUARE] * 3 + [WHOLE] * 3 + [pltpu.SemaphoreType.DMA((8,))],
        compiler_params=vmem(63), cost_estimate=cost(5 * 10**9),
    )(context, w_query, w_key, w_value, tables, gain)


def second_half(context, half, weights):
    return pl.pallas_call(
        second_half_kernel,
        out_shape=jax.ShapeDtypeStruct((1, BLOCK, D_ENC), BF16),
        in_specs=[HBM] * 3 + [VMEM],
        out_specs=HBM,
        scratch_shapes=[WHOLE, SQUARE] + [WHOLE] * 5 + [pltpu.SemaphoreType.DMA((6,))],
        compiler_params=vmem(63), cost_estimate=cost(5 * 10**9),
    )(context, half, weights[3], weights[6])


def three_parts(values):
    high = values.astype(BF16).astype(F32)
    middle = (values - high).astype(BF16).astype(F32)
    return high, middle, values - high - middle


def ring_chips(me):
    z, y = me // 4, lax.rem(me // 2, 2)
    place = jnp.where(z == 3, 2, jnp.where(z == 2, 3, z))
    chips = []
    for step in range(CHIPS // 2):
        at = lax.rem(place + 4 - step, 4)
        z = jnp.where(at == 2, 3, jnp.where(at == 3, 2, at))
        chips.append((2 * z + y, 2 * z + 1 - y))
    return chips


def last_load(me):
    place = ring_chips(me)[3][1]
    return place, lax.rem(place, HALF_HEADS)


def live_tokens(counts_ref, token0, token12, far0, far12, token_buf, token_sems):
    own_live, other_live, _ = live_counts(counts_ref)
    tokens = (token0.at[0], token12.at[0], token12.at[1], far0.at[0], far12.at[0], far12.at[1])
    lives = [own_live > at for at in range(CAP)] + [other_live > at for at in range(CAP)]
    copies = [pltpu.make_async_copy(tokens[at], token_buf.at[at], token_sems.at[at]) for at in range(2 * CAP)]
    return list(zip(lives, copies))


def score(key, query):
    return lax.dot_general(
        key, query, (((1,), (1,)), ((), ())), preferred_element_type=F32) * (1.0 / math.sqrt(HEAD_DIM))


def weigh(weights, value):
    return lax.dot_general(
        weights.astype(BF16), value, (((0,), (0,)), ((), ())), preferred_element_type=F32)


def cross_kernel(counts_ref, *refs):
    loads, rows = refs[4:11], refs[11:15]
    out_ref, stat_ref, rest_ref, last_query_ref = refs[15:19]
    token_buf, weight_buf, query_buf, kv_ref, score_ref, total_ref, top_ref, sum_ref = refs[19:27]
    sems, token_sems, row_sems = refs[27:]
    me = lax.axis_index("ctx")
    core = lax.rem(me, 2)
    chips = [chip for pair in ring_chips(me) for chip in pair]
    last, last_head = last_load(me)
    heads = [jnp.where(last_head <= at, at + 1, at) for at in range(HALF_HEADS - 1)]
    copies = []
    for at, load in enumerate(loads):
        column = pl.multiple_of(chips[at] * LANES, LANES)
        copies.append(pltpu.make_async_copy(load, weight_buf.at[:, pl.ds(column, LANES)], sems.at[at]))
    for at, chip in enumerate(chips):
        for far in range(2):
            part = 1 - core if far else core
            start = pl.multiple_of((2 * chip + part) * LINES, LINES)
            copies.append(pltpu.make_async_copy(
                rows[2 * (at % 2) + far].at[at // 2, :, core], query_buf.at[:, pl.ds(start, LINES), :],
                row_sems.at[2 * at + far]))
    tokens = live_tokens(counts_ref, *refs[:4], token_buf, token_sems)
    for copy in copies:
        copy.start()
    for live, copy in tokens:
        @pl.when(live)
        def _():
            copy.start()
    total_ref[...] = jnp.zeros_like(total_ref)
    sum_ref[...] = jnp.zeros_like(sum_ref)
    top_ref[...] = jnp.full_like(top_ref, -jnp.inf)
    for copy in copies:
        copy.wait()

    for at, (live, copy) in enumerate(tokens):
        @pl.when(live)
        def _():
            copy.wait()
            both = jnp.dot(token_buf[at], weight_buf[...], preferred_element_type=F32).astype(BF16)
            for place in range(KV_HEADS):
                kv_ref[at, place] = both[:, place * LANES : (place + 1) * LANES]
            rest_ref[at] = kv_ref[at, lax.rem(last + HALF_HEADS, KV_HEADS)]
            for i, head in enumerate(heads):
                scores = score(kv_ref[at, head], query_buf[head])
                score_ref[at, i] = scores
                top_ref[i] = jnp.maximum(top_ref[i], jnp.max(scores, axis=0, keepdims=True))

    for at, (live, _) in enumerate(tokens):
        @pl.when(live)
        def _():
            for i, head in enumerate(heads):
                weights = jnp.exp(score_ref[at, i] - top_ref[i])
                sum_ref[i] += jnp.sum(weights, axis=0, keepdims=True)
                total_ref[i] += weigh(weights, kv_ref[at, HALF_HEADS + head])

    last_query_ref[...] = query_buf[last_head]
    for i, head in enumerate(heads):
        stat_ref[0, head] = top_ref[i]
        stat_ref[1, head] = sum_ref[i]
        out_ref[:, head] = total_ref[i].astype(BF16).reshape(2 * CHIPS, LINES, LANES)


def cross(counts, *arrays):
    lines = 2 * CHIPS * LINES
    heads = HALF_HEADS - 1
    line = pltpu.VMEM((heads, 1, lines), F32)
    return pl.pallas_call(
        cross_kernel,
        out_shape=[
            jax.ShapeDtypeStruct((2 * CHIPS, HALF_HEADS + 1, LINES, LANES), BF16),
            jax.ShapeDtypeStruct((2, HALF_HEADS, 1, lines), F32),
            jax.ShapeDtypeStruct((2 * CAP, BLOCK, LANES), BF16),
            jax.ShapeDtypeStruct((lines, LANES), BF16),
        ],
        in_specs=[SMEM] + [HBM] * 15,
        out_specs=[VMEM] * 4,
        scratch_shapes=[
            pltpu.VMEM((2 * CAP, BLOCK, D_ENC), BF16),
            pltpu.VMEM((D_ENC, KV_HEADS * LANES), BF16),
            pltpu.VMEM((HALF_HEADS, lines, LANES), BF16),
            pltpu.VMEM((2 * CAP, KV_HEADS, BLOCK, LANES), BF16),
            pltpu.VMEM((2 * CAP, heads, BLOCK, lines), F32),
            pltpu.VMEM((heads, lines, LANES), F32),
            line, line,
            pltpu.SemaphoreType.DMA((CHIPS - 1,)), pltpu.SemaphoreType.DMA((2 * CAP,)),
            pltpu.SemaphoreType.DMA((2 * CHIPS,)),
        ],
        compiler_params=vmem(63), cost_estimate=cost(8 * 10**9),
    )(counts, *arrays)


def last_head_kernel(counts_ref, *refs):
    load_ref, rest_ref, stat_ref, query_ref, _, out_ref = refs[4:10]
    token_buf, weight_buf, rest_buf, value_ref, score_ref, total_ref, top_ref, sum_ref, head_buf, note_buf = refs[10:20]
    sems, token_sems = refs[20:]
    last, last_head = last_load(lax.axis_index("ctx"))
    keys_last = last < HALF_HEADS
    copies = [
        pltpu.make_async_copy(load_ref, weight_buf, sems.at[0]),
        pltpu.make_async_copy(rest_ref, rest_buf, sems.at[1]),
    ]
    tokens = live_tokens(counts_ref, *refs[:4], token_buf, token_sems)
    for copy in copies:
        copy.start()
    for live, copy in tokens:
        @pl.when(live)
        def _():
            copy.start()
    total_ref[...] = jnp.zeros_like(total_ref)
    sum_ref[...] = jnp.zeros_like(sum_ref)
    top_ref[...] = jnp.full_like(top_ref, -jnp.inf)
    for copy in copies:
        copy.wait()

    for at, (live, copy) in enumerate(tokens):
        @pl.when(live)
        def _():
            copy.wait()
            fresh = jnp.dot(token_buf[at], weight_buf[...], preferred_element_type=F32).astype(BF16)
            rest = rest_buf[at]
            value_ref[at] = jnp.where(keys_last, rest, fresh)
            scores = score(jnp.where(keys_last, fresh, rest), query_ref[...])
            score_ref[at] = scores
            top_ref[...] = jnp.maximum(top_ref[...], jnp.max(scores, axis=0, keepdims=True))

    for at, (live, _) in enumerate(tokens):
        @pl.when(live)
        def _():
            weights = jnp.exp(score_ref[at] - top_ref[...])
            sum_ref[...] += jnp.sum(weights, axis=0, keepdims=True)
            total_ref[...] += weigh(weights, value_ref[at])

    lines = query_ref.shape[0]
    notes = []
    for head in range(HALF_HEADS):
        fresh = last_head == head
        notes += list(three_parts(jnp.where(fresh, top_ref[...], stat_ref[0, head])))
        notes += list(three_parts(jnp.where(fresh, sum_ref[...], stat_ref[1, head])))
    notes = jnp.concatenate(notes + [jnp.zeros((LANES - len(notes), lines), F32)], axis=0).T
    head_buf[...] = total_ref[...].astype(BF16).reshape(2 * CHIPS, LINES, LANES)
    note_buf[...] = notes.astype(BF16).reshape(2 * CHIPS, LINES, LANES)
    copy_all([(head_buf, out_ref.at[:, last_head]), (note_buf, out_ref.at[:, HALF_HEADS])], sems)


def add_last_head(counts, tokens, load, rest, stats, query, parts):
    lines = 2 * CHIPS * LINES
    piece = pltpu.VMEM((2 * CHIPS, LINES, LANES), BF16)
    return pl.pallas_call(
        last_head_kernel,
        out_shape=jax.ShapeDtypeStruct(parts.shape, BF16),
        in_specs=[SMEM] + [HBM] * 6 + [VMEM] * 2 + [HBM],
        out_specs=HBM,
        scratch_shapes=[
            pltpu.VMEM((2 * CAP, BLOCK, D_ENC), BF16),
            pltpu.VMEM((D_ENC, LANES), BF16),
            pltpu.VMEM((2 * CAP, BLOCK, LANES), BF16),
            pltpu.VMEM((2 * CAP, BLOCK, LANES), BF16),
            pltpu.VMEM((2 * CAP, BLOCK, lines), F32),
            pltpu.VMEM((lines, LANES), F32),
            pltpu.VMEM((1, lines), F32), pltpu.VMEM((1, lines), F32),
            piece, piece,
            pltpu.SemaphoreType.DMA((2,)), pltpu.SemaphoreType.DMA((2 * CAP,)),
        ],
        input_output_aliases={9: 0},
        compiler_params=vmem(63), cost_estimate=cost(4 * 10**9),
    )(counts, *tokens, load, rest, stats, query, parts)


def combine_kernel(parts_ref, out_ref):
    for core in range(2):
        pieces = [parts_ref.at[2 * chip + core] for chip in range(CHIPS)]
        notes = [piece[HALF_HEADS].astype(F32) for piece in pieces]
        for at in range(HALF_HEADS):
            lane = 6 * at
            tops = [n[:, lane : lane + 1] + n[:, lane + 1 : lane + 2] + n[:, lane + 2 : lane + 3] for n in notes]
            sums = [n[:, lane + 3 : lane + 4] + n[:, lane + 4 : lane + 5] + n[:, lane + 5 : lane + 6] for n in notes]
            top = functools.reduce(jnp.maximum, tops)
            numerator, denominator = 0.0, 0.0
            for share, amount, piece in zip([jnp.exp(t - top) for t in tops], sums, pieces):
                numerator += share * piece[at].astype(F32)
                denominator += share * amount
            lines = numerator / denominator
            for g in range(GROUP):
                start = ((2 * at + core) * GROUP + g) * LANES
                out_ref[:, start : start + LANES] = lines[g * ROWS : (g + 1) * ROWS].astype(BF16)


def combine(parts):
    return pl.pallas_call(
        combine_kernel, out_shape=jax.ShapeDtypeStruct((ROWS, QW), BF16), in_specs=[VMEM], out_specs=VMEM,
        compiler_params=vmem(8),
    )(parts)


NEXT_Z = (1, 3, 0, 2)


def exchange(values, bits):
    return lax.ppermute(values, "ctx", [(i, i ^ bits) for i in range(2 * CHIPS)])


def round_z(values, steps=1):
    ring = []
    for i in range(2 * CHIPS):
        z = i // 4
        for _ in range(steps):
            z = NEXT_Z[z]
        ring.append((i, 4 * z + i % 4))
    return lax.ppermute(values, "ctx", ring)


def local(context, counts, queries, norm_gain, w_query, w_key, w_value, w_out, final_gain, w_kv):
    weights = (w_query, w_key, w_value, w_out, rotary_lanes(), norm_gain, final_gain)
    load0 = w_kv
    load1, beside0, taken = round_z(load0), exchange(load0, 2), exchange(context, 1)
    rows0 = prepare(queries)
    rows1 = round_z(rows0)
    half = first_half(context, weights)
    load1, beside0, taken, half, rows0, rows1 = lax.optimization_barrier((load1, beside0, taken, half, rows0, rows1))
    load2, beside1 = round_z(load1), exchange(load1, 2)
    rows2, rows3 = round_z(rows0, 2), round_z(rows0, 3)
    token0 = second_half(context, half, weights)
    load2, beside1, token0, rows2, rows3 = lax.optimization_barrier((load2, beside1, token0, rows2, rows3))
    load3, beside2, far0 = round_z(load2), exchange(load2, 2), exchange(token0, 1)
    near = stack(rows0, rows1, rows2, rows3)
    side, far = exchange(near, 2), exchange(near, 1)
    token12 = encode((1, 2), counts, context, taken, weights)
    load3, beside2, far0, token12, side, far = lax.optimization_barrier((load3, beside2, far0, token12, side, far))
    beside3, far12, far_side = exchange(load3, 2), exchange(token12, 1), exchange(side, 1)
    tokens = (token0, token12, far0, far12)
    parts, stats, rest, query = cross(
        counts, *tokens, load0, beside0, load1, beside1, load2, beside2, load3, near, far, side, far_side)
    parts = add_last_head(counts, tokens, beside3, rest, stats, query, parts)
    return combine(lax.all_to_all(parts, "ctx", 0, 0, tiled=True))


def rotary_tables(length, head_width):
    position = jnp.arange(length).astype(jnp.float32)[:, None]
    frequency = jnp.exp(
        jnp.arange(head_width // 2).astype(jnp.float32) * (-2.0 * math.log(10000.0) / head_width)
    )
    phase_angle = position * frequency[None, :]
    return (jnp.cos(phase_angle)[:, None, :], jnp.sin(phase_angle)[:, None, :])


def rotate(values, cosine_table, sine_table):
    half_width = values.shape[-1] // 2
    lower_half = values[..., :half_width]
    upper_half = values[..., half_width:]
    return jnp.concatenate(
        [
            lower_half * cosine_table - upper_half * sine_table,
            upper_half * cosine_table + lower_half * sine_table,
        ],
        axis=-1,
    )


def weighted_sums(cross_scores, top_scores, key_alive, cross_values):
    cross_weights = jnp.where(key_alive, jnp.exp(cross_scores - top_scores[..., None]), 0.0)
    total_rows = cross_scores.shape[0]
    denominator = jnp.sum(cross_weights, axis=-1).reshape(total_rows, Q_HEADS)
    numerator = jnp.einsum(
        "rkgt,tkd->rkgd",
        cross_weights.astype(jnp.bfloat16),
        cross_values,
        preferred_element_type=jnp.float32,
    )
    return (numerator.reshape(total_rows, QW), denominator)


def local_any(context, counts, queries, norm_gain, w_query, w_key, w_value, w_out, final_gain, w_kv):
    places = lax.axis_size("ctx")
    device_index = lax.axis_index("ctx")
    device_number = jnp.arange(places)
    own_count = jnp.sum(jnp.where(device_number == device_index, counts, 0))
    alive_slot = jnp.arange(CAP) < own_count
    slot_count = context.shape[0]
    row_count = slot_count * BLOCK
    normed = root_scale(context, norm_gain).astype(jnp.bfloat16).reshape(row_count, D_ENC)
    cosine_table, sine_table = rotary_tables(BLOCK, ENC_HD)

    def project(weight):
        return jnp.dot(normed, weight, preferred_element_type=jnp.float32).reshape(
            slot_count, BLOCK, ENC_HEADS, ENC_HD
        )

    query_rows = rotate(project(w_query), cosine_table, sine_table).astype(jnp.bfloat16)
    key_rows = rotate(project(w_key), cosine_table, sine_table).astype(jnp.bfloat16)
    value_rows = project(w_value).astype(jnp.bfloat16)
    scores = jnp.einsum(
        "sqhd,skhd->shqk", query_rows, key_rows, preferred_element_type=jnp.float32
    ) / math.sqrt(ENC_HD)
    weights = jax.nn.softmax(scores, axis=-1).astype(jnp.bfloat16)
    mixed_rows = jnp.einsum(
        "shqk,skhd->sqhd", weights, value_rows, preferred_element_type=jnp.float32
    )
    mixed_rows = mixed_rows.astype(jnp.bfloat16).reshape(row_count, D_ENC)
    residual = context.reshape(row_count, D_ENC).astype(jnp.float32) + jnp.dot(
        mixed_rows, w_out, preferred_element_type=jnp.float32
    )
    final_norm = root_scale(residual, final_gain).astype(jnp.bfloat16)
    key_value = jnp.dot(
        final_norm,
        lax.all_gather(w_kv, "ctx", axis=1, tiled=True),
        preferred_element_type=jnp.float32,
    ).astype(jnp.bfloat16)
    cross_keys = key_value[:, : KV_HEADS * HEAD_DIM].reshape(row_count, KV_HEADS, HEAD_DIM)
    cross_values = key_value[:, KV_HEADS * HEAD_DIM :].reshape(row_count, KV_HEADS, HEAD_DIM)
    every_query = lax.all_gather(queries, "ctx", axis=0, tiled=True)
    total_rows = every_query.shape[0]
    grouped = every_query.reshape(total_rows, KV_HEADS, GROUP, HEAD_DIM)
    cross_scores = jnp.einsum(
        "rkgd,tkd->rkgt", grouped, cross_keys, preferred_element_type=jnp.float32
    ) / math.sqrt(HEAD_DIM)
    key_alive = jnp.repeat(alive_slot, BLOCK)
    local_top = jnp.max(jnp.where(key_alive, cross_scores, -jnp.inf), axis=-1)
    row_top = lax.pmax(local_top.astype(jnp.bfloat16), "ctx").astype(local_top.dtype)
    numerator, denominator = weighted_sums(cross_scores, row_top, key_alive, cross_values)
    own_numerator, own_denominator = (
        lax.psum_scatter(numerator, "ctx", scatter_dimension=0, tiled=True),
        lax.psum_scatter(denominator, "ctx", scatter_dimension=0, tiled=True),
    )
    own_rows = own_numerator.shape[0]
    result = own_numerator.reshape(own_rows, Q_HEADS, HEAD_DIM) / own_denominator[..., None]
    return result.reshape(own_rows, QW).astype(jnp.bfloat16)


def solution(mesh):
    in_specs = (
        P(("groups", "ctx"), None, None),
        P("groups"),
        P(("groups", "ctx"), None),
        P(),
        P(),
        P(),
        P(),
        P(),
        P(),
        P(None, "ctx"),
    )
    out_specs = P(("groups", "ctx"), None)
    small = mesh.shape["ctx"] == 2 * CHIPS
    return jax.shard_map(local if small else local_any, mesh=mesh, in_specs=in_specs, out_specs=out_specs, check_vma=False)
```

```python
import functools
import math

import jax
import jax.numpy as jnp
import numpy as np
from jax import lax
from jax.experimental import pallas as pl
from jax.experimental.pallas import tpu as pltpu
from jax.sharding import PartitionSpec as P

D_ENC = 1024
ENC_HEADS = 16
ENC_HD = 64
BLOCK = 256
KV_HEADS = 8
HEAD_DIM = 128
Q_HEADS = 32
GROUP = 4
QW = 4096
CAP = 3
HALF_HEADS = KV_HEADS // 2
LANES = 128
CHIPS = 8
ROWS = 4
LINES = ROWS * GROUP
F32 = jnp.float32
BF16 = jnp.bfloat16
VMEM = pl.BlockSpec(memory_space=pltpu.VMEM)
SMEM = pl.BlockSpec(memory_space=pltpu.SMEM)
HBM = pl.BlockSpec(memory_space=pltpu.HBM)
ANY = pl.BlockSpec(memory_space=pl.ANY)
PARTS = 4
PART = D_ENC // PARTS
QUERY_LINES = KV_HEADS * LINES
HALF_LOAD = (D_ENC + QUERY_LINES) // 2


def root_scale(values, gain):
    values = values.astype(F32)
    return (
        values
        * lax.rsqrt(jnp.mean(values * values, axis=-1, keepdims=True) + 1e-05)
        * gain.astype(F32)
    )


def rotary_lanes():
    position = np.arange(BLOCK, dtype=np.float64)[:, None]
    frequency = 10000.0 ** (-2.0 * np.arange(ENC_HD // 2) / ENC_HD)
    angle = position * frequency[None, :]
    cosine, sine = np.cos(angle), np.sin(angle)
    return jnp.asarray(np.stack([
        np.concatenate([cosine, cosine, cosine, cosine], axis=1),
        np.concatenate([-sine, sine, -sine, sine], axis=1),
    ]), F32)


def live_counts(counts_ref):
    me = lax.axis_index("ctx")
    own, other = counts_ref[me], counts_ref[me + 1 - 2 * lax.rem(me, 2)]
    gives = jnp.where((own == 3) & (other == 1), 1, 0)
    takes = jnp.where((own == 1) & (other == 3), 1, 0)
    return own - gives + takes, other + gives - takes, takes


def prepare_kernel(w_kv_ref, query_ref, out_ref, query_buf, sems):
    copies = [
        pltpu.make_async_copy(query_ref, query_buf, sems.at[0]),
        pltpu.make_async_copy(w_kv_ref, out_ref.at[pl.ds(0, D_ENC), :], sems.at[1]),
    ]
    for copy in copies:
        copy.start()
    copies[0].wait()
    rows = query_buf[...].astype(F32)
    for head in range(KV_HEADS):
        first = head * GROUP
        out_ref[D_ENC + head * LINES : D_ENC + (head + 1) * LINES, :] = jnp.concatenate(
            [rows[:, (first + g) * LANES : (first + g + 1) * LANES] for g in range(GROUP)], axis=0
        ).astype(BF16)
    copies[1].wait()


def prepare(w_kv, queries):
    return pl.pallas_call(
        prepare_kernel,
        out_shape=jax.ShapeDtypeStruct((D_ENC + QUERY_LINES, LANES), BF16),
        in_specs=[HBM] * 2, out_specs=VMEM,
        scratch_shapes=[pltpu.VMEM((ROWS, QW), BF16), pltpu.SemaphoreType.DMA((2,))],
        compiler_params=vmem(63),
    )(w_kv, queries)


def copy_all(pairs, sems):
    copies = [pltpu.make_async_copy(source, target, sems.at[at]) for at, (source, target) in enumerate(pairs)]
    for copy in copies:
        copy.start()
    for copy in copies:
        copy.wait()


def last_parts_kernel(*refs):
    loads, (rows_ref, upper_ref, lower_ref, across_ref, sems) = refs[:7], refs[7:]
    rows = [ref.at[pl.ds(D_ENC, QUERY_LINES), :] for ref in loads]
    copy_all([
        (loads[6].at[pl.ds(0, HALF_LOAD), :], upper_ref),
        (loads[5].at[pl.ds(HALF_LOAD, HALF_LOAD), :], lower_ref),
        (rows[5], across_ref),
    ] + [(row, rows_ref.at[at]) for at, row in enumerate(rows)], sems)


def last_parts(*loads):
    rows, upper, lower, across = pl.pallas_call(
        last_parts_kernel,
        out_shape=[
            jax.ShapeDtypeStruct((7, QUERY_LINES, LANES), BF16),
            jax.ShapeDtypeStruct((HALF_LOAD, LANES), BF16),
            jax.ShapeDtypeStruct((HALF_LOAD, LANES), BF16),
            jax.ShapeDtypeStruct((QUERY_LINES, LANES), BF16),
        ],
        in_specs=[ANY] * 7, out_specs=[ANY] * 4, scratch_shapes=[pltpu.SemaphoreType.DMA((10,))],
        compiler_params=vmem(8),
    )(*loads)
    shape = (HALF_HEADS, 2, LINES, LANES)
    return rows.reshape((7,) + shape), upper, lower, across.reshape(shape)


def project_block(x_ref, copies, table_buf, gain_ref, q_buf, k_buf, v_buf, q_ref, k_ref, v_ref):
    normed = root_scale(x_ref[...], gain_ref[...]).astype(BF16)
    for copy in copies[:2]:
        copy.wait()
    cosine, sine = table_buf[0], table_buf[1]
    lane = lax.broadcasted_iota(jnp.int32, (BLOCK, LANES), 1)
    lower = (lane % ENC_HD) < ENC_HD // 2

    def project(buf, to_ref, cosine, sine):
        for part in range(PARTS):
            values = jnp.dot(normed, buf[:, part * PART : (part + 1) * PART], preferred_element_type=F32)
            for at in range(PART // LANES):
                cut = values[:, at * LANES : (at + 1) * LANES]
                swapped = jnp.where(
                    lower, pltpu.roll(cut, LANES - ENC_HD // 2, 1), pltpu.roll(cut, ENC_HD // 2, 1))
                start = part * PART + at * LANES
                to_ref[:, start : start + LANES] = (cut * cosine + swapped * sine).astype(BF16)

    project(q_buf, q_ref, cosine * 0.125, sine * 0.125)
    for copy in copies[2:3]:
        copy.wait()
    project(k_buf, k_ref, cosine, sine)
    for copy in copies[3:4]:
        copy.wait()
    v_ref[...] = jnp.dot(normed, v_buf[...], preferred_element_type=F32).astype(BF16)


def attend_block(x_ref, copies, q_ref, k_ref, v_ref, o_buf, fgain_ref, mixed_ref, final_ref):
    first = lax.broadcasted_iota(jnp.int32, (BLOCK, LANES), 1) < ENC_HD
    for pair in range(ENC_HEADS // 2):
        cut = slice(pair * LANES, (pair + 1) * LANES)
        query, key, value = q_ref[:, cut], k_ref[:, cut], v_ref[:, cut]
        mixed = []
        for own in (first, jnp.logical_not(first)):
            scores = lax.dot_general(
                key, jnp.where(own, query, jnp.zeros_like(query)),
                (((1,), (1,)), ((), ())), preferred_element_type=F32)
            weights = jnp.exp(scores - jnp.max(scores, axis=0, keepdims=True))
            weights = (weights * (1.0 / jnp.sum(weights, axis=0, keepdims=True))).astype(BF16)
            mixed.append(lax.dot_general(
                weights, value, (((0,), (0,)), ((), ())), preferred_element_type=F32))
        mixed_ref[:, cut] = jnp.where(first, mixed[0], mixed[1]).astype(BF16)
    for copy in copies[4:]:
        copy.wait()
    residual = x_ref[...].astype(F32) + jnp.dot(mixed_ref[...], o_buf[...], preferred_element_type=F32)
    final_ref[...] = root_scale(residual, fgain_ref[...]).astype(BF16)


def first_half_kernel(context_ref, wq_ref, wk_ref, wv_ref, table_ref, gain_ref, out_ref,
                      x_ref, table_buf, q_buf, k_buf, v_buf, q_ref, k_ref, v_ref, sems):
    copies = [
        pltpu.make_async_copy(hbm, buf, sems.at[at])
        for at, (hbm, buf) in enumerate(
            ((context_ref.at[0], x_ref), (wq_ref, q_buf), (table_ref, table_buf), (wk_ref, k_buf), (wv_ref, v_buf)))
    ]
    for copy in copies:
        copy.start()
    copies[0].wait()
    project_block(x_ref, copies[1:], table_buf, gain_ref, q_buf, k_buf, v_buf, q_ref, k_ref, v_ref)
    writes = [
        pltpu.make_async_copy(buf, out_ref.at[at], sems.at[5 + at]) for at, buf in enumerate((q_ref, k_ref, v_ref))]
    for copy in writes:
        copy.start()
    for copy in writes:
        copy.wait()


def second_half_kernel(context_ref, half_ref, wo_ref, fgain_ref, out_ref,
                       x_ref, o_buf, q_ref, k_ref, v_ref, mixed_ref, final_ref, sems):
    copies = [
        pltpu.make_async_copy(hbm, buf, sems.at[at])
        for at, (hbm, buf) in enumerate(
            ((half_ref.at[0], q_ref), (half_ref.at[1], k_ref), (half_ref.at[2], v_ref), (context_ref.at[0], x_ref),
             (wo_ref, o_buf)))
    ]
    for copy in copies:
        copy.start()
    for copy in copies[:4]:
        copy.wait()
    attend_block(x_ref, copies, q_ref, k_ref, v_ref, o_buf, fgain_ref, mixed_ref, final_ref)
    copy = pltpu.make_async_copy(final_ref, out_ref.at[0], sems.at[5])
    copy.start()
    copy.wait()


def encoder_kernel(first_slot, slots, counts_ref, context_ref, taken_ref, wq_ref, wk_ref, wv_ref, wo_ref, table_ref,
                   gain_ref, fgain_ref, out_ref, mixed_ref, x_buf, q_ref, k_ref, v_ref, final_buf, table_buf,
                   q_buf, k_buf, v_buf, o_buf, sems, x_sems, out_sems):
    live, _, takes = live_counts(counts_ref)
    copies = [
        pltpu.make_async_copy(hbm, buf, sems.at[at])
        for at, (hbm, buf) in enumerate(
            ((wq_ref, q_buf), (table_ref, table_buf), (wk_ref, k_buf), (wv_ref, v_buf), (wo_ref, o_buf)))
    ]

    def read(slot):
        at = slot - first_slot
        return pltpu.make_async_copy(context_ref.at[slot], x_buf.at[at], x_sems.at[at])

    def write(slot):
        at = slot - first_slot
        return pltpu.make_async_copy(final_buf.at[at], out_ref.at[at], out_sems.at[at])

    @pl.when(live > first_slot)
    def _():
        if first_slot == 1:
            @pl.when(takes != 0)
            def _():
                pltpu.make_async_copy(taken_ref.at[CAP - 1], x_buf.at[0], x_sems.at[0]).start()

            @pl.when(takes == 0)
            def _():
                read(1).start()
        else:
            read(first_slot).start()
        for copy in copies:
            copy.start()

    for slot in slots[1:]:
        @pl.when(live > slot)
        def _():
            read(slot).start()

    for slot in slots:
        @pl.when(live > slot)
        def _():
            at = slot - first_slot
            pending = copies if slot == first_slot else []
            read(slot).wait()
            project_block(
                x_buf.at[at], pending, table_buf, gain_ref, q_buf, k_buf, v_buf, q_ref, k_ref, v_ref)
            attend_block(
                x_buf.at[at], pending, q_ref, k_ref, v_ref, o_buf, fgain_ref, mixed_ref, final_buf.at[at])
            write(slot).start()

    for slot in slots:
        @pl.when(live > slot)
        def _():
            write(slot).wait()


SQUARE, WHOLE = pltpu.VMEM((D_ENC, D_ENC), BF16), pltpu.VMEM((BLOCK, D_ENC), BF16)
TABLES = pltpu.VMEM((2, BLOCK, LANES), F32)


def vmem(mebibytes):
    return pltpu.CompilerParams(vmem_limit_bytes=mebibytes * 2**20)


def cost(flops):
    return pl.CostEstimate(flops=flops, bytes_accessed=9 * 2**20, transcendentals=2**20)


def encode(slots, counts, context, taken, weights):
    blocks = pltpu.VMEM((len(slots), BLOCK, D_ENC), BF16)
    return pl.pallas_call(
        functools.partial(encoder_kernel, slots[0], slots),
        out_shape=jax.ShapeDtypeStruct((len(slots), BLOCK, D_ENC), BF16),
        in_specs=[SMEM] + [HBM] * 7 + [VMEM] * 2,
        out_specs=HBM,
        scratch_shapes=[WHOLE, blocks, WHOLE, WHOLE, WHOLE, blocks, TABLES] + [SQUARE] * 4
        + [pltpu.SemaphoreType.DMA((5,)), pltpu.SemaphoreType.DMA((2,)), pltpu.SemaphoreType.DMA((2,))],
        compiler_params=vmem(63), cost_estimate=cost(9 * 10**9),
    )(counts, context, taken, *weights)


def first_half(context, weights):
    w_query, w_key, w_value, _, tables, gain, _ = weights
    return pl.pallas_call(
        first_half_kernel,
        out_shape=jax.ShapeDtypeStruct((3, BLOCK, D_ENC), BF16),
        in_specs=[HBM] * 5 + [VMEM],
        out_specs=HBM,
        scratch_shapes=[WHOLE, TABLES] + [SQUARE] * 3 + [WHOLE] * 3 + [pltpu.SemaphoreType.DMA((8,))],
        compiler_params=vmem(63), cost_estimate=cost(5 * 10**9),
    )(context, w_query, w_key, w_value, tables, gain)


def second_half(context, half, weights):
    return pl.pallas_call(
        second_half_kernel,
        out_shape=jax.ShapeDtypeStruct((1, BLOCK, D_ENC), BF16),
        in_specs=[HBM] * 3 + [VMEM],
        out_specs=HBM,
        scratch_shapes=[WHOLE, SQUARE] + [WHOLE] * 5 + [pltpu.SemaphoreType.DMA((6,))],
        compiler_params=vmem(63), cost_estimate=cost(5 * 10**9),
    )(context, half, weights[3], weights[6])


def three_parts(values):
    high = values.astype(BF16).astype(F32)
    middle = (values - high).astype(BF16).astype(F32)
    return high, middle, values - high - middle


def ring_chips(me):
    z, y = me // 4, lax.rem(me // 2, 2)
    place = jnp.where(z == 3, 2, jnp.where(z == 2, 3, z))
    chips = []
    for step in range(CHIPS // 2):
        at = lax.rem(place + 4 - step, 4)
        z = jnp.where(at == 2, 3, jnp.where(at == 3, 2, at))
        chips.append((2 * z + y, 2 * z + 1 - y))
    return chips


def cross_kernel(counts_ref, *refs):
    token0, token12, far0, far12 = refs[:4]
    loads, (upper_ref, lower_ref, near_ref, far_ref, across_ref) = refs[4:11], refs[11:16]
    out_ref, token_buf, weight_buf, query_buf, score_ref, value_ref, total_ref, top_ref, sum_ref = refs[16:25]
    sems, token_sems, row_sems = refs[25:]
    tokens = (token0.at[0], token12.at[0], token12.at[1], far0.at[0], far12.at[0], far12.at[1])
    me = lax.axis_index("ctx")
    core = lax.rem(me, 2)
    own_live, other_live, _ = live_counts(counts_ref)
    chips = [chip for pair in ring_chips(me) for chip in pair]
    columns = [pl.ds(pl.multiple_of(chip * LANES, LANES), LANES) for chip in chips]
    copies = [
        pltpu.make_async_copy(load.at[pl.ds(0, D_ENC), :], weight_buf.at[:, columns[at]], sems.at[at])
        for at, load in enumerate(loads)
    ]
    rest = D_ENC - HALF_LOAD
    copies.append(pltpu.make_async_copy(
        upper_ref, weight_buf.at[pl.ds(0, HALF_LOAD), columns[CHIPS - 1]], sems.at[CHIPS - 1]))
    copies.append(pltpu.make_async_copy(
        lower_ref.at[pl.ds(0, rest), :], weight_buf.at[pl.ds(HALF_LOAD, rest), columns[CHIPS - 1]], sems.at[CHIPS]))

    def fetch(at, part, source, heads):
        start = pl.multiple_of((2 * chips[at] + part) * LINES, LINES)
        copies.append(pltpu.make_async_copy(
            source, query_buf.at[heads, pl.ds(start, LINES), :], row_sems.at[len(copies) - CHIPS - 1]))

    every = slice(0, HALF_HEADS)
    for at in range(CHIPS - 1):
        fetch(at, core, near_ref.at[at, :, core], every)
        fetch(at, 1 - core, far_ref.at[at, :, core], every)
    fetch(CHIPS - 1, 1 - core, across_ref.at[:, core], every)
    for head in range(HALF_HEADS):
        start = pl.multiple_of(rest + (2 * head + core) * LINES, LINES)
        fetch(CHIPS - 1, core, lower_ref.at[pl.ds(start, LINES), :], head)

    def token_copy(at):
        return pltpu.make_async_copy(tokens[at], token_buf.at[at], token_sems.at[at])

    def live(at):
        return (own_live > at) if at < CAP else (other_live > at - CAP)

    for copy in copies:
        copy.start()
    for at in range(2 * CAP):
        @pl.when(live(at))
        def _():
            token_copy(at).start()
    total_ref[...] = jnp.zeros_like(total_ref)
    sum_ref[...] = jnp.zeros_like(sum_ref)
    top_ref[...] = jnp.full_like(top_ref, -jnp.inf)
    for copy in copies:
        copy.wait()

    for at in range(2 * CAP):
        @pl.when(live(at))
        def _():
            token_copy(at).wait()
            both = jnp.dot(token_buf[at], weight_buf[...], preferred_element_type=F32).astype(BF16)
            value_ref[at] = both[:, HALF_HEADS * LANES :]
            for head in range(HALF_HEADS):
                scores = lax.dot_general(
                    both[:, head * LANES : (head + 1) * LANES], query_buf[head],
                    (((1,), (1,)), ((), ())), preferred_element_type=F32,
                ) * (1.0 / math.sqrt(HEAD_DIM))
                score_ref[at, head] = scores
                top_ref[head] = jnp.maximum(top_ref[head], jnp.max(scores, axis=0, keepdims=True))

    for at in range(2 * CAP):
        @pl.when(live(at))
        def _():
            for head in range(HALF_HEADS):
                weights = jnp.exp(score_ref[at, head] - top_ref[head])
                sum_ref[head] += jnp.sum(weights, axis=0, keepdims=True)
                total_ref[head] += lax.dot_general(
                    weights.astype(BF16), value_ref[at, :, head * LANES : (head + 1) * LANES],
                    (((0,), (0,)), ((), ())), preferred_element_type=F32)

    lines = total_ref.shape[1]
    notes = []
    for head in range(HALF_HEADS):
        notes += list(three_parts(top_ref[head])) + list(three_parts(sum_ref[head]))
        out_ref[:, head] = total_ref[head].astype(BF16).reshape(2 * CHIPS, LINES, LANES)
    notes = jnp.concatenate(notes + [jnp.zeros((LANES - len(notes), lines), F32)], axis=0).T
    out_ref[:, HALF_HEADS] = notes.astype(BF16).reshape(2 * CHIPS, LINES, LANES)


def cross(counts, *arrays):
    lines = 2 * CHIPS * LINES
    line = pltpu.VMEM((HALF_HEADS, 1, lines), F32)
    return pl.pallas_call(
        cross_kernel,
        out_shape=jax.ShapeDtypeStruct((2 * CHIPS, HALF_HEADS + 1, LINES, LANES), BF16),
        in_specs=[SMEM] + [HBM] * 16,
        out_specs=VMEM,
        scratch_shapes=[
            pltpu.VMEM((2 * CAP, BLOCK, D_ENC), BF16),
            pltpu.VMEM((D_ENC, KV_HEADS * LANES), BF16),
            pltpu.VMEM((HALF_HEADS, lines, LANES), BF16),
            pltpu.VMEM((2 * CAP, HALF_HEADS, BLOCK, lines), F32),
            pltpu.VMEM((2 * CAP, BLOCK, HALF_HEADS * LANES), BF16),
            pltpu.VMEM((HALF_HEADS, lines, LANES), F32),
            line, line,
            pltpu.SemaphoreType.DMA((CHIPS + 1,)), pltpu.SemaphoreType.DMA((2 * CAP,)), pltpu.SemaphoreType.DMA((19,)),
        ],
        compiler_params=vmem(63),
        cost_estimate=pl.CostEstimate(flops=6 * 10**9, bytes_accessed=8 * 2**20, transcendentals=2**20),
    )(counts, *arrays)


def combine_kernel(parts_ref, out_ref):
    for core in range(2):
        pieces = [parts_ref.at[2 * chip + core] for chip in range(CHIPS)]
        notes = [piece[HALF_HEADS].astype(F32) for piece in pieces]
        for at in range(HALF_HEADS):
            lane = 6 * at
            tops = [n[:, lane : lane + 1] + n[:, lane + 1 : lane + 2] + n[:, lane + 2 : lane + 3] for n in notes]
            sums = [n[:, lane + 3 : lane + 4] + n[:, lane + 4 : lane + 5] + n[:, lane + 5 : lane + 6] for n in notes]
            top = functools.reduce(jnp.maximum, tops)
            numerator, denominator = 0.0, 0.0
            for share, amount, piece in zip([jnp.exp(t - top) for t in tops], sums, pieces):
                numerator += share * piece[at].astype(F32)
                denominator += share * amount
            lines = numerator / denominator
            for g in range(GROUP):
                start = ((2 * at + core) * GROUP + g) * LANES
                out_ref[:, start : start + LANES] = lines[g * ROWS : (g + 1) * ROWS].astype(BF16)


def combine(parts):
    return pl.pallas_call(
        combine_kernel, out_shape=jax.ShapeDtypeStruct((ROWS, QW), BF16), in_specs=[VMEM], out_specs=VMEM,
        compiler_params=vmem(8),
    )(parts)


NEXT_Z = (1, 3, 0, 2)


def exchange(values, bits):
    return lax.ppermute(values, "ctx", [(i, i ^ bits) for i in range(2 * CHIPS)])


def round_z(values, bits=0):
    return lax.ppermute(values, "ctx", [(i, (4 * NEXT_Z[i // 4] + i % 4) ^ bits) for i in range(2 * CHIPS)])


def local(context, counts, queries, norm_gain, w_query, w_key, w_value, w_out, final_gain, w_kv):
    weights = (w_query, w_key, w_value, w_out, rotary_lanes(), norm_gain, final_gain)
    load0 = prepare(w_kv, queries)
    load1, beside0, taken = round_z(load0), exchange(load0, 2), exchange(context, 1)
    half = first_half(context, weights)
    load1, beside0, taken, half = lax.optimization_barrier((load1, beside0, taken, half))
    load2, beside1 = round_z(load1), exchange(load1, 2)
    token0 = second_half(context, half, weights)
    load2, beside1, token0 = lax.optimization_barrier((load2, beside1, token0))
    load3, beside2, far0 = round_z(load2), exchange(load2, 2), exchange(token0, 1)
    token12 = encode((1, 2), counts, context, taken, weights)
    load3, beside2, far0, token12 = lax.optimization_barrier((load3, beside2, far0, token12))
    rows, upper, lower, across = last_parts(load0, beside0, load1, beside1, load2, beside2, load3)
    upper, lower, across, far_rows = exchange(upper, 2), round_z(lower), round_z(across, 1), exchange(rows, 1)
    far12 = exchange(token12, 1)
    parts = cross(
        counts, token0, token12, far0, far12, load0, beside0, load1, beside1, load2, beside2, load3,
        upper, lower, rows, far_rows, across)
    return combine(lax.all_to_all(parts, "ctx", 0, 0, tiled=True))


def rotary_tables(length, head_width):
    position = jnp.arange(length).astype(jnp.float32)[:, None]
    frequency = jnp.exp(
        jnp.arange(head_width // 2).astype(jnp.float32) * (-2.0 * math.log(10000.0) / head_width)
    )
    phase_angle = position * frequency[None, :]
    return (jnp.cos(phase_angle)[:, None, :], jnp.sin(phase_angle)[:, None, :])


def rotate(values, cosine_table, sine_table):
    half_width = values.shape[-1] // 2
    lower_half = values[..., :half_width]
    upper_half = values[..., half_width:]
    return jnp.concatenate(
        [
            lower_half * cosine_table - upper_half * sine_table,
            upper_half * cosine_table + lower_half * sine_table,
        ],
        axis=-1,
    )


def weighted_sums(cross_scores, top_scores, key_alive, cross_values):
    cross_weights = jnp.where(key_alive, jnp.exp(cross_scores - top_scores[..., None]), 0.0)
    total_rows = cross_scores.shape[0]
    denominator = jnp.sum(cross_weights, axis=-1).reshape(total_rows, Q_HEADS)
    numerator = jnp.einsum(
        "rkgt,tkd->rkgd",
        cross_weights.astype(jnp.bfloat16),
        cross_values,
        preferred_element_type=jnp.float32,
    )
    return (numerator.reshape(total_rows, QW), denominator)


def local_any(context, counts, queries, norm_gain, w_query, w_key, w_value, w_out, final_gain, w_kv):
    places = lax.axis_size("ctx")
    device_index = lax.axis_index("ctx")
    device_number = jnp.arange(places)
    own_count = jnp.sum(jnp.where(device_number == device_index, counts, 0))
    alive_slot = jnp.arange(CAP) < own_count
    slot_count = context.shape[0]
    row_count = slot_count * BLOCK
    normed = root_scale(context, norm_gain).astype(jnp.bfloat16).reshape(row_count, D_ENC)
    cosine_table, sine_table = rotary_tables(BLOCK, ENC_HD)

    def project(weight):
        return jnp.dot(normed, weight, preferred_element_type=jnp.float32).reshape(
            slot_count, BLOCK, ENC_HEADS, ENC_HD
        )

    query_rows = rotate(project(w_query), cosine_table, sine_table).astype(jnp.bfloat16)
    key_rows = rotate(project(w_key), cosine_table, sine_table).astype(jnp.bfloat16)
    value_rows = project(w_value).astype(jnp.bfloat16)
    scores = jnp.einsum(
        "sqhd,skhd->shqk", query_rows, key_rows, preferred_element_type=jnp.float32
    ) / math.sqrt(ENC_HD)
    weights = jax.nn.softmax(scores, axis=-1).astype(jnp.bfloat16)
    mixed_rows = jnp.einsum(
        "shqk,skhd->sqhd", weights, value_rows, preferred_element_type=jnp.float32
    )
    mixed_rows = mixed_rows.astype(jnp.bfloat16).reshape(row_count, D_ENC)
    residual = context.reshape(row_count, D_ENC).astype(jnp.float32) + jnp.dot(
        mixed_rows, w_out, preferred_element_type=jnp.float32
    )
    final_norm = root_scale(residual, final_gain).astype(jnp.bfloat16)
    key_value = jnp.dot(
        final_norm,
        lax.all_gather(w_kv, "ctx", axis=1, tiled=True),
        preferred_element_type=jnp.float32,
    ).astype(jnp.bfloat16)
    cross_keys = key_value[:, : KV_HEADS * HEAD_DIM].reshape(row_count, KV_HEADS, HEAD_DIM)
    cross_values = key_value[:, KV_HEADS * HEAD_DIM :].reshape(row_count, KV_HEADS, HEAD_DIM)
    every_query = lax.all_gather(queries, "ctx", axis=0, tiled=True)
    total_rows = every_query.shape[0]
    grouped = every_query.reshape(total_rows, KV_HEADS, GROUP, HEAD_DIM)
    cross_scores = jnp.einsum(
        "rkgd,tkd->rkgt", grouped, cross_keys, preferred_element_type=jnp.float32
    ) / math.sqrt(HEAD_DIM)
    key_alive = jnp.repeat(alive_slot, BLOCK)
    local_top = jnp.max(jnp.where(key_alive, cross_scores, -jnp.inf), axis=-1)
    row_top = lax.pmax(local_top.astype(jnp.bfloat16), "ctx").astype(local_top.dtype)
    numerator, denominator = weighted_sums(cross_scores, row_top, key_alive, cross_values)
    own_numerator, own_denominator = (
        lax.psum_scatter(numerator, "ctx", scatter_dimension=0, tiled=True),
        lax.psum_scatter(denominator, "ctx", scatter_dimension=0, tiled=True),
    )
    own_rows = own_numerator.shape[0]
    result = own_numerator.reshape(own_rows, Q_HEADS, HEAD_DIM) / own_denominator[..., None]
    return result.reshape(own_rows, QW).astype(jnp.bfloat16)


def solution(mesh):
    in_specs = (
        P(("groups", "ctx"), None, None),
        P("groups"),
        P(("groups", "ctx"), None),
        P(),
        P(),
        P(),
        P(),
        P(),
        P(),
        P(None, "ctx"),
    )
    out_specs = P(("groups", "ctx"), None)
    small = mesh.shape["ctx"] == 2 * CHIPS
    return jax.shard_map(local if small else local_any, mesh=mesh, in_specs=in_specs, out_specs=out_specs, check_vma=False)
```

```python
import functools
import math

import jax
import jax.numpy as jnp
import numpy as np
from jax import lax
from jax.experimental import pallas as pl
from jax.experimental.pallas import tpu as pltpu
from jax.sharding import PartitionSpec as P

D_ENC = 1024
ENC_HEADS = 16
ENC_HD = 64
BLOCK = 256
KV_HEADS = 8
HEAD_DIM = 128
Q_HEADS = 32
GROUP = 4
QW = 4096
CAP = 3
HALF_HEADS = KV_HEADS // 2
LANES = 128
CHIPS = 8
ROWS = 4
LINES = ROWS * GROUP
F32 = jnp.float32
BF16 = jnp.bfloat16
VMEM = pl.BlockSpec(memory_space=pltpu.VMEM)
SMEM = pl.BlockSpec(memory_space=pltpu.SMEM)
HBM = pl.BlockSpec(memory_space=pltpu.HBM)
ANY = pl.BlockSpec(memory_space=pl.ANY)
PARTS = 4
PART = D_ENC // PARTS
QUERY_LINES = KV_HEADS * LINES
HALF_LOAD = (D_ENC + QUERY_LINES) // 2


def root_scale(values, gain):
    values = values.astype(F32)
    return (
        values
        * lax.rsqrt(jnp.mean(values * values, axis=-1, keepdims=True) + 1e-05)
        * gain.astype(F32)
    )


def rotary_lanes():
    position = np.arange(BLOCK, dtype=np.float64)[:, None]
    frequency = 10000.0 ** (-2.0 * np.arange(ENC_HD // 2) / ENC_HD)
    angle = position * frequency[None, :]
    cosine, sine = np.cos(angle), np.sin(angle)
    return jnp.asarray(np.stack([
        np.concatenate([cosine, cosine, cosine, cosine], axis=1),
        np.concatenate([-sine, sine, -sine, sine], axis=1),
    ]), F32)


def live_counts(counts_ref):
    me = lax.axis_index("ctx")
    own, other = counts_ref[me], counts_ref[me + 1 - 2 * lax.rem(me, 2)]
    gives = jnp.where((own == 3) & (other == 1), 1, 0)
    takes = jnp.where((own == 1) & (other == 3), 1, 0)
    return own - gives + takes, other + gives - takes, takes


def prepare_kernel(w_kv_ref, query_ref, out_ref, query_buf, sems):
    copies = [
        pltpu.make_async_copy(query_ref, query_buf, sems.at[0]),
        pltpu.make_async_copy(w_kv_ref, out_ref.at[pl.ds(0, D_ENC), :], sems.at[1]),
    ]
    for copy in copies:
        copy.start()
    copies[0].wait()
    rows = query_buf[...].astype(F32)
    for head in range(KV_HEADS):
        first = head * GROUP
        out_ref[D_ENC + head * LINES : D_ENC + (head + 1) * LINES, :] = jnp.concatenate(
            [rows[:, (first + g) * LANES : (first + g + 1) * LANES] for g in range(GROUP)], axis=0
        ).astype(BF16)
    copies[1].wait()


def prepare(w_kv, queries):
    return pl.pallas_call(
        prepare_kernel,
        out_shape=jax.ShapeDtypeStruct((D_ENC + QUERY_LINES, LANES), BF16),
        in_specs=[HBM] * 2, out_specs=VMEM,
        scratch_shapes=[pltpu.VMEM((ROWS, QW), BF16), pltpu.SemaphoreType.DMA((2,))],
        compiler_params=vmem(63),
    )(w_kv, queries)


def copy_all(pairs, sems):
    copies = [pltpu.make_async_copy(source, target, sems.at[at]) for at, (source, target) in enumerate(pairs)]
    for copy in copies:
        copy.start()
    for copy in copies:
        copy.wait()


def last_parts_kernel(*refs):
    loads, (rows_ref, upper_ref, lower_ref, across_ref, sems) = refs[:7], refs[7:]
    rows = [ref.at[pl.ds(D_ENC, QUERY_LINES), :] for ref in loads]
    copy_all([
        (loads[6].at[pl.ds(0, HALF_LOAD), :], upper_ref),
        (loads[5].at[pl.ds(HALF_LOAD, HALF_LOAD), :], lower_ref),
        (rows[5], across_ref),
    ] + [(row, rows_ref.at[at]) for at, row in enumerate(rows)], sems)


def last_parts(*loads):
    rows, upper, lower, across = pl.pallas_call(
        last_parts_kernel,
        out_shape=[
            jax.ShapeDtypeStruct((7, QUERY_LINES, LANES), BF16),
            jax.ShapeDtypeStruct((HALF_LOAD, LANES), BF16),
            jax.ShapeDtypeStruct((HALF_LOAD, LANES), BF16),
            jax.ShapeDtypeStruct((QUERY_LINES, LANES), BF16),
        ],
        in_specs=[ANY] * 7, out_specs=[ANY] * 4, scratch_shapes=[pltpu.SemaphoreType.DMA((10,))],
        compiler_params=vmem(8),
    )(*loads)
    shape = (HALF_HEADS, 2, LINES, LANES)
    return rows.reshape((7,) + shape), upper, lower, across.reshape(shape)


def start_read(slot, context_ref, taken_ref, takes, x_ref, sem):
    if slot == 1:
        @pl.when(takes != 0)
        def _():
            pltpu.make_async_copy(taken_ref.at[CAP - 1], x_ref, sem).start()

        @pl.when(takes == 0)
        def _():
            pltpu.make_async_copy(context_ref.at[slot], x_ref, sem).start()
    else:
        pltpu.make_async_copy(context_ref.at[slot], x_ref, sem).start()


def project_rotated(normed, copies, table_buf, q_buf, k_buf, q_ref, k_ref):
    for copy in copies[:2]:
        copy.wait()
    cosine, sine = table_buf[0], table_buf[1]
    lane = lax.broadcasted_iota(jnp.int32, (BLOCK, LANES), 1)
    lower = (lane % ENC_HD) < ENC_HD // 2

    def project(buf, to_ref, cosine, sine):
        for part in range(PARTS):
            values = jnp.dot(normed, buf[:, part * PART : (part + 1) * PART], preferred_element_type=F32)
            for at in range(PART // LANES):
                cut = values[:, at * LANES : (at + 1) * LANES]
                swapped = jnp.where(
                    lower, pltpu.roll(cut, LANES - ENC_HD // 2, 1), pltpu.roll(cut, ENC_HD // 2, 1))
                start = part * PART + at * LANES
                to_ref[:, start : start + LANES] = (cut * cosine + swapped * sine).astype(BF16)

    project(q_buf, q_ref, cosine * 0.125, sine * 0.125)
    copies[2].wait()
    project(k_buf, k_ref, cosine, sine)


def attend_block(x_ref, copies, q_ref, k_ref, v_ref, o_buf, fgain_ref, mixed_ref, final_ref):
    first = lax.broadcasted_iota(jnp.int32, (BLOCK, LANES), 1) < ENC_HD
    for pair in range(ENC_HEADS // 2):
        cut = slice(pair * LANES, (pair + 1) * LANES)
        query, key, value = q_ref[:, cut], k_ref[:, cut], v_ref[:, cut]
        mixed = []
        for own in (first, jnp.logical_not(first)):
            scores = lax.dot_general(
                key, jnp.where(own, query, jnp.zeros_like(query)),
                (((1,), (1,)), ((), ())), preferred_element_type=F32)
            weights = jnp.exp(scores - jnp.max(scores, axis=0, keepdims=True))
            weights = (weights * (1.0 / jnp.sum(weights, axis=0, keepdims=True))).astype(BF16)
            mixed.append(lax.dot_general(
                weights, value, (((0,), (0,)), ((), ())), preferred_element_type=F32))
        mixed_ref[:, cut] = jnp.where(first, mixed[0], mixed[1]).astype(BF16)
    for copy in copies[4:]:
        copy.wait()
    residual = x_ref[...].astype(F32) + jnp.dot(mixed_ref[...], o_buf[...], preferred_element_type=F32)
    final_ref[...] = root_scale(residual, fgain_ref[...]).astype(BF16)


def first_half_kernel(context_ref, wq_ref, wk_ref, wv_ref, table_ref, gain_ref, out_ref,
                      x_ref, table_buf, q_buf, k_buf, v_buf, q_ref, k_ref, v_ref, sems):
    copies = [
        pltpu.make_async_copy(hbm, buf, sems.at[at])
        for at, (hbm, buf) in enumerate(
            ((context_ref.at[0], x_ref), (wq_ref, q_buf), (table_ref, table_buf), (wk_ref, k_buf), (wv_ref, v_buf)))
    ]
    for copy in copies:
        copy.start()
    copies[0].wait()
    normed = root_scale(x_ref[...], gain_ref[...]).astype(BF16)
    project_rotated(normed, copies[1:4], table_buf, q_buf, k_buf, q_ref, k_ref)
    copies[4].wait()
    v_ref[...] = jnp.dot(normed, v_buf[...], preferred_element_type=F32).astype(BF16)
    writes = [
        pltpu.make_async_copy(buf, out_ref.at[at], sems.at[5 + at]) for at, buf in enumerate((q_ref, k_ref, v_ref))]
    for copy in writes:
        copy.start()
    for copy in writes:
        copy.wait()


def second_half_kernel(counts_ref, context_ref, taken_ref, half_ref, wo_ref, wq_ref, wk_ref, table_ref, gain_ref,
                       fgain_ref, out_ref, next_ref, x_ref, o_buf, q_ref, k_ref, v_ref, mixed_ref, final_ref,
                       x_next, q_buf, k_buf, table_buf, q_next, k_next, sems):
    live, _, takes = live_counts(counts_ref)
    copies = [
        pltpu.make_async_copy(hbm, buf, sems.at[at])
        for at, (hbm, buf) in enumerate(
            ((half_ref.at[0], q_ref), (half_ref.at[1], k_ref), (half_ref.at[2], v_ref), (context_ref.at[0], x_ref),
             (wo_ref, o_buf)))
    ]
    ahead = [
        pltpu.make_async_copy(hbm, buf, sems.at[5 + at])
        for at, (hbm, buf) in enumerate(((wq_ref, q_buf), (table_ref, table_buf), (wk_ref, k_buf)))
    ]
    for copy in copies:
        copy.start()

    @pl.when(live > 1)
    def _():
        start_read(1, context_ref, taken_ref, takes, x_next, sems.at[8])
        for copy in ahead:
            copy.start()

    for copy in copies[:4]:
        copy.wait()
    attend_block(x_ref, copies, q_ref, k_ref, v_ref, o_buf, fgain_ref, mixed_ref, final_ref)
    write = pltpu.make_async_copy(final_ref, out_ref.at[0], sems.at[9])
    write.start()

    @pl.when(live > 1)
    def _():
        pltpu.make_async_copy(context_ref.at[1], x_next, sems.at[8]).wait()
        normed = root_scale(x_next[...], gain_ref[...]).astype(BF16)
        project_rotated(normed, ahead, table_buf, q_buf, k_buf, q_next, k_next)
        copy_all([(q_next, next_ref.at[0]), (k_next, next_ref.at[1])], sems)

    write.wait()


def encoder_kernel(counts_ref, context_ref, taken_ref, next_ref, wq_ref, wk_ref, wv_ref, wo_ref, table_ref,
                   gain_ref, fgain_ref, out_ref, mixed_ref, x_buf, q_ref, k_ref, v_ref, final_buf, table_buf,
                   q_buf, k_buf, v_buf, o_buf, sems, x_sems, out_sems):
    live, _, takes = live_counts(counts_ref)
    later = [
        pltpu.make_async_copy(hbm, buf, sems.at[at])
        for at, (hbm, buf) in enumerate(((wq_ref, q_buf), (table_ref, table_buf), (wk_ref, k_buf)))
    ]
    copies = [
        pltpu.make_async_copy(hbm, buf, sems.at[3 + at])
        for at, (hbm, buf) in enumerate(
            ((wv_ref, v_buf), (next_ref.at[0], q_ref), (next_ref.at[1], k_ref), (wo_ref, o_buf)))
    ]

    def write(at):
        return pltpu.make_async_copy(final_buf.at[at], out_ref.at[at], out_sems.at[at])

    @pl.when(live > 1)
    def _():
        start_read(1, context_ref, taken_ref, takes, x_buf.at[0], x_sems.at[0])
        for copy in copies:
            copy.start()

    @pl.when(live > 2)
    def _():
        start_read(2, context_ref, taken_ref, takes, x_buf.at[1], x_sems.at[1])
        for copy in later:
            copy.start()

    for at in range(2):
        @pl.when(live > 1 + at)
        def _():
            pltpu.make_async_copy(context_ref.at[1 + at], x_buf.at[at], x_sems.at[at]).wait()
            normed = root_scale(x_buf[at], gain_ref[...]).astype(BF16)
            if at == 0:
                copies[0].wait()
            else:
                project_rotated(normed, later, table_buf, q_buf, k_buf, q_ref, k_ref)
            v_ref[...] = jnp.dot(normed, v_buf[...], preferred_element_type=F32).astype(BF16)
            if at == 0:
                for copy in copies[1:3]:
                    copy.wait()
            attend_block(
                x_buf.at[at], [None] + copies if at == 0 else [], q_ref, k_ref, v_ref, o_buf, fgain_ref, mixed_ref,
                final_buf.at[at])
            write(at).start()

    for at in range(2):
        @pl.when(live > 1 + at)
        def _():
            write(at).wait()


SQUARE, WHOLE = pltpu.VMEM((D_ENC, D_ENC), BF16), pltpu.VMEM((BLOCK, D_ENC), BF16)
TABLES = pltpu.VMEM((2, BLOCK, LANES), F32)


def vmem(mebibytes):
    return pltpu.CompilerParams(vmem_limit_bytes=mebibytes * 2**20)


def cost(flops):
    return pl.CostEstimate(flops=flops, bytes_accessed=9 * 2**20, transcendentals=2**20)


def encode(counts, context, taken, ahead, weights):
    blocks = pltpu.VMEM((2, BLOCK, D_ENC), BF16)
    return pl.pallas_call(
        encoder_kernel,
        out_shape=jax.ShapeDtypeStruct((2, BLOCK, D_ENC), BF16),
        in_specs=[SMEM] + [HBM] * 8 + [VMEM] * 2,
        out_specs=HBM,
        scratch_shapes=[WHOLE, blocks, WHOLE, WHOLE, WHOLE, blocks, TABLES] + [SQUARE] * 4
        + [pltpu.SemaphoreType.DMA((7,)), pltpu.SemaphoreType.DMA((2,)), pltpu.SemaphoreType.DMA((2,))],
        compiler_params=vmem(63), cost_estimate=cost(9 * 10**9),
    )(counts, context, taken, ahead, *weights)


def first_half(context, weights):
    w_query, w_key, w_value, _, tables, gain, _ = weights
    return pl.pallas_call(
        first_half_kernel,
        out_shape=jax.ShapeDtypeStruct((3, BLOCK, D_ENC), BF16),
        in_specs=[HBM] * 5 + [VMEM],
        out_specs=HBM,
        scratch_shapes=[WHOLE, TABLES] + [SQUARE] * 3 + [WHOLE] * 3 + [pltpu.SemaphoreType.DMA((8,))],
        compiler_params=vmem(63), cost_estimate=cost(5 * 10**9),
    )(context, w_query, w_key, w_value, tables, gain)


def second_half(counts, context, taken, half, weights):
    w_query, w_key, _, w_out, tables, gain, final_gain = weights
    return pl.pallas_call(
        second_half_kernel,
        out_shape=[
            jax.ShapeDtypeStruct((1, BLOCK, D_ENC), BF16), jax.ShapeDtypeStruct((2, BLOCK, D_ENC), BF16)],
        in_specs=[SMEM] + [HBM] * 7 + [VMEM] * 2,
        out_specs=[HBM] * 2,
        scratch_shapes=[WHOLE, SQUARE] + [WHOLE] * 6 + [SQUARE, SQUARE, TABLES, WHOLE, WHOLE]
        + [pltpu.SemaphoreType.DMA((10,))],
        compiler_params=vmem(63), cost_estimate=cost(6 * 10**9),
    )(counts, context, taken, half, w_out, w_query, w_key, tables, gain, final_gain)


def three_parts(values):
    high = values.astype(BF16).astype(F32)
    middle = (values - high).astype(BF16).astype(F32)
    return high, middle, values - high - middle


def ring_chips(me):
    z, y = me // 4, lax.rem(me // 2, 2)
    place = jnp.where(z == 3, 2, jnp.where(z == 2, 3, z))
    chips = []
    for step in range(CHIPS // 2):
        at = lax.rem(place + 4 - step, 4)
        z = jnp.where(at == 2, 3, jnp.where(at == 3, 2, at))
        chips.append((2 * z + y, 2 * z + 1 - y))
    return chips


def cross_kernel(counts_ref, *refs):
    token0, token12, far0, far12 = refs[:4]
    loads, (upper_ref, lower_ref, near_ref, far_ref, across_ref) = refs[4:11], refs[11:16]
    out_ref, token_buf, weight_buf, query_buf, score_ref, value_ref, total_ref, top_ref, sum_ref = refs[16:25]
    sems, token_sems, row_sems = refs[25:]
    tokens = (token0.at[0], token12.at[0], token12.at[1], far0.at[0], far12.at[0], far12.at[1])
    me = lax.axis_index("ctx")
    core = lax.rem(me, 2)
    own_live, other_live, _ = live_counts(counts_ref)
    chips = [chip for pair in ring_chips(me) for chip in pair]
    columns = [pl.ds(pl.multiple_of(chip * LANES, LANES), LANES) for chip in chips]
    copies = [
        pltpu.make_async_copy(load.at[pl.ds(0, D_ENC), :], weight_buf.at[:, columns[at]], sems.at[at])
        for at, load in enumerate(loads)
    ]
    rest = D_ENC - HALF_LOAD
    copies.append(pltpu.make_async_copy(
        upper_ref, weight_buf.at[pl.ds(0, HALF_LOAD), columns[CHIPS - 1]], sems.at[CHIPS - 1]))
    copies.append(pltpu.make_async_copy(
        lower_ref.at[pl.ds(0, rest), :], weight_buf.at[pl.ds(HALF_LOAD, rest), columns[CHIPS - 1]], sems.at[CHIPS]))

    def fetch(at, part, source, heads):
        start = pl.multiple_of((2 * chips[at] + part) * LINES, LINES)
        copies.append(pltpu.make_async_copy(
            source, query_buf.at[heads, pl.ds(start, LINES), :], row_sems.at[len(copies) - CHIPS - 1]))

    every = slice(0, HALF_HEADS)
    for at in range(CHIPS - 1):
        fetch(at, core, near_ref.at[at, :, core], every)
        fetch(at, 1 - core, far_ref.at[at, :, core], every)
    fetch(CHIPS - 1, 1 - core, across_ref.at[:, core], every)
    for head in range(HALF_HEADS):
        start = pl.multiple_of(rest + (2 * head + core) * LINES, LINES)
        fetch(CHIPS - 1, core, lower_ref.at[pl.ds(start, LINES), :], head)

    def token_copy(at):
        return pltpu.make_async_copy(tokens[at], token_buf.at[at], token_sems.at[at])

    def live(at):
        return (own_live > at) if at < CAP else (other_live > at - CAP)

    for copy in copies:
        copy.start()
    for at in range(2 * CAP):
        @pl.when(live(at))
        def _():
            token_copy(at).start()
    total_ref[...] = jnp.zeros_like(total_ref)
    sum_ref[...] = jnp.zeros_like(sum_ref)
    top_ref[...] = jnp.full_like(top_ref, -jnp.inf)
    for copy in copies:
        copy.wait()

    for at in range(2 * CAP):
        @pl.when(live(at))
        def _():
            token_copy(at).wait()
            both = jnp.dot(token_buf[at], weight_buf[...], preferred_element_type=F32).astype(BF16)
            value_ref[at] = both[:, HALF_HEADS * LANES :]
            for head in range(HALF_HEADS):
                scores = lax.dot_general(
                    both[:, head * LANES : (head + 1) * LANES], query_buf[head],
                    (((1,), (1,)), ((), ())), preferred_element_type=F32,
                ) * (1.0 / math.sqrt(HEAD_DIM))
                score_ref[at, head] = scores
                top_ref[head] = jnp.maximum(top_ref[head], jnp.max(scores, axis=0, keepdims=True))

    for at in range(2 * CAP):
        @pl.when(live(at))
        def _():
            for head in range(HALF_HEADS):
                weights = jnp.exp(score_ref[at, head] - top_ref[head])
                sum_ref[head] += jnp.sum(weights, axis=0, keepdims=True)
                total_ref[head] += lax.dot_general(
                    weights.astype(BF16), value_ref[at, :, head * LANES : (head + 1) * LANES],
                    (((0,), (0,)), ((), ())), preferred_element_type=F32)

    lines = total_ref.shape[1]
    notes = []
    for head in range(HALF_HEADS):
        notes += list(three_parts(top_ref[head])) + list(three_parts(sum_ref[head]))
        out_ref[:, head] = total_ref[head].astype(BF16).reshape(2 * CHIPS, LINES, LANES)
    notes = jnp.concatenate(notes + [jnp.zeros((LANES - len(notes), lines), F32)], axis=0).T
    out_ref[:, HALF_HEADS] = notes.astype(BF16).reshape(2 * CHIPS, LINES, LANES)


def cross(counts, *arrays):
    lines = 2 * CHIPS * LINES
    line = pltpu.VMEM((HALF_HEADS, 1, lines), F32)
    return pl.pallas_call(
        cross_kernel,
        out_shape=jax.ShapeDtypeStruct((2 * CHIPS, HALF_HEADS + 1, LINES, LANES), BF16),
        in_specs=[SMEM] + [HBM] * 16,
        out_specs=VMEM,
        scratch_shapes=[
            pltpu.VMEM((2 * CAP, BLOCK, D_ENC), BF16),
            pltpu.VMEM((D_ENC, KV_HEADS * LANES), BF16),
            pltpu.VMEM((HALF_HEADS, lines, LANES), BF16),
            pltpu.VMEM((2 * CAP, HALF_HEADS, BLOCK, lines), F32),
            pltpu.VMEM((2 * CAP, BLOCK, HALF_HEADS * LANES), BF16),
            pltpu.VMEM((HALF_HEADS, lines, LANES), F32),
            line, line,
            pltpu.SemaphoreType.DMA((CHIPS + 1,)), pltpu.SemaphoreType.DMA((2 * CAP,)), pltpu.SemaphoreType.DMA((19,)),
        ],
        compiler_params=vmem(63),
        cost_estimate=pl.CostEstimate(flops=6 * 10**9, bytes_accessed=8 * 2**20, transcendentals=2**20),
    )(counts, *arrays)


def combine_kernel(parts_ref, out_ref):
    for core in range(2):
        pieces = [parts_ref.at[2 * chip + core] for chip in range(CHIPS)]
        notes = [piece[HALF_HEADS].astype(F32) for piece in pieces]
        for at in range(HALF_HEADS):
            lane = 6 * at
            tops = [n[:, lane : lane + 1] + n[:, lane + 1 : lane + 2] + n[:, lane + 2 : lane + 3] for n in notes]
            sums = [n[:, lane + 3 : lane + 4] + n[:, lane + 4 : lane + 5] + n[:, lane + 5 : lane + 6] for n in notes]
            top = functools.reduce(jnp.maximum, tops)
            numerator, denominator = 0.0, 0.0
            for share, amount, piece in zip([jnp.exp(t - top) for t in tops], sums, pieces):
                numerator += share * piece[at].astype(F32)
                denominator += share * amount
            lines = numerator / denominator
            for g in range(GROUP):
                start = ((2 * at + core) * GROUP + g) * LANES
                out_ref[:, start : start + LANES] = lines[g * ROWS : (g + 1) * ROWS].astype(BF16)


def combine(parts):
    return pl.pallas_call(
        combine_kernel, out_shape=jax.ShapeDtypeStruct((ROWS, QW), BF16), in_specs=[VMEM], out_specs=VMEM,
        compiler_params=vmem(8),
    )(parts)


NEXT_Z = (1, 3, 0, 2)


def exchange(values, bits):
    return lax.ppermute(values, "ctx", [(i, i ^ bits) for i in range(2 * CHIPS)])


def round_z(values, bits=0):
    return lax.ppermute(values, "ctx", [(i, (4 * NEXT_Z[i // 4] + i % 4) ^ bits) for i in range(2 * CHIPS)])


def local(context, counts, queries, norm_gain, w_query, w_key, w_value, w_out, final_gain, w_kv):
    weights = (w_query, w_key, w_value, w_out, rotary_lanes(), norm_gain, final_gain)
    load0 = prepare(w_kv, queries)
    load1, beside0, taken = round_z(load0), exchange(load0, 2), exchange(context, 1)
    half = first_half(context, weights)
    load1, beside0, taken, half = lax.optimization_barrier((load1, beside0, taken, half))
    load2, beside1 = round_z(load1), exchange(load1, 2)
    token0, ahead = second_half(counts, context, taken, half, weights)
    load2, beside1, token0, ahead = lax.optimization_barrier((load2, beside1, token0, ahead))
    load3, beside2, far0 = round_z(load2), exchange(load2, 2), exchange(token0, 1)
    token12 = encode(counts, context, taken, ahead, weights)
    load3, beside2, far0, token12 = lax.optimization_barrier((load3, beside2, far0, token12))
    rows, upper, lower, across = last_parts(load0, beside0, load1, beside1, load2, beside2, load3)
    upper, lower, across, far_rows = exchange(upper, 2), round_z(lower), round_z(across, 1), exchange(rows, 1)
    far12 = exchange(token12, 1)
    parts = cross(
        counts, token0, token12, far0, far12, load0, beside0, load1, beside1, load2, beside2, load3,
        upper, lower, rows, far_rows, across)
    return combine(lax.all_to_all(parts, "ctx", 0, 0, tiled=True))


def rotary_tables(length, head_width):
    position = jnp.arange(length).astype(jnp.float32)[:, None]
    frequency = jnp.exp(
        jnp.arange(head_width // 2).astype(jnp.float32) * (-2.0 * math.log(10000.0) / head_width)
    )
    phase_angle = position * frequency[None, :]
    return (jnp.cos(phase_angle)[:, None, :], jnp.sin(phase_angle)[:, None, :])


def rotate(values, cosine_table, sine_table):
    half_width = values.shape[-1] // 2
    lower_half = values[..., :half_width]
    upper_half = values[..., half_width:]
    return jnp.concatenate(
        [
            lower_half * cosine_table - upper_half * sine_table,
            upper_half * cosine_table + lower_half * sine_table,
        ],
        axis=-1,
    )


def weighted_sums(cross_scores, top_scores, key_alive, cross_values):
    cross_weights = jnp.where(key_alive, jnp.exp(cross_scores - top_scores[..., None]), 0.0)
    total_rows = cross_scores.shape[0]
    denominator = jnp.sum(cross_weights, axis=-1).reshape(total_rows, Q_HEADS)
    numerator = jnp.einsum(
        "rkgt,tkd->rkgd",
        cross_weights.astype(jnp.bfloat16),
        cross_values,
        preferred_element_type=jnp.float32,
    )
    return (numerator.reshape(total_rows, QW), denominator)


def local_any(context, counts, queries, norm_gain, w_query, w_key, w_value, w_out, final_gain, w_kv):
    places = lax.axis_size("ctx")
    device_index = lax.axis_index("ctx")
    device_number = jnp.arange(places)
    own_count = jnp.sum(jnp.where(device_number == device_index, counts, 0))
    alive_slot = jnp.arange(CAP) < own_count
    slot_count = context.shape[0]
    row_count = slot_count * BLOCK
    normed = root_scale(context, norm_gain).astype(jnp.bfloat16).reshape(row_count, D_ENC)
    cosine_table, sine_table = rotary_tables(BLOCK, ENC_HD)

    def project(weight):
        return jnp.dot(normed, weight, preferred_element_type=jnp.float32).reshape(
            slot_count, BLOCK, ENC_HEADS, ENC_HD
        )

    query_rows = rotate(project(w_query), cosine_table, sine_table).astype(jnp.bfloat16)
    key_rows = rotate(project(w_key), cosine_table, sine_table).astype(jnp.bfloat16)
    value_rows = project(w_value).astype(jnp.bfloat16)
    scores = jnp.einsum(
        "sqhd,skhd->shqk", query_rows, key_rows, preferred_element_type=jnp.float32
    ) / math.sqrt(ENC_HD)
    weights = jax.nn.softmax(scores, axis=-1).astype(jnp.bfloat16)
    mixed_rows = jnp.einsum(
        "shqk,skhd->sqhd", weights, value_rows, preferred_element_type=jnp.float32
    )
    mixed_rows = mixed_rows.astype(jnp.bfloat16).reshape(row_count, D_ENC)
    residual = context.reshape(row_count, D_ENC).astype(jnp.float32) + jnp.dot(
        mixed_rows, w_out, preferred_element_type=jnp.float32
    )
    final_norm = root_scale(residual, final_gain).astype(jnp.bfloat16)
    key_value = jnp.dot(
        final_norm,
        lax.all_gather(w_kv, "ctx", axis=1, tiled=True),
        preferred_element_type=jnp.float32,
    ).astype(jnp.bfloat16)
    cross_keys = key_value[:, : KV_HEADS * HEAD_DIM].reshape(row_count, KV_HEADS, HEAD_DIM)
    cross_values = key_value[:, KV_HEADS * HEAD_DIM :].reshape(row_count, KV_HEADS, HEAD_DIM)
    every_query = lax.all_gather(queries, "ctx", axis=0, tiled=True)
    total_rows = every_query.shape[0]
    grouped = every_query.reshape(total_rows, KV_HEADS, GROUP, HEAD_DIM)
    cross_scores = jnp.einsum(
        "rkgd,tkd->rkgt", grouped, cross_keys, preferred_element_type=jnp.float32
    ) / math.sqrt(HEAD_DIM)
    key_alive = jnp.repeat(alive_slot, BLOCK)
    local_top = jnp.max(jnp.where(key_alive, cross_scores, -jnp.inf), axis=-1)
    row_top = lax.pmax(local_top.astype(jnp.bfloat16), "ctx").astype(local_top.dtype)
    numerator, denominator = weighted_sums(cross_scores, row_top, key_alive, cross_values)
    own_numerator, own_denominator = (
        lax.psum_scatter(numerator, "ctx", scatter_dimension=0, tiled=True),
        lax.psum_scatter(denominator, "ctx", scatter_dimension=0, tiled=True),
    )
    own_rows = own_numerator.shape[0]
    result = own_numerator.reshape(own_rows, Q_HEADS, HEAD_DIM) / own_denominator[..., None]
    return result.reshape(own_rows, QW).astype(jnp.bfloat16)


def solution(mesh):
    in_specs = (
        P(("groups", "ctx"), None, None),
        P("groups"),
        P(("groups", "ctx"), None),
        P(),
        P(),
        P(),
        P(),
        P(),
        P(),
        P(None, "ctx"),
    )
    out_specs = P(("groups", "ctx"), None)
    small = mesh.shape["ctx"] == 2 * CHIPS
    return jax.shard_map(local if small else local_any, mesh=mesh, in_specs=in_specs, out_specs=out_specs, check_vma=False)
```
